32 devices in a mesh: batch: 16 (over z, y, x), head: 2 (over core).
Axes of the slice: x: 2, y: 2, z: 4, core: 2. Of those that a mesh axis runs over, the one named last changes fastest.
Arguments:
- tokens: bfloat16 [32, 197, 768], P(('batch', 'head')), may hold values from -6 to 6
- kept_index: int32 [32, 196], P(('batch', 'head')), may hold values from 0 to 195, as said below
- kept_count: int32 [32], P(('batch', 'head')), may hold values from 79 to 196
- prompts: bfloat16 [50, 768], replicated, may hold values from -6 to 6
- gain_one: bfloat16 [768], replicated, may hold values from 0.3984375 to 1.59375
- shift_one: bfloat16 [768], replicated, may hold values from -1.5 to 1.5
- w_query: bfloat16 [768, 768], P(None, 'head'), may hold values from -0.21875 to 0.21875
- b_query: bfloat16 [768], P('head'), may hold values from -1.5 to 1.5
- w_key: bfloat16 [768, 768], P(None, 'head'), may hold values from -0.21875 to 0.21875
- w_value: bfloat16 [768, 768], P(None, 'head'), may hold values from -0.21875 to 0.21875
- b_value: bfloat16 [768], P('head'), may hold values from -1.5 to 1.5
- w_out: bfloat16 [768, 768], P('head'), may hold values from -1.5 to 1.5
- b_out: bfloat16 [768], replicated, may hold values from -1.5 to 1.5
- gain_two: bfloat16 [768], replicated, may hold values from 0.3984375 to 1.59375
- shift_two: bfloat16 [768], replicated, may hold values from -1.5 to 1.5
- w_fc1: bfloat16 [3072, 768], P(('batch', 'head')), may hold values from -0.21875 to 0.21875
- b_fc1: bfloat16 [3072], P(('batch', 'head')), may hold values from -1.5 to 1.5
- w_fc2: bfloat16 [3072, 768], P(('batch', 'head')), may hold values from -0.109375 to 0.109375
- b_fc2: bfloat16 [768], replicated, may hold values from -1.5 to 1.5
- cotangent: bfloat16 [32, 256, 768], P(('batch', 'head')), may hold values from -6 to 6
Outputs:
- layer_out: bfloat16 [32, 256, 768], P(('batch', 'head'))
- grad_tokens: float32 [32, 197, 768], P(('batch', 'head'))
- grad_prompts: float32 [50, 768], replicated
- grad_gain_one: float32 [768], replicated
- grad_shift_one: float32 [768], replicated
- grad_w_query: float32 [768, 768], P(None, 'head')
- grad_b_query: float32 [768], P('head')
- grad_w_key: float32 [768, 768], P(None, 'head')
- grad_w_value: float32 [768, 768], P(None, 'head')
- grad_b_value: float32 [768], P('head')
- grad_w_out: float32 [768, 768], P('head')
- grad_b_out: float32 [768], replicated
- grad_gain_two: float32 [768], replicated
- grad_shift_two: float32 [768], replicated
- grad_w_fc1: float32 [3072, 768], P(('batch', 'head'))
- grad_b_fc1: float32 [3072], P(('batch', 'head'))
- grad_w_fc2: float32 [3072, 768], P(('batch', 'head'))
- grad_b_fc2: float32 [768], replicated
The draws below stay inside these ranges and needn't reach their ends.
Inputs may be any that keep to these rules, and one draw needn't show every extreme that they name: `kept_index`: row i holds kept_count[i] different patch numbers in rising order, then zeros.
All inputs are finite; a program needn't handle non-finite values.
Results may differ from the reference program's by a relative error of at most 0.013.
Values may be sent and summed in bfloat16 or wider, within the bound.
A program may use at most 128 MiB of HBM per device.

```python
import math
import jax
import jax.numpy as jnp
from jax import lax

D = 768
HEADS = 12
HEAD_DIM = 64
FF = 3072
PROMPTS = 50
PATCHES = 196
SEQ_PAD = 256
KEEP_MIN = 79
IMAGES = 32


def kept_patches(key):
    count_key, order_key, place_key = jax.random.split(key, 3)
    counts_drawn = jax.random.randint(count_key, (IMAGES,), KEEP_MIN, PATCHES + 1, dtype=jnp.int32)
    places = jax.random.permutation(place_key, IMAGES)
    counts_drawn = jnp.where(places == 0, PATCHES, counts_drawn)
    counts_drawn = jnp.where(places == 1, KEEP_MIN, counts_drawn)
    rank_keys = jax.random.randint(order_key, (IMAGES, PATCHES), 0, 1 << 20, dtype=jnp.int32) * PATCHES + jnp.arange(PATCHES, dtype=jnp.int32)[None, :]
    shuffled = jnp.argsort(rank_keys, axis=1, stable=True).astype(jnp.int32)
    slot_ids = jnp.arange(PATCHES, dtype=jnp.int32)[None, :]
    chosen = jnp.where(slot_ids < counts_drawn[:, None], shuffled, PATCHES)
    chosen = jnp.sort(chosen, axis=1)
    chosen = jnp.where(slot_ids < counts_drawn[:, None], chosen, 0)
    return (chosen.astype(jnp.int32), counts_drawn.astype(jnp.int32))


def draw_kept_index(key, part):
    return kept_patches(key)[0]


def draw_kept_count(key, part):
    return kept_patches(key)[1]


def block_levels(rng, extent, cuts, low, largest):
    def one(position, shards_of):
        draws = jax.random.uniform(jax.random.fold_in(jax.random.fold_in(rng, 6), position), (shards_of,), jnp.float32, low / len(cuts), largest / len(cuts))
        return jnp.repeat(jnp.exp(draws), extent[position] // shards_of).reshape((-1,) + (1,) * (len(extent) - position - 1))

    factor_of = one(*cuts[0])
    for cut in cuts[1:]:
        factor_of = factor_of * one(*cut)
    return factor_of


def noise(key, shape, width, limit, cuts=(), held_as=jnp.bfloat16):
    level = block_levels(key, shape, cuts, -0.22, 0.18) if cuts else 1.0
    values = jax.random.normal(key, shape, jnp.float32) * width * level
    return jnp.minimum(jnp.maximum(values, -limit), limit).astype(held_as)


def setup_inputs(seed: int = 0) -> dict:
    streams_of = jax.random.split(jax.random.key(seed), 21)
    return {
        "tokens": noise(streams_of[0], (IMAGES, PATCHES + 1, D), 1.0, 6.0, ((0, 32),)),
        "kept_index": draw_kept_index(jax.random.fold_in(streams_of[20], 71), 0),
        "kept_count": draw_kept_count(jax.random.fold_in(streams_of[20], 71), 0),
        "prompts": noise(streams_of[3], (PROMPTS, D), 1.0, 6.0),
        "gain_one": jnp.clip(1.0 + 0.12 * jax.random.normal(streams_of[4], (D,), jnp.float32), 0.3984375, 1.59375).astype(jnp.bfloat16),
        "shift_one": noise(streams_of[5], (D,), 0.3, 1.5),
        "w_query": noise(streams_of[6], (D, D), D ** -0.5, 0.21875, ((1, 2),)),
        "b_query": noise(streams_of[7], (D,), 0.3, 1.5, ((0, 2),)),
        "w_key": noise(streams_of[8], (D, D), D ** -0.5, 0.21875, ((1, 2),)),
        "w_value": noise(streams_of[9], (D, D), D ** -0.5, 0.21875, ((1, 2),)),
        "b_value": noise(streams_of[10], (D,), 0.3, 1.5, ((0, 2),)),
        "w_out": noise(streams_of[11], (D, D), (D // 48) ** -0.5, 1.5, ((0, 2),)),
        "b_out": noise(streams_of[12], (D,), 0.3, 1.5),
        "gain_two": jnp.clip(1.0 + 0.12 * jax.random.normal(streams_of[13], (D,), jnp.float32), 0.3984375, 1.59375).astype(jnp.bfloat16),
        "shift_two": noise(streams_of[14], (D,), 0.3, 1.5),
        "w_fc1": noise(streams_of[15], (FF, D), D ** -0.5, 0.21875, ((0, 32),)),
        "b_fc1": noise(streams_of[16], (FF,), 0.3, 1.5, ((0, 32),)),
        "w_fc2": noise(streams_of[17], (FF, D), FF ** -0.5, 0.109375, ((0, 32),)),
        "b_fc2": noise(streams_of[18], (D,), 0.3, 1.5),
        "cotangent": noise(streams_of[19], (IMAGES, SEQ_PAD, D), 1.0, 6.0, ((0, 32),)),
    }


@jax.custom_vjp
def low(v):
    return lax.optimization_barrier(v.astype(jnp.bfloat16)).astype(jnp.float32)

@jax.custom_vjp
def low_back(v):
    return v

def low_keep(v):
    return (low(v), None)

def low_pass(kept, grad):
    return (grad,)

def back_keep(v):
    return (v, None)

def back_low(kept, grad):
    return (low(grad),)
low.defvjp(low_keep, low_pass)
low_back.defvjp(back_keep, back_low)
EPSILON = 1e-06
HIGHEST = lax.Precision.HIGHEST

def layer_norm(rows_in, gain_vec, shift_vec):
    centre = lax.optimization_barrier(jnp.mean(rows_in, axis=-1, keepdims=True))
    centred = rows_in - centre
    spread = lax.optimization_barrier(jnp.mean(centred * centred, axis=-1, keepdims=True))
    return centred * lax.rsqrt(spread + EPSILON) * gain_vec + shift_vec

def assemble(tokens, prompts, kept_index, kept_count, seq_rows):
    image_count = tokens.shape[0]
    model_width = tokens.shape[2]
    patch_count = kept_index.shape[1]
    prompt_count = prompts.shape[0]
    slot_ids = jnp.arange(patch_count, dtype=jnp.int32)
    slot_live = slot_ids[None, :] < kept_count[:, None]
    where_from = jnp.broadcast_to((kept_index + 1)[:, :, None], (image_count, patch_count, model_width))
    picked = jnp.take_along_axis(tokens, where_from, axis=1)
    picked = jnp.where(slot_live[:, :, None], picked, jnp.zeros_like(picked))
    leading = tokens[:, 0:1, :]
    prompt_rows = jnp.broadcast_to(prompts[None, :, :], (image_count, prompt_count, model_width))
    padding = jnp.zeros((image_count, seq_rows - 1 - prompt_count - patch_count, model_width), tokens.dtype)
    return jnp.concatenate([leading, prompt_rows, picked, padding], axis=1)

def live_rows(kept_count, prompt_count, seq_rows):
    limit_row = 1 + prompt_count + kept_count
    return jnp.arange(seq_rows, dtype=jnp.int32)[None, :] < limit_row[:, None]

def forward(kept_index, kept_count, tokens, prompts, gain_one, shift_one, w_query, b_query, w_key, w_value, b_value, w_out, b_out, gain_two, shift_two, w_fc1, b_fc1, w_fc2, b_fc2):
    image_count = tokens.shape[0]
    model_width = tokens.shape[2]
    stream_in = assemble(tokens, prompts, kept_index, kept_count, SEQ_PAD)
    normed = low(layer_norm(stream_in, gain_one, shift_one))
    queries = low_back(low(jnp.einsum('bsd,de->bse', normed, w_query, precision=HIGHEST) + b_query))
    key_rows = low_back(low(jnp.einsum('bsd,de->bse', normed, w_key, precision=HIGHEST)))
    value_rows = low_back(low(jnp.einsum('bsd,de->bse', normed, w_value, precision=HIGHEST) + b_value))
    shape_heads = (image_count, SEQ_PAD, HEADS, HEAD_DIM)
    scores = jnp.einsum('bqhe,bkhe->bhqk', queries.reshape(shape_heads), key_rows.reshape(shape_heads), precision=HIGHEST)
    scores = low_back(scores * HEAD_DIM ** (-0.5))
    live_mask = live_rows(kept_count, PROMPTS, SEQ_PAD)
    scores = jnp.where(live_mask[:, None, None, :], scores, -1e+30)
    row_max = lax.optimization_barrier(jnp.max(scores, axis=-1, keepdims=True))
    weights = jnp.exp(scores - row_max)
    attn_probs = low(weights / lax.optimization_barrier(jnp.sum(weights, axis=-1, keepdims=True)))
    mixed_rows = jnp.einsum('bhqk,bkhe->bqhe', attn_probs, value_rows.reshape(shape_heads), precision=HIGHEST)
    mixed_rows = low_back(low(mixed_rows.reshape(image_count, SEQ_PAD, model_width)))
    branch = low_back(jnp.einsum('bsd,de->bse', mixed_rows, w_out, precision=HIGHEST) + b_out)
    stream_mid = stream_in + branch
    normed_two = low(layer_norm(stream_mid, gain_two, shift_two))
    before = low_back(jnp.einsum('bsd,fd->bsf', normed_two, w_fc1, precision=HIGHEST) + b_fc1)
    hidden = low(jax.nn.gelu(before, approximate=True))
    result = jnp.einsum('bsf,fd->bsd', hidden, w_fc2, precision=HIGHEST) + b_fc2
    return jnp.where(live_mask[:, :, None], stream_mid + result, jnp.zeros_like(result))

def reference(tokens, kept_index, kept_count, prompts, gain_one, shift_one, w_query, b_query, w_key, w_value, b_value, w_out, b_out, gain_two, shift_two, w_fc1, b_fc1, w_fc2, b_fc2, cotangent):
    members = (prompts, gain_one, shift_one, w_query, b_query, w_key, w_value, b_value, w_out, b_out, gain_two, shift_two, w_fc1, b_fc1, w_fc2, b_fc2)
    floats = tuple((member.astype(jnp.float32) for member in members))
    per_step = math.gcd(IMAGES, max(1, 4096 // SEQ_PAD))
    step_count = IMAGES // per_step

    def blocked(array):
        return array.reshape((step_count, per_step) + array.shape[1:])

    def one_step(totals, pieces):
        token_block, index_block, count_block, cot_block = pieces

        def run_block(token_rows, *params_in):
            return forward(index_block, count_block, token_rows, *params_in)
        output_block, pull_back = jax.vjp(run_block, token_block.astype(jnp.float32), *floats)
        gradients = pull_back(cot_block.astype(jnp.float32))
        totals = tuple((running + latest for running, latest in zip(totals, gradients[1:])))
        return (totals, (output_block.astype(jnp.bfloat16), gradients[0]))
    start_totals = tuple((jnp.zeros(member.shape, jnp.float32) for member in floats))
    totals, outputs = lax.scan(one_step, start_totals, (blocked(tokens), blocked(kept_index), blocked(kept_count), blocked(cotangent)))
    layer_out = outputs[0].reshape(IMAGES, SEQ_PAD, D)
    grad_tokens = outputs[1].reshape(IMAGES, PATCHES + 1, D)
    return (layer_out, grad_tokens, totals[0], totals[1], totals[2], totals[3], totals[4], totals[5], totals[6], totals[7], totals[8], totals[9], totals[10], totals[11], totals[12], totals[13], totals[14], totals[15])
```

```python
import functools
from types import SimpleNamespace

import jax
import jax.numpy as jnp
from jax import lax
from jax.experimental import pallas as pl
from jax.experimental.pallas import tpu as pltpu
from jax.sharding import PartitionSpec as P

MESH = pl.DeviceIdType.MESH
HEAD_DIM = 64
EPSILON = 1e-06
LANES = 128
BF16 = jnp.bfloat16
F32 = jnp.float32


def round_up(value, step):
    return -(-value // step) * step


def mm(left, right):
    return lax.dot_general(left, right, (((1,), (0,)), ((), ())), preferred_element_type=F32)


def mm_nt(left, right):
    return lax.dot_general(left, right, (((1,), (1,)), ((), ())), preferred_element_type=F32)


def mm_tn(left, right):
    return lax.dot_general(left, right, (((0,), (0,)), ((), ())), preferred_element_type=F32)


def fold_rows(rows):
    count, width = rows.shape
    return jnp.sum(rows.reshape(count // 8, 8, width), axis=0)


def normalise(rows):
    width = rows.shape[1]
    centre = jnp.sum(rows, axis=1, keepdims=True) * (1.0 / width)
    centred = rows - centre
    spread = jnp.sum(centred * centred, axis=1, keepdims=True) * (1.0 / width)
    scale = lax.rsqrt(spread + EPSILON)
    return centred * scale, scale


def norm_back(grad_rows, gain_row, unit_rows, scale):
    width = grad_rows.shape[1]
    scaled = grad_rows * gain_row
    mean_one = jnp.sum(scaled, axis=1, keepdims=True) * (1.0 / width)
    mean_two = jnp.sum(scaled * unit_rows, axis=1, keepdims=True) * (1.0 / width)
    return scale * (scaled - mean_one - unit_rows * mean_two)


GELU_A = 0.7978845608028654
GELU_B = 0.044715


def gelu_both(value):
    square = value * value
    bend = jnp.tanh(value * (GELU_A + (GELU_A * GELU_B) * square))
    half = 0.5 + 0.5 * bend
    slope = half + (0.5 * value) * (1.0 - bend * bend) * (
        GELU_A + (3.0 * GELU_A * GELU_B) * square
    )
    return value * half, slope


class Links:
    def __init__(self, send_sems, recv_sems):
        self.send_sems = send_sems
        self.recv_sems = recv_sems
        self.copies = []

    def send(self, source, target, device):
        place = len(self.copies)
        copy = pltpu.make_async_remote_copy(
            src_ref=source,
            dst_ref=target,
            send_sem=self.send_sems.at[place],
            recv_sem=self.recv_sems.at[place],
            device_id=device,
            device_id_type=MESH,
        )
        copy.start()
        self.copies.append(copy)
        return copy

    def drain(self):
        for copy in self.copies:
            copy.wait_send()


def layer_kernel(dims, *refs):
    it = iter(refs)
    tokens, kept, count_ref, prompts, vecs, wq, wk, wv, wout, fc1, fc2, cot = (
        next(it) for _ in range(12)
    )
    out_rows, out_tok, out_attn, out_small, out_fc1, out_fc2, out_bias = (
        next(it) for _ in range(7)
    )
    s = SimpleNamespace(**dict(zip(dims.scratch, it)))
    seq, width, local = dims.seq, dims.width, dims.local
    pairs = local // LANES
    rows_per = dims.rows_per
    n, ring, slots = dims.n, dims.ring, dims.slots
    chunk_slots = dims.chunk_slots
    chunk = chunk_slots * rows_per
    chunks = slots // chunk_slots
    tok_rows, tok_pad, prompt_pad = dims.tok_rows, dims.tok_pad, dims.prompt_pad
    prompt_rows, patches = dims.prompt_rows, dims.patches
    rest_count = n // 16
    score_scale = HEAD_DIM**-0.5
    block = 32
    blocks = seq // block

    b = lax.axis_index("batch")
    h = lax.axis_index("head")
    bx = b % 2
    by = (b // 2) % 2
    zz = b // 4
    sib = (b, 1 - h)
    xdev = (b + 1 - 2 * bx, h)
    ydev = (b + 2 - 4 * by, h)
    corner = b % 4
    ring_next = (((zz + 1) % ring) * 4 + corner, h)
    ring_prev = (((zz + ring - 1) % ring) * 4 + corner, h)
    zq = zz % 4
    zdev = [((zz - zq + (zq + hop) % 4) * 4 + corner, h) for hop in range(4)]
    rest = b // 16
    rdev = [(((rest + hop) % rest_count) * 16 + b % 16, h) for hop in range(rest_count)]
    one_dev = (xdev[0] * (1 - h) + ydev[0] * h, h)
    two_dev = (ydev[0] * (1 - h) + xdev[0] * h, h)
    p_one = bx * (1 - h) + by * h
    p_two = by * (1 - h) + bx * h

    partners = [sib, xdev, ydev] + zdev[1:]
    if ring > 4:
        partners += [ring_next, ring_prev] + rdev[1:]
    barrier = pltpu.get_barrier_semaphore()
    for partner in partners:
        pl.semaphore_signal(barrier, inc=1, device_id=partner, device_id_type=MESH)

    links = Links(s.send_sems, s.recv_sems)

    w_all, b_all, cot_all = s.w_all, s.b_all, s.cot_all
    w_all[0, 0:rows_per] = fc1[...]
    w_all[0, rows_per : 2 * rows_per] = fc2[...]
    b_all[0] = jnp.broadcast_to(vecs[7:8, 0:LANES], (8, LANES))
    limit = count_ref[0] + (1 + prompt_rows)
    s.meta[0] = jnp.broadcast_to(limit, (8, LANES))

    @pl.loop(0, blocks)
    def _(step):
        at = pl.ds(pl.multiple_of(step * block, block), block)
        row_ids = lax.broadcasted_iota(jnp.int32, (block, 1), 0) + step * block
        rows = cot[at, :].astype(F32)
        cot_all[0, at, :] = jnp.where(row_ids < limit, rows, 0.0).astype(BF16)

    pl.semaphore_wait(barrier, len(partners))

    gather_ring, gather_y = {}, {}

    def gather_step(distance):
        if distance > 0:
            for copy in gather_ring[distance]:
                copy.wait_recv()
        mine = 2 * distance
        if distance + 1 < ring:
            gather_ring[distance + 1] = [
                links.send(w_all.at[mine], w_all.at[mine + 2], ring_next),
                links.send(b_all.at[mine], b_all.at[mine + 2], ring_next),
            ]
        gather_y[distance] = [
            links.send(w_all.at[mine], w_all.at[mine + 1], ydev),
            links.send(b_all.at[mine], b_all.at[mine + 1], ydev),
        ]

    gather_done = [0]

    def gather_until(distance):
        while gather_done[0] <= min(distance, ring - 1):
            gather_step(gather_done[0])
            gather_done[0] += 1

    gather_until(0)
    cot_x = links.send(cot_all.at[0], cot_all.at[2], xdev)
    cot_sib = links.send(cot_all.at[0], cot_all.at[1], sib)
    meta_sib = links.send(s.meta.at[0], s.meta.at[1], sib)

    src, pick = s.src, s.pick
    src[...] = jnp.zeros(src.shape, BF16)
    src[0:tok_rows, :] = tokens[...]
    src[tok_pad : tok_pad + prompt_rows, :] = prompts[...]
    s.idx[...] = jnp.zeros((8, seq), jnp.int32)
    s.idx[0:1, 0:patches] = kept[...]
    shifted = pltpu.roll(s.idx[...], 1 + prompt_rows, axis=1)[0:1, :]
    spot = lax.broadcasted_iota(jnp.int32, (1, seq), 1)
    wanted = jnp.where(
        spot < 1 + prompt_rows,
        jnp.where(spot == 0, 0, tok_pad - 1 + spot),
        jnp.where(spot < limit, shifted + 1, -1),
    )
    pick[...] = jnp.where(
        lax.broadcasted_iota(jnp.int32, pick.shape, 0) == wanted, 1.0, 0.0
    ).astype(BF16)
    stream = s.stream
    stream[...] = mm_tn(pick[...], src[...])

    n1 = s.n1

    @pl.loop(0, blocks)
    def _(step):
        at = pl.ds(pl.multiple_of(step * block, block), block)
        unit_rows, _ = normalise(stream[at, :])
        n1[0, at, :] = (unit_rows * vecs[0:1, :] + vecs[1:2, :]).astype(BF16)

    n1_sib = links.send(n1.at[0], n1.at[1], sib)

    def project(image):
        rows = n1[image]
        queries = mm(rows, wq[...]) + vecs[6:7, 0:local]
        keys = mm(rows, wk[...])
        values = mm(rows, wv[...]) + vecs[6:7, local : 2 * local]
        for pair in range(pairs):
            at = slice(pair * LANES, (pair + 1) * LANES)
            s.q[image, pair] = queries[:, at].astype(BF16)
            s.k[image, pair] = keys[:, at].astype(BF16)
            s.v[image, pair] = values[:, at].astype(BF16)

    lane_ids = lax.broadcasted_iota(jnp.int32, (1, LANES), 1)
    lane_half = [
        jnp.where(lane_ids // HEAD_DIM == half, 1.0, 0.0).astype(BF16) for half in range(2)
    ]
    key_ids = lax.broadcasted_iota(jnp.int32, (seq, 1), 0)

    def attend(image):
        key_live = key_ids < s.meta[image, 0:1, 0:1]

        @pl.loop(0, pairs)
        def _(pair):
            queries, keys = s.q[image, pair], s.k[image, pair]
            values_t = s.v[image, pair].T
            for half in range(2):
                scores = mm_nt(keys, queries * lane_half[half]) * score_scale
                scores = jnp.where(key_live, scores, -1e30)
                weights = jnp.exp(scores - jnp.max(scores, axis=0, keepdims=True))
                probs = weights * (1.0 / jnp.sum(weights, axis=0, keepdims=True))
                s.probs[image * 2 * pairs + pair * 2 + half] = probs
                mixed_t = mm(values_t[half * HEAD_DIM : (half + 1) * HEAD_DIM], probs.astype(BF16))
                at = pl.ds(pl.multiple_of(pair * LANES + half * HEAD_DIM, HEAD_DIM), HEAD_DIM)
                s.mixed_t[image, at, :] = mixed_t.astype(BF16)

    project(0)
    n1_sib.wait_recv()
    meta_sib.wait_recv()
    project(1)
    attend(1)
    s.branch_out[...] = mm_tn(s.mixed_t[1], wout[...])
    branch_sib = links.send(s.branch_out, s.branch_in, sib)
    gather_until(1)
    attend(0)
    s.branch_own[...] = mm_tn(s.mixed_t[0], wout[...])
    branch_sib.wait_recv()

    middle, n2 = s.middle, s.n2

    @pl.loop(0, blocks)
    def _(step):
        at = pl.ds(pl.multiple_of(step * block, block), block)
        rows = stream[at, :] + (s.branch_own[at, :] + s.branch_in[at, :] + vecs[2:3, :])
        middle[at, :] = rows
        unit_rows, _ = normalise(rows)
        n2[0, at, :] = (unit_rows * vecs[3:4, :] + vecs[4:5, :]).astype(BF16)

    n2_x = links.send(n2.at[0], n2.at[2], xdev)
    n2_sib = links.send(n2.at[0], n2.at[1], sib)
    cot_x.wait_recv()
    cot_far = links.send(cot_all.at[2], cot_all.at[3], sib)
    gather_until(ring // 2)

    hidden_all, before_all = s.hidden, s.grad_before
    result, grad_two = s.result, s.grad_two
    unpack = jnp.where(
        lax.broadcasted_iota(jnp.int32, (LANES, chunk), 1) % rows_per
        == lax.broadcasted_iota(jnp.int32, (LANES, chunk), 0),
        1.0,
        0.0,
    )
    owner_of = (
        lax.broadcasted_iota(jnp.int32, (chunk_slots, chunk), 1) // rows_per
        == lax.broadcasted_iota(jnp.int32, (chunk_slots, chunk), 0)
    )

    def feed(part, images):
        first = part * chunk_slots
        span = slice(first, first + chunk_slots)
        tiles = b_all[span, 0, :].astype(BF16)
        bias_row = jnp.sum(
            jnp.where(owner_of, mm(tiles, unpack.astype(BF16)), 0.0), axis=0, keepdims=True
        )

        def one(image, total):
            up = w_all[span, 0:rows_per].reshape(chunk, width)
            down = w_all[span, rows_per : 2 * rows_per].reshape(chunk, width)
            before = mm_nt(n2[image], up) + bias_row
            hidden, slope = gelu_both(before)
            hidden = hidden.astype(BF16)
            hidden_all[image] = hidden
            grad_before = (mm_nt(cot_all[image], down) * slope).astype(BF16)
            before_all[image] = grad_before
            if part == 0:
                result[image] = mm(hidden, down)
                grad_two[image] = mm(grad_before, up)
            else:
                result[image] += mm(hidden, down)
                grad_two[image] += mm(grad_before, up)
            return total + fold_rows(grad_before.astype(F32))

        return lax.fori_loop(images[0], images[1], one, jnp.zeros((8, chunk), F32))

    g_all, gb_all = s.g_all, s.gb_all

    def feed_weights(part, bias_total):
        first = part * chunk_slots
        span = slice(first, first + chunk_slots)

        for left, right, base in ((before_all, n2, 0), (hidden_all, cot_all, rows_per)):
            total = jnp.zeros((chunk, width), F32)
            for image in range(4):
                total += mm_tn(left[image], right[image])
            g_all[span, base : base + rows_per] = (
                total.astype(BF16).reshape(chunk_slots, rows_per, width)
            )
        bias_row = jnp.sum(bias_total, axis=0, keepdims=True)
        spread = jnp.where(owner_of, jnp.broadcast_to(bias_row, owner_of.shape), 0.0)
        high = spread.astype(BF16)
        low = (spread - high.astype(F32)).astype(BF16)
        packed = mm_nt(high, unpack.astype(BF16)) + mm_nt(low, unpack.astype(BF16))
        for slot in range(chunk_slots):
            gb_all[first + slot] = jnp.broadcast_to(packed[slot : slot + 1], (8, LANES))

    order = list(range(1, ring)) + [0]
    sum_y, sum_ring = {}, {}

    def sum_send_y(distance):
        slot = 2 * distance + 1
        sum_y[distance] = [
            links.send(g_all.at[slot], s.ry.at[distance], ydev),
            links.send(gb_all.at[slot], s.ryb.at[distance], ydev),
        ]

    def sum_step(distance):
        for copy in sum_y[distance]:
            copy.wait_recv()
        mine = 2 * distance
        total = g_all[mine].astype(F32) + s.ry[distance].astype(F32)
        bias = gb_all[mine] + s.ryb[distance]
        if distance != 1:
            before = (distance + ring - 1) % ring
            for copy in sum_ring[before]:
                copy.wait_recv()
            total += s.rz_in[before].astype(F32)
            bias += s.rzb_in[before]
        if distance == 0:
            out_fc1[...] = total[0:rows_per]
            out_fc2[...] = total[rows_per : 2 * rows_per]
            out_bias[...] = bias
        else:
            s.rz_out[distance] = total.astype(BF16)
            s.rzb_out[distance] = bias
            sum_ring[distance] = [
                links.send(s.rz_out.at[distance], s.rz_in.at[distance], ring_next),
                links.send(s.rzb_out.at[distance], s.rzb_in.at[distance], ring_next),
            ]

    sums_done = [0]

    def sum_until(steps):
        while sums_done[0] < min(steps, ring):
            sum_step(order[sums_done[0]])
            sums_done[0] += 1

    def gather_wait(part):
        per = chunk_slots // 2
        gather_until((part + 1) * per)
        for distance in range(part * per, (part + 1) * per):
            for copy in gather_y[distance]:
                copy.wait_recv()

    gather_wait(0)
    n2_sib.wait_recv()
    cot_sib.wait_recv()
    near = feed(0, (0, 2))
    n2_x.wait_recv()
    n2_far = links.send(n2.at[2], n2.at[3], sib)
    gather_until(ring - 1)
    cot_far.wait_recv()
    n2_far.wait_recv()
    feed_weights(0, near + feed(0, (2, 4)))
    for distance in range(1, chunk_slots // 2):
        sum_send_y(distance)
    if chunks == 2:
        gather_wait(1)
        bias_total = feed(1, (0, 4))

    part_out, part_in = s.part_out, s.part_in
    cross_out, cross_in = s.cross_out, s.cross_in
    part_sib, cross = {}, {}
    for kind, total in enumerate((grad_two, result)):
        for place, image in enumerate((3, 1)):
            part_out[kind, place] = total[image].astype(BF16)
            part_sib[kind, place] = links.send(
                part_out.at[kind, place], part_in.at[kind, place], sib
            )
    for kind, total in enumerate((grad_two, result)):
        part_sib[kind, 0].wait_recv()
        cross_out[kind] = (total[2] + part_in[kind, 0].astype(F32)).astype(BF16)
        cross[kind] = links.send(cross_out.at[kind], cross_in.at[kind], xdev)
    if chunks == 2:
        feed_weights(1, bias_total)
    for distance in range(chunk_slots // 2, ring):
        sum_send_y(distance)
    sum_send_y(0)
    sum_until(1)

    part_sib[0, 1].wait_recv()
    cross[0].wait_recv()

    grad_mid, grad_branch = s.grad_mid, s.grad_branch

    def mid_back(step, totals):
        at = pl.ds(pl.multiple_of(step * block, block), block)
        grads = (
            grad_two[0, at, :] + part_in[0, 1, at, :].astype(F32) + cross_in[0, at, :].astype(F32)
        )
        unit_rows, scale = normalise(middle[at, :])
        passed = cot_all[0, at, :].astype(F32)
        mid = passed + norm_back(grads, vecs[3:4, :], unit_rows, scale)
        grad_mid[at, :] = mid
        low = mid.astype(BF16)
        grad_branch[0, at, :] = low
        return (
            totals[0] + fold_rows(grads * unit_rows),
            totals[1] + fold_rows(grads),
            totals[2] + fold_rows(low.astype(F32)),
            totals[3] + fold_rows(passed),
        )

    empty = jnp.zeros((8, width), F32)
    gain_two_sum, shift_two_sum, out_bias_sum, fc2_bias_sum = lax.fori_loop(
        0, blocks, mid_back, (empty,) * 4
    )
    branch_back = links.send(grad_branch.at[0], grad_branch.at[1], sib)

    def mixed_back(image):
        grads = mm_nt(grad_branch[image], wout[...])
        for pair in range(pairs):
            s.grad_mixed[image, pair] = grads[:, pair * LANES : (pair + 1) * LANES].astype(BF16)

    grads_qkv = s.grads_qkv

    def attend_back(image):
        @pl.loop(0, pairs)
        def _(pair):
            queries, keys = s.q[image, pair], s.k[image, pair]
            values, grads = s.v[image, pair], s.grad_mixed[image, pair]
            keys_t = keys.T
            grad_values = jnp.zeros((seq, LANES), F32)
            grad_keys = jnp.zeros((seq, LANES), F32)
            grad_queries = []
            for half in range(2):
                probs = s.probs[image * 2 * pairs + pair * 2 + half]
                grads_half = grads * lane_half[half]
                grad_values += mm(probs.astype(BF16), grads_half)
                grad_probs = mm_nt(values, grads_half)
                inner = jnp.sum(grad_probs * probs, axis=0, keepdims=True)
                grad_scores = (probs * (grad_probs - inner)).astype(BF16)
                grad_keys += mm(grad_scores, queries * lane_half[half])
                grad_queries.append(
                    mm(keys_t[half * HEAD_DIM : (half + 1) * HEAD_DIM], grad_scores)
                )
            grad_query = jnp.concatenate(grad_queries, axis=0).T
            for place, value in enumerate(
                (grad_query * score_scale, grad_keys * score_scale, grad_values)
            ):
                at = pl.ds(pl.multiple_of(place * local + pair * LANES, LANES), LANES)
                grads_qkv[image, :, at] = value.astype(BF16)

    def rows_back(image):
        return (
            mm_nt(grads_qkv[image, :, 0:local], wq[...])
            + mm_nt(grads_qkv[image, :, local : 2 * local], wk[...])
            + mm_nt(grads_qkv[image, :, 2 * local : 3 * local], wv[...])
        )

    mixed_back(0)
    branch_back.wait_recv()
    mixed_back(1)

    ar = s.ar
    flat = [
        (ar.at[item], s.ar_one.at[item], s.ar_two.at[item], s.ar_z.at[item],
         s.ar_rest.at[item], out_attn.at[item], width)
        for item in range(4)
    ]
    small_half = seq // 2
    small = (s.small, s.small_one, s.small_two, s.small_z, s.small_rest,
             s.small_all, small_half)
    items = flat + [small]
    stages = [dict() for _ in range(7)]

    def piece(total_rows):
        half, quarter, leaf = total_rows // 2, total_rows // 4, total_rows // 16
        at_one = pl.multiple_of(p_one * half, half)
        at_two = pl.multiple_of(at_one + p_two * quarter, quarter)
        return half, quarter, leaf, at_one, at_two

    def reduce_one(item):
        data, one = items[item][0], items[item][1]
        half, _, _, _, _ = piece(items[item][6])
        other = pl.ds(pl.multiple_of((1 - p_one) * half, half), half)
        stages[0][item] = [links.send(data.at[other], one, one_dev)]

    def reduce_two(item):
        data, one, two = items[item][:3]
        half, quarter, _, at_one, _ = piece(items[item][6])
        stages[0][item][0].wait_recv()
        mine = pl.ds(at_one, half)
        data[mine] = (data[mine].astype(F32) + one[...].astype(F32)).astype(data.dtype)
        other = pl.ds(pl.multiple_of(at_one + (1 - p_two) * quarter, quarter), quarter)
        stages[1][item] = [links.send(data.at[other], two, two_dev)]

    def reduce_z(item):
        data, _, two, by_z = items[item][:4]
        _, quarter, leaf, _, at_two = piece(items[item][6])
        stages[1][item][0].wait_recv()
        mine = pl.ds(at_two, quarter)
        data[mine] = (data[mine].astype(F32) + two[...].astype(F32)).astype(data.dtype)
        stages[2][item] = [
            links.send(
                data.at[pl.ds(pl.multiple_of(at_two + ((zq + hop) % 4) * leaf, leaf), leaf)],
                by_z.at[hop - 1],
                zdev[hop],
            )
            for hop in range(1, 4)
        ]

    def spread_z(item):
        data, _, _, by_z, by_rest, done = items[item][:6]
        _, _, leaf, _, at_two = piece(items[item][6])
        for copy in stages[2][item]:
            copy.wait_recv()
        mine = pl.ds(pl.multiple_of(at_two + zq * leaf, leaf), leaf)
        total = data[mine].astype(F32)
        for hop in range(3):
            total += by_z[hop].astype(F32)
        if rest_count > 1:
            by_rest[0] = total.astype(data.dtype)
            copies = [
                links.send(by_rest.at[0], by_rest.at[hop], rdev[hop])
                for hop in range(1, rest_count)
            ]
            for copy in copies:
                copy.wait_recv()
            total = jnp.zeros(total.shape, F32)
            for owner in range(rest_count):
                total += by_rest[(rest - owner + rest_count) % rest_count].astype(F32)
        done[mine] = total.astype(done.dtype)
        stages[3][item] = [
            links.send(done.at[mine], done.at[mine], zdev[hop]) for hop in range(1, 4)
        ]

    def spread_two(item):
        done = items[item][5]
        _, quarter, _, _, at_two = piece(items[item][6])
        for copy in stages[3][item]:
            copy.wait_recv()
        mine = pl.ds(at_two, quarter)
        stages[4][item] = [links.send(done.at[mine], done.at[mine], two_dev)]

    def spread_one(item):
        done = items[item][5]
        half, _, _, at_one, _ = piece(items[item][6])
        stages[4][item][0].wait_recv()
        mine = pl.ds(at_one, half)
        stages[5][item] = [links.send(done.at[mine], done.at[mine], one_dev)]

    def finish(item):
        stages[5][item][0].wait_recv()

    steps = [reduce_one, reduce_two, reduce_z, spread_z, spread_two, spread_one, finish]

    for half in range(2):
        at = slice(half * local, (half + 1) * local)
        total = mm(s.mixed_t[0], grad_branch[0, :, at]) + mm(
            s.mixed_t[1], grad_branch[1, :, at]
        )
        ar[0, at, :] = total.astype(BF16)
    reduce_one(0)
    attend_back(1)
    s.rows_out[...] = rows_back(1).astype(BF16)
    rows_sib = links.send(s.rows_out, s.rows_in, sib)
    sum_until(2)
    attend_back(0)
    s.rows_own[...] = rows_back(0)
    sum_until(3)

    for base in range(0, width, 256):
        rows = slice(base, base + 256)
        total = mm_tn(n1[0, :, rows], grads_qkv[0]) + mm_tn(n1[1, :, rows], grads_qkv[1])
        for place in range(3):
            ar[1 + place, rows, :] = total[:, place * local : (place + 1) * local].astype(BF16)
    for item in range(1, 4):
        reduce_one(item)
    reduce_two(0)
    sum_until(ring)

    part_sib[1, 1].wait_recv()
    cross[1].wait_recv()

    @pl.loop(0, blocks)
    def _(step):
        at = pl.ds(pl.multiple_of(step * block, block), block)
        row_ids = lax.broadcasted_iota(jnp.int32, (block, 1), 0) + step * block
        total = result[0, at, :] + part_in[1, 1, at, :].astype(F32) + cross_in[1, at, :].astype(F32)
        rows = middle[at, :] + (total + vecs[5:6, :])
        out_rows[at, :] = jnp.where(row_ids < limit, rows, 0.0).astype(BF16)

    rows_sib.wait_recv()

    def in_back(step, totals):
        at = pl.ds(pl.multiple_of(step * block, block), block)
        grads = (s.rows_own[at, :] + s.rows_in[at, :].astype(F32))
        unit_rows, scale = normalise(stream[at, :])
        grad_mid[at, :] += norm_back(grads, vecs[0:1, :], unit_rows, scale)
        return (totals[0] + fold_rows(grads * unit_rows), totals[1] + fold_rows(grads))

    gain_one_sum, shift_one_sum = lax.fori_loop(0, blocks, in_back, (empty,) * 2)
    grad_in = grad_mid[...]
    high = grad_in.astype(BF16)
    low = (grad_in - high.astype(F32)).astype(BF16)
    placed = mm(pick[...], high) + mm(pick[...], low)
    out_tok[...] = placed[0:tok_rows]

    small_ref, small_own = s.small_full, s.small
    small_ref[...] = jnp.zeros(small_ref.shape, F32)
    part_width = small_ref.shape[1]
    parts = width // part_width
    for part in range(parts):
        small_ref[part * prompt_pad : part * prompt_pad + prompt_pad, :] = placed[
            tok_pad : tok_pad + prompt_pad, part * part_width : (part + 1) * part_width
        ]
    base = parts * prompt_pad
    sums = (gain_one_sum, shift_one_sum, out_bias_sum, gain_two_sum, shift_two_sum, fc2_bias_sum)
    for place, total in enumerate(sums):
        row = jnp.sum(total, axis=0, keepdims=True)
        for part in range(parts):
            at = base + place * parts + part
            small_ref[at : at + 1, :] = row[:, part * part_width : (part + 1) * part_width]
    base += len(sums) * parts
    for place in range(2):
        at = slice(2 * place * local, 2 * place * local + local)
        row = jnp.sum(
            grads_qkv[0, :, at].astype(F32) + grads_qkv[1, :, at].astype(F32),
            axis=0,
            keepdims=True,
        )
        for head in range(2):
            chosen = row * (h if head == 1 else 1 - h).astype(F32)
            at = base + head * 4 + place * 2
            small_ref[at : at + 1, :] = chosen[:, 0:part_width]
            small_ref[at + 1 : at + 2, 0 : local - part_width] = chosen[:, part_width:local]
    theirs = pl.ds(pl.multiple_of((1 - h) * small_half, small_half), small_half)
    ours = pl.ds(pl.multiple_of(h * small_half, small_half), small_half)
    small_sib = links.send(small_ref.at[theirs], s.small_in, sib)
    small_sib.wait_recv()
    small_own[...] = small_ref[ours] + s.small_in[...]
    reduce_one(4)

    begun = [2, 1, 1, 1, 1]
    for wave in range(1, len(steps) + len(items)):
        for item in range(len(items)):
            stage = wave - item
            if begun[item] <= stage < len(steps):
                steps[stage](item)
                begun[item] = stage + 1
    out_small[ours] = s.small_all[...]
    small_back = links.send(out_small.at[ours], out_small.at[ours], sib)
    small_back.wait_recv()
    links.drain()


def layer(dims, operands):
    seq, width, local = dims.seq, dims.width, dims.local
    n, ring, slots, rows_per = dims.n, dims.ring, dims.slots, dims.rows_per
    pairs = local // LANES
    chunk = dims.chunk_slots * rows_per
    rest_count = n // 16
    small_half = seq // 2
    part_width = 256
    copies = 4 * ring + 4 * ring + 40 + 5 * (10 + rest_count)
    vmem = pltpu.VMEM
    shared = 2 * rows_per
    scratch = dict(
        send_sems=pltpu.SemaphoreType.DMA((copies,)),
        recv_sems=pltpu.SemaphoreType.DMA((copies,)),
        w_all=vmem((slots, shared, width), BF16),
        b_all=vmem((slots, 8, LANES), F32),
        cot_all=vmem((4, seq, width), BF16),
        meta=vmem((2, 8, LANES), jnp.int32),
        src=vmem((dims.tok_pad + dims.prompt_pad, width), BF16),
        pick=vmem((dims.tok_pad + dims.prompt_pad, seq), BF16),
        idx=vmem((8, seq), jnp.int32),
        stream=vmem((seq, width), F32),
        middle=vmem((seq, width), F32),
        n1=vmem((2, seq, width), BF16),
        n2=vmem((4, seq, width), BF16),
        q=vmem((2, pairs, seq, LANES), BF16),
        k=vmem((2, pairs, seq, LANES), BF16),
        v=vmem((2, pairs, seq, LANES), BF16),
        probs=vmem((4 * pairs, seq, seq), F32),
        mixed_t=vmem((2, local, seq), BF16),
        branch_out=vmem((seq, width), F32),
        branch_in=vmem((seq, width), F32),
        branch_own=vmem((seq, width), F32),
        hidden=vmem((4, seq, chunk), BF16),
        grad_before=vmem((4, seq, chunk), BF16),
        result=vmem((4, seq, width), F32),
        grad_two=vmem((4, seq, width), F32),
        part_out=vmem((2, 2, seq, width), BF16),
        part_in=vmem((2, 2, seq, width), BF16),
        cross_out=vmem((2, seq, width), BF16),
        cross_in=vmem((2, seq, width), BF16),
        g_all=vmem((slots, shared, width), BF16),
        gb_all=vmem((slots, 8, LANES), F32),
        ry=vmem((ring, shared, width), BF16),
        ryb=vmem((ring, 8, LANES), F32),
        rz_out=vmem((ring, shared, width), BF16),
        rzb_out=vmem((ring, 8, LANES), F32),
        rz_in=vmem((ring, shared, width), BF16),
        rzb_in=vmem((ring, 8, LANES), F32),
        grad_mid=vmem((seq, width), F32),
        grad_branch=vmem((2, seq, width), BF16),
        grad_mixed=vmem((2, pairs, seq, LANES), BF16),
        grads_qkv=vmem((2, seq, 3 * local), BF16),
        rows_out=vmem((seq, width), BF16),
        rows_in=vmem((seq, width), BF16),
        rows_own=vmem((seq, width), F32),
        ar=vmem((4, width, local), BF16),
        ar_one=vmem((4, width // 2, local), BF16),
        ar_two=vmem((4, width // 4, local), BF16),
        ar_z=vmem((4, 3, width // 16, local), BF16),
        ar_rest=vmem((4, rest_count, width // 16, local), BF16),
        small_full=vmem((seq, part_width), F32),
        small_in=vmem((small_half, part_width), F32),
        small=vmem((small_half, part_width), F32),
        small_one=vmem((small_half // 2, part_width), F32),
        small_two=vmem((small_half // 4, part_width), F32),
        small_z=vmem((3, small_half // 16, part_width), F32),
        small_rest=vmem((rest_count, small_half // 16, part_width), F32),
        small_all=vmem((small_half, part_width), F32),
    )
    dims = SimpleNamespace(**vars(dims), scratch=tuple(scratch))
    whole = pl.BlockSpec(memory_space=pltpu.VMEM)
    in_specs = [whole] * len(operands)
    in_specs[2] = pl.BlockSpec(memory_space=pltpu.SMEM)
    shape = jax.ShapeDtypeStruct
    return pl.pallas_call(
        functools.partial(layer_kernel, dims),
        out_shape=(
            shape((seq, width), BF16),
            shape((dims.tok_rows, width), F32),
            shape((4, width, local), BF16),
            shape((seq, part_width), F32),
            shape((rows_per, width), F32),
            shape((rows_per, width), F32),
            shape((8, LANES), F32),
        ),
        in_specs=in_specs,
        out_specs=[whole] * 7,
        scratch_shapes=list(scratch.values()),
        compiler_params=pltpu.CompilerParams(
            collective_id=0, has_side_effects=True, vmem_limit_bytes=60 * 2**20
        ),
    )(*operands)


def body(n, *arguments):
    (
        tokens, kept_index, kept_count, prompts, gain_one, shift_one, w_query, b_query, w_key,
        w_value, b_value, w_out, b_out, gain_two, shift_two, w_fc1, b_fc1, w_fc2, b_fc2, cotangent,
    ) = arguments
    seq, width = cotangent.shape[1:]
    local = w_query.shape[1]
    rows = w_fc1.shape[0]
    rows_per = round_up(rows, 16)
    ring = n // 4
    slots = 2 * ring
    halves = slots // 2
    chunk_slots = halves if (halves % 2 == 0 and halves * rows_per % LANES == 0) else slots
    tok_rows, prompt_rows = tokens.shape[1], prompts.shape[0]
    dims = SimpleNamespace(
        n=n, ring=ring, slots=slots, chunk_slots=chunk_slots, rows_per=rows_per, seq=seq,
        width=width, local=local, tok_rows=tok_rows, tok_pad=round_up(tok_rows, 16),
        prompt_rows=prompt_rows, prompt_pad=round_up(prompt_rows, 16),
        patches=kept_index.shape[1],
    )
    if rows_per != rows:
        spare = ((0, rows_per - rows), (0, 0))
        w_fc1, w_fc2 = jnp.pad(w_fc1, spare), jnp.pad(w_fc2, spare)
    vecs = jnp.stack(
        [
            gain_one, shift_one, b_out, gain_two, shift_two, b_fc2,
            jnp.concatenate([b_query, b_value]), jnp.pad(b_fc1, (0, width - rows)),
        ]
    ).astype(F32)
    operands = (
        tokens[0], kept_index, kept_count, prompts, vecs, w_query, w_key, w_value, w_out,
        w_fc1, w_fc2, cotangent[0],
    )
    out_rows, out_tok, out_attn, small, grad_fc1, grad_fc2, grad_bias = layer(dims, operands)
    prompt_pad = dims.prompt_pad
    part_width = small.shape[1]
    parts = width // part_width
    grad_prompts = jnp.concatenate(
        [small[part * prompt_pad : part * prompt_pad + prompt_rows] for part in range(parts)], axis=1
    )
    base = parts * prompt_pad
    vectors = small[base : base + 6 * parts].reshape(6, width)
    base += 6 * parts
    own = lax.dynamic_slice_in_dim(small, base + 4 * lax.axis_index("head"), 4, 0)
    own = own.reshape(2, 2 * part_width)[:, :local]
    grads = out_attn.astype(F32)
    grad_out = jnp.concatenate([grads[0, :local], grads[0, local:]], axis=1)
    return (
        out_rows[None], out_tok[None], grad_prompts, vectors[0], vectors[1], grads[1], own[0],
        grads[2], grads[3], own[1], grad_out, vectors[2], vectors[3], vectors[4],
        grad_fc1[:rows], grad_bias[0, :rows], grad_fc2[:rows], vectors[5],
    )


def solution(mesh):
    batch, head = mesh.axis_names
    both = (batch, head)
    placed = (
        P(both, None, None), P(both, None), P(both), P(), P(), P(), P(None, head), P(head),
        P(None, head), P(None, head), P(head), P(head, None), P(), P(), P(),
        P(both, None), P(both), P(both, None), P(), P(both, None, None),
    )
    return jax.shard_map(
        functools.partial(body, mesh.shape[batch]),
        mesh=mesh,
        in_specs=placed,
        out_specs=(
            P(both, None, None), P(both, None, None), P(), P(), P(), P(None, head), P(head),
            P(None, head), P(None, head), P(head), P(head, None), P(), P(), P(),
            P(both, None), P(both), P(both, None), P(),
        ),
        check_vma=False,
    )
```

```python
import functools
from types import SimpleNamespace

import jax
import jax.numpy as jnp
from jax import lax
from jax.experimental import pallas as pl
from jax.experimental.pallas import tpu as pltpu
from jax.sharding import PartitionSpec as P

MESH = pl.DeviceIdType.MESH
HEAD_DIM = 64
EPSILON = 1e-06
LANES = 128
BF16 = jnp.bfloat16
F32 = jnp.float32


def round_up(value, step):
    return -(-value // step) * step


def mm(left, right):
    return lax.dot_general(left, right, (((1,), (0,)), ((), ())), preferred_element_type=F32)


def mm_nt(left, right):
    return lax.dot_general(left, right, (((1,), (1,)), ((), ())), preferred_element_type=F32)


def mm_tn(left, right):
    return lax.dot_general(left, right, (((0,), (0,)), ((), ())), preferred_element_type=F32)


def fold_rows(rows):
    count, width = rows.shape
    return jnp.sum(rows.reshape(count // 8, 8, width), axis=0)


def normalise(rows):
    width = rows.shape[1]
    centre = jnp.sum(rows, axis=1, keepdims=True) * (1.0 / width)
    centred = rows - centre
    spread = jnp.sum(centred * centred, axis=1, keepdims=True) * (1.0 / width)
    scale = lax.rsqrt(spread + EPSILON)
    return centred * scale, scale


def norm_back(grad_rows, gain_row, unit_rows, scale):
    width = grad_rows.shape[1]
    scaled = grad_rows * gain_row
    mean_one = jnp.sum(scaled, axis=1, keepdims=True) * (1.0 / width)
    mean_two = jnp.sum(scaled * unit_rows, axis=1, keepdims=True) * (1.0 / width)
    return scale * (scaled - mean_one - unit_rows * mean_two)


GELU_A = 0.7978845608028654
GELU_B = 0.044715


def gelu_both(value):
    square = value * value
    bend = jnp.tanh(value * (GELU_A + (GELU_A * GELU_B) * square))
    half = 0.5 + 0.5 * bend
    slope = half + (0.5 * value) * (1.0 - bend * bend) * (
        GELU_A + (3.0 * GELU_A * GELU_B) * square
    )
    return value * half, slope


VECTORS = (
    "gain_one", "shift_one", "b_query", "b_value", "b_out", "gain_two", "shift_two", "b_fc1", "b_fc2",
)


class Loads:
    def __init__(self, sems):
        self.sems = sems
        self.count = 0

    def start(self, source, target):
        copy = pltpu.make_async_copy(source, target, self.sems.at[self.count])
        copy.start()
        self.count += 1
        return copy


class Links:
    def __init__(self, send_sems, recv_sems):
        self.send_sems = send_sems
        self.recv_sems = recv_sems
        self.copies = []

    def send(self, source, target, device):
        place = len(self.copies)
        copy = pltpu.make_async_remote_copy(
            src_ref=source,
            dst_ref=target,
            send_sem=self.send_sems.at[place],
            recv_sem=self.recv_sems.at[place],
            device_id=device,
            device_id_type=MESH,
        )
        copy.start()
        self.copies.append(copy)
        return copy

    def drain(self):
        for copy in self.copies:
            copy.wait_send()


def layer_kernel(dims, *refs):
    it = iter(refs)
    count_ref = next(it)
    tokens, kept, prompts, fc1, fc2, cot = (next(it) for _ in range(6))
    weights_in = [next(it) for _ in range(4)]
    vectors_in = [next(it) for _ in range(9)]
    out_rows, out_tok, out_attn, out_small, out_fc1, out_fc2, out_bias = (
        next(it) for _ in range(7)
    )
    s = SimpleNamespace(**dict(zip(dims.scratch, it)))
    w_pair, wout = s.w_pair, s.wout
    vecs = s.vecs
    seq, width, local = dims.seq, dims.width, dims.local
    pairs = local // LANES
    rows_per = dims.rows_per
    n, ring, slots = dims.n, dims.ring, dims.slots
    chunk_slots = dims.chunk_slots
    chunk = chunk_slots * rows_per
    chunks = slots // chunk_slots
    tok_rows, tok_pad, prompt_pad = dims.tok_rows, dims.tok_pad, dims.prompt_pad
    prompt_rows, patches = dims.prompt_rows, dims.patches
    rest_count = n // 16
    score_scale = HEAD_DIM**-0.5
    block = 32
    blocks = seq // block

    b = lax.axis_index("batch")
    h = lax.axis_index("head")
    bx = b % 2
    by = (b // 2) % 2
    zz = b // 4
    sib = (b, 1 - h)
    xdev = (b + 1 - 2 * bx, h)
    ydev = (b + 2 - 4 * by, h)
    corner = b % 4
    ring_next = (((zz + 1) % ring) * 4 + corner, h)
    ring_prev = (((zz + ring - 1) % ring) * 4 + corner, h)
    zq = zz % 4
    zdev = [((zz - zq + (zq + hop) % 4) * 4 + corner, h) for hop in range(4)]
    rest = b // 16
    rdev = [(((rest + hop) % rest_count) * 16 + b % 16, h) for hop in range(rest_count)]
    one_dev = (xdev[0] * (1 - h) + ydev[0] * h, h)
    two_dev = (ydev[0] * (1 - h) + xdev[0] * h, h)
    p_one = bx * (1 - h) + by * h
    p_two = by * (1 - h) + bx * h

    partners = [sib, xdev, ydev] + zdev[1:]
    if ring > 4:
        partners += [ring_next, ring_prev] + rdev[1:]
    barrier = pltpu.get_barrier_semaphore()
    for partner in partners:
        pl.semaphore_signal(barrier, inc=1, device_id=partner, device_id_type=MESH)

    links = Links(s.send_sems, s.recv_sems)

    w_all, b_all, cot_all = s.w_all, s.b_all, s.cot_all
    loads = Loads(s.load_sems)
    load_kept = loads.start(kept, s.kept)
    load_fc = [
        loads.start(fc1, w_all.at[0, pl.ds(0, rows_per)]),
        loads.start(fc2, w_all.at[0, pl.ds(rows_per, rows_per)]),
    ]
    load_cot = loads.start(cot.at[0], cot_all.at[0])
    load_rows = [loads.start(tokens, s.tokens), loads.start(prompts, s.prompts)]
    load_vectors = [loads.start(ref, getattr(s, name)) for ref, name in zip(vectors_in, VECTORS)]
    load_weights = [loads.start(weights_in[3], wout)]
    for pair in range(pairs):
        for place in range(3):
            load_weights.append(
                loads.start(
                    weights_in[place].at[:, pl.ds(pair * LANES, LANES)],
                    w_pair.at[pair, :, pl.ds(place * LANES, LANES)],
                )
            )

    limit = count_ref[0] + (1 + prompt_rows)
    src, pick = s.src, s.pick
    s.meta[0] = jnp.broadcast_to(limit, (8, LANES))
    s.idx[...] = jnp.zeros((8, seq), jnp.int32)
    src[tok_rows - tok_rows % 16 : tok_pad] = jnp.zeros((tok_pad - tok_rows + tok_rows % 16, width), BF16)
    src[tok_pad:] = jnp.zeros((prompt_pad, width), BF16)
    vecs[...] = jnp.zeros(vecs.shape, F32)
    load_kept.wait()
    s.idx[0:1, 0:patches] = s.kept[...]
    shifted = pltpu.roll(s.idx[...], 1 + prompt_rows, axis=1)[0:1, :]
    spot = lax.broadcasted_iota(jnp.int32, (1, seq), 1)
    wanted = jnp.where(
        spot < 1 + prompt_rows,
        jnp.where(spot == 0, 0, tok_pad - 1 + spot),
        jnp.where(spot < limit, shifted + 1, -1),
    )
    pick[...] = jnp.where(
        lax.broadcasted_iota(jnp.int32, pick.shape, 0) == wanted, 1.0, 0.0
    ).astype(BF16)
    for copy in load_vectors:
        copy.wait()
    for place, name in enumerate(("gain_one", "shift_one", "b_out", "gain_two", "shift_two", "b_fc2")):
        vecs[place : place + 1, :] = getattr(s, name)[...].astype(F32).reshape(1, width)
    vecs[6:7, 0:local] = s.b_query[...].astype(F32).reshape(1, local)
    vecs[6:7, local : 2 * local] = s.b_value[...].astype(F32).reshape(1, local)
    bias_rows = s.b_fc1.shape[0]
    vecs[7:8, 0:bias_rows] = s.b_fc1[...].astype(F32).reshape(1, bias_rows)
    b_all[0] = jnp.broadcast_to(vecs[7:8, 0:LANES], (8, LANES))
    load_cot.wait()

    @pl.loop(0, blocks)
    def _(step):
        at = pl.ds(pl.multiple_of(step * block, block), block)
        row_ids = lax.broadcasted_iota(jnp.int32, (block, 1), 0) + step * block
        rows = cot_all[0, at, :].astype(F32)
        cot_all[0, at, :] = jnp.where(row_ids < limit, rows, 0.0).astype(BF16)

    for copy in load_rows:
        copy.wait()
    src[0:tok_rows, :] = s.tokens[0]
    src[tok_pad : tok_pad + prompt_rows, :] = s.prompts[...]
    stream = s.stream
    stream[...] = mm_tn(pick[...], src[...])

    n1 = s.n1

    @pl.loop(0, blocks)
    def _(step):
        at = pl.ds(pl.multiple_of(step * block, block), block)
        unit_rows, s.scale_one[at, :] = normalise(stream[at, :])
        s.unit_one[at, :] = unit_rows
        n1[0, at, :] = (unit_rows * vecs[0:1, :] + vecs[1:2, :]).astype(BF16)

    for copy in load_fc:
        copy.wait()
    pl.semaphore_wait(barrier, len(partners))

    gather_ring, gather_y = {}, {}

    def gather_step(distance, kind):
        if distance > 0:
            for copy in gather_ring[distance, kind]:
                copy.wait_recv()
        rows = pl.ds(kind * rows_per, rows_per)
        mine = 2 * distance

        def hand_on(slot, device):
            copies = [links.send(w_all.at[mine, rows], w_all.at[slot, rows], device)]
            if kind == 0:
                copies.append(links.send(b_all.at[mine], b_all.at[slot], device))
            return copies

        if distance + 1 < ring:
            gather_ring[distance + 1, kind] = hand_on(mine + 2, ring_next)
        gather_y[distance, kind] = hand_on(mine + 1, ydev)

    gather_done = [0]

    def gather_until(distance, kind):
        while gather_done[0] <= min(2 * distance + kind, 2 * ring - 1):
            gather_step(gather_done[0] // 2, gather_done[0] % 2)
            gather_done[0] += 1

    n1_sib = links.send(n1.at[0], n1.at[1], sib)
    gather_until(0, 1)
    cot_x = links.send(cot_all.at[0], cot_all.at[2], xdev)
    cot_sib = links.send(cot_all.at[0], cot_all.at[1], sib)
    meta_sib = links.send(s.meta.at[0], s.meta.at[1], sib)


    def project(image):
        rows = n1[image]
        for pair in range(pairs):
            found = mm(rows, w_pair[pair])
            at = slice(pair * LANES, (pair + 1) * LANES)
            s.q[image, pair] = (found[:, 0:LANES] + vecs[6:7, at]).astype(BF16)
            s.k[image, pair] = found[:, LANES : 2 * LANES].astype(BF16)
            at = slice(local + pair * LANES, local + (pair + 1) * LANES)
            s.v[image, pair] = (found[:, 2 * LANES :] + vecs[6:7, at]).astype(BF16)

    lane_ids = lax.broadcasted_iota(jnp.int32, (1, LANES), 1)
    lane_half = [
        jnp.where(lane_ids // HEAD_DIM == half, 1.0, 0.0).astype(BF16) for half in range(2)
    ]
    lane_scaled = [
        jnp.where(lane_ids // HEAD_DIM == half, score_scale, 0.0).astype(BF16) for half in range(2)
    ]
    lane_spare = [
        jnp.where(lane_ids == (1 - half) * HEAD_DIM, 1.0, 0.0).astype(BF16) for half in range(2)
    ]
    key_ids = lax.broadcasted_iota(jnp.int32, (seq, 1), 0)

    def attend(image, first, last):
        key_bias = jnp.where(key_ids < s.meta[image, 0:1, 0:1], 0.0, -1e30).astype(BF16)

        @pl.loop(first, last)
        def _(pair):
            queries, keys = s.q[image, pair], s.k[image, pair]
            values_t = s.v[image, pair].T
            for half in range(2):
                scores = mm_nt(
                    keys * lane_half[half] + key_bias * lane_spare[half],
                    queries * lane_scaled[half] + lane_spare[half],
                )
                weights = jnp.exp(scores - jnp.max(scores, axis=0, keepdims=True))
                probs = weights * (1.0 / jnp.sum(weights, axis=0, keepdims=True))
                s.probs[image * 2 * pairs + pair * 2 + half] = probs
                mixed_t = mm(values_t[half * HEAD_DIM : (half + 1) * HEAD_DIM], probs.astype(BF16))
                at = pl.ds(pl.multiple_of(pair * LANES + half * HEAD_DIM, HEAD_DIM), HEAD_DIM)
                s.mixed_t[image, at, :] = mixed_t.astype(BF16)

    for copy in load_weights:
        copy.wait()
    project(0)
    n1_sib.wait_recv()
    meta_sib.wait_recv()
    project(1)
    attend(1, 0, pairs)
    s.branch_out[...] = mm_tn(s.mixed_t[1], wout[...])
    branch_sib = links.send(s.branch_out, s.branch_in, sib)
    gather_until(1, 0)
    attend(0, 0, pairs)
    gather_until(1, 1)
    s.branch_own[...] = mm_tn(s.mixed_t[0], wout[...])
    branch_sib.wait_recv()
    middle, n2 = s.middle, s.n2

    @pl.loop(0, blocks)
    def _(step):
        at = pl.ds(pl.multiple_of(step * block, block), block)
        rows = stream[at, :] + (s.branch_own[at, :] + s.branch_in[at, :] + vecs[2:3, :])
        middle[at, :] = rows
        unit_rows, s.scale_two[at, :] = normalise(rows)
        s.unit_two[at, :] = unit_rows
        n2[0, at, :] = (unit_rows * vecs[3:4, :] + vecs[4:5, :]).astype(BF16)

    n2_x = links.send(n2.at[0], n2.at[2], xdev)
    n2_sib = links.send(n2.at[0], n2.at[1], sib)
    gather_until(2, 0)
    cot_x.wait_recv()
    cot_far = links.send(cot_all.at[2], cot_all.at[3], sib)
    hidden_all, before_all = s.hidden, s.grad_before
    result, grad_two = s.result, s.grad_two
    unpack = jnp.where(
        lax.broadcasted_iota(jnp.int32, (LANES, chunk), 1) % rows_per
        == lax.broadcasted_iota(jnp.int32, (LANES, chunk), 0),
        1.0,
        0.0,
    )
    owner_of = (
        lax.broadcasted_iota(jnp.int32, (chunk_slots, chunk), 1) // rows_per
        == lax.broadcasted_iota(jnp.int32, (chunk_slots, chunk), 0)
    )

    def feed_spans(part):
        span = slice(part * chunk_slots, (part + 1) * chunk_slots)
        return (
            w_all[span, 0:rows_per].reshape(chunk, width),
            w_all[span, rows_per : 2 * rows_per].reshape(chunk, width),
        )

    def feed(part, images, totals):
        span = slice(part * chunk_slots, (part + 1) * chunk_slots)
        tiles = b_all[span, 0, :].astype(BF16)
        bias_row = jnp.sum(
            jnp.where(owner_of, mm(tiles, unpack.astype(BF16)), 0.0), axis=0, keepdims=True
        )
        first, last = images

        def one(step, total):
            image = first + step if last > first else first - step
            up, down = feed_spans(part)
            before = mm_nt(n2[image], up) + bias_row
            hidden, slope = gelu_both(before)
            hidden_all[part, image] = hidden.astype(BF16)
            grad_before = (mm_nt(cot_all[image], down) * slope).astype(BF16)
            before_all[image] = grad_before
            if part == 0:
                grad_two[image] = mm(grad_before, up)
            else:
                grad_two[image] += mm(grad_before, up)
            return total + fold_rows(grad_before.astype(F32))

        return lax.fori_loop(0, abs(last - first) + 1, one, totals)

    def feed_result(part):
        @pl.loop(0, 4)
        def _(image):
            _, down = feed_spans(part)
            if part == 0:
                result[image] = mm(hidden_all[part, image], down)
            else:
                result[image] += mm(hidden_all[part, image], down)

    g_all, gb_all = s.g_all, s.gb_all

    def feed_weights(part, bias_total):
        first = part * chunk_slots
        span = slice(first, first + chunk_slots)

        for left, right, base in ((before_all, n2, 0), (hidden_all.at[part], cot_all, rows_per)):
            total = jnp.zeros((chunk, width), F32)
            for image in range(4):
                total += mm_tn(left[image], right[image])
            g_all[span, base : base + rows_per] = (
                total.astype(BF16).reshape(chunk_slots, rows_per, width)
            )
        bias_row = jnp.sum(bias_total, axis=0, keepdims=True)
        spread = jnp.where(owner_of, jnp.broadcast_to(bias_row, owner_of.shape), 0.0)
        high = spread.astype(BF16)
        low = (spread - high.astype(F32)).astype(BF16)
        packed = mm_nt(high, unpack.astype(BF16)) + mm_nt(low, unpack.astype(BF16))
        for slot in range(chunk_slots):
            gb_all[first + slot] = jnp.broadcast_to(packed[slot : slot + 1], (8, LANES))

    order = list(range(1, ring)) + [0]
    stores = []
    sum_y, sum_ring, sum_both, sum_last = {}, {}, {}, []
    first_rows, second_rows = pl.ds(0, rows_per), pl.ds(rows_per, rows_per)

    def sum_send_y(distance):
        slot = 2 * distance + 1
        sum_y[distance] = [
            links.send(g_all.at[slot, first_rows], s.ry.at[distance], ydev),
            links.send(gb_all.at[slot], s.ryb.at[distance], ydev),
        ]

    def sum_a_step(distance):
        for copy in sum_y[distance]:
            copy.wait_recv()
        mine = 2 * distance
        total = g_all[mine, 0:rows_per].astype(F32) + s.ry[distance].astype(F32)
        bias = gb_all[mine] + s.ryb[distance]
        if distance != 1:
            before = (distance + ring - 1) % ring
            for copy in sum_ring[before]:
                copy.wait_recv()
            total += s.rz_in[before].astype(F32)
            bias += s.rzb_in[before]
        if distance == 0:
            s.own_fc1[...] = total
            s.own_bias[...] = bias
            stores.append(loads.start(s.own_fc1, out_fc1))
            stores.append(loads.start(s.own_bias, out_bias))
        else:
            s.rz_out[distance] = total.astype(BF16)
            s.rzb_out[distance] = bias
            sum_ring[distance] = [
                links.send(s.rz_out.at[distance], s.rz_in.at[distance], ring_next),
                links.send(s.rzb_out.at[distance], s.rzb_in.at[distance], ring_next),
            ]

    def sum_b_step(distance):
        if distance == 1:
            source = g_all.at[pl.ds(2, 2), second_rows]
            sum_both[1] = links.send(source, s.rb_in.at[1], ring_next)
            return
        before = (distance + ring - 1) % ring
        sum_both[before].wait_recv()
        for line in range(2):
            total = g_all[2 * distance + line, rows_per:].astype(F32) + s.rb_in[before, line].astype(F32)
            if distance == 0 and line == 0:
                s.own_fc2[...] = total
            else:
                s.rb_out[distance, line] = total.astype(BF16)
        if distance == 0:
            sum_last.append(links.send(s.rb_out.at[0, 1], s.ry_last, ydev))
        else:
            sum_both[distance] = links.send(s.rb_out.at[distance], s.rb_in.at[distance], ring_next)

    def sum_b_end():
        sum_last[0].wait_recv()
        s.own_fc2[...] += s.ry_last[...].astype(F32)
        stores.append(loads.start(s.own_fc2, out_fc2))

    sums_done = [0, 1]

    def sum_a_until(steps):
        while sums_done[0] < min(steps, ring):
            sum_a_step(order[sums_done[0]])
            sums_done[0] += 1

    def sum_b_until(steps):
        while sums_done[1] < min(steps, ring):
            sum_b_step(order[sums_done[1]])
            sums_done[1] += 1

    def gather_wait(part):
        per = chunk_slots // 2
        gather_until((part + 1) * per - 1, 1)
        for distance in range(part * per, (part + 1) * per):
            for kind in range(2):
                for copy in gather_y[distance, kind]:
                    copy.wait_recv()

    part_out, part_in = s.part_out, s.part_in
    cross_out, cross_in = s.cross_out, s.cross_in
    part_sib, cross = {}, {}

    def hand_part(kind, place):
        total = (grad_two, result)[kind]
        part_out[kind, place] = total[(3, 1)[place]].astype(BF16)
        part_sib[kind, place] = links.send(part_out.at[kind, place], part_in.at[kind, place], sib)

    def hand_cross(kind):
        total = (grad_two, result)[kind]
        part_sib[kind, 0].wait_recv()
        cross_out[kind] = (total[2] + part_in[kind, 0].astype(F32)).astype(BF16)
        cross[kind] = links.send(cross_out.at[kind], cross_in.at[kind], xdev)

    gather_until(2, 1)
    gather_wait(0)
    n2_sib.wait_recv()
    cot_sib.wait_recv()
    no_bias = jnp.zeros((8, chunk), F32)
    bias_total = feed(0, (0, 0), no_bias)
    bias_total = feed(0, (1, 1), bias_total)
    gather_until(ring - 1, 0)
    n2_x.wait_recv()
    n2_far = links.send(n2.at[2], n2.at[3], sib)
    gather_until(ring - 1, 1)
    cot_far.wait_recv()
    bias_total = feed(0, (2, 2), bias_total)
    n2_far.wait_recv()
    bias_total = feed(0, (3, 3), bias_total)
    feed_weights(0, bias_total)
    sum_b_step(1)
    for distance in range(1, chunk_slots // 2):
        sum_send_y(distance)
    feed_result(0)
    if chunks == 2:
        gather_wait(1)
        bias_total = feed(1, (3, 3), no_bias)
        hand_part(0, 0)
        bias_total = feed(1, (2, 2), bias_total)
    else:
        hand_part(0, 0)
    hand_cross(0)
    if chunks == 2:
        bias_total = feed(1, (1, 0), bias_total)
    hand_part(0, 1)
    sum_a_until(1)
    if chunks == 2:
        feed_weights(1, bias_total)
    for distance in range(chunk_slots // 2, ring):
        sum_send_y(distance)
    sum_send_y(0)
    sum_b_until(2)
    if chunks == 2:
        feed_result(1)
    hand_part(1, 0)
    hand_part(1, 1)
    hand_cross(1)
    for image in range(2):
        s.n1_t[:, image * seq : (image + 1) * seq] = n1[image].T
    part_sib[0, 1].wait_recv()
    cross[0].wait_recv()
    grad_mid, grad_branch = stream, s.grad_branch

    def mid_back(step, totals):
        at = pl.ds(pl.multiple_of(step * block, block), block)
        grads = (
            grad_two[0, at, :] + part_in[0, 1, at, :].astype(F32) + cross_in[0, at, :].astype(F32)
        )
        unit_rows, scale = s.unit_two[at, :], s.scale_two[at, :]
        passed = cot_all[0, at, :].astype(F32)
        mid = passed + norm_back(grads, vecs[3:4, :], unit_rows, scale)
        grad_mid[at, :] = mid
        low = mid.astype(BF16)
        grad_branch[0, at, :] = low
        return (
            totals[0] + fold_rows(grads * unit_rows),
            totals[1] + fold_rows(grads),
            totals[2] + fold_rows(low.astype(F32)),
            totals[3] + fold_rows(passed),
        )

    empty = jnp.zeros((8, width), F32)
    gain_two_sum, shift_two_sum, out_bias_sum, fc2_bias_sum = lax.fori_loop(
        0, blocks, mid_back, (empty,) * 4
    )
    branch_back = links.send(grad_branch.at[0], grad_branch.at[1], sib)

    def mixed_back(image):
        grads = mm_nt(grad_branch[image], wout[...])
        for pair in range(pairs):
            s.grad_mixed[image, pair] = grads[:, pair * LANES : (pair + 1) * LANES].astype(BF16)

    grads_pair = s.grads_pair

    def attend_back(image, pair):
        queries, keys = s.q[image, pair], s.k[image, pair]
        values, grads = s.v[image, pair], s.grad_mixed[image, pair]
        keys_t = (keys * score_scale).T
        grad_values = jnp.zeros((seq, LANES), F32)
        grad_keys = jnp.zeros((seq, LANES), F32)
        grad_queries = []
        for half in range(2):
            probs = s.probs[image * 2 * pairs + pair * 2 + half]
            grads_half = grads * lane_half[half]
            grad_values += mm(probs.astype(BF16), grads_half)
            grad_probs = mm_nt(values, grads_half)
            inner = jnp.sum(grad_probs * probs, axis=0, keepdims=True)
            grad_scores = (probs * (grad_probs - inner)).astype(BF16)
            grad_keys += mm(grad_scores, queries * lane_scaled[half])
            grad_queries.append(
                mm(keys_t[half * HEAD_DIM : (half + 1) * HEAD_DIM], grad_scores)
            )
        grad_query = jnp.concatenate(grad_queries, axis=0).T
        for place, value in enumerate(
            (grad_query, grad_keys, grad_values)
        ):
            grads_pair[pair, image, :, place * LANES : (place + 1) * LANES] = value.astype(BF16)

    def rows_back(image):
        total = mm_nt(grads_pair[0, image], w_pair[0])
        for pair in range(1, pairs):
            total += mm_nt(grads_pair[pair, image], w_pair[pair])
        return total

    def weights_back(pair):
        both = grads_pair[pair].reshape(2 * seq, 3 * LANES)
        for base in range(0, width, 256):
            rows = slice(base, base + 256)
            ar[1 + pair, rows, :] = mm(s.n1_t[rows, :], both).astype(BF16)

    mixed_back(0)
    sum_a_until(2)
    sum_b_until(3)
    branch_back.wait_recv()
    mixed_back(1)

    ar = s.ar
    by_core = (one_dev, two_dev, p_one, p_two)
    flat = [
        (ar.at[item], s.ar_one.at[item], s.ar_two.at[item], s.ar_z.at[item],
         s.ar_rest.at[item], s.attn.at[item], width, by_core)
        for item in range(4)
    ]
    small_half = seq // 2
    small = (s.small, s.small_one, s.small_two, s.small_z, s.small_rest,
             s.small_all, small_half, by_core)
    items = flat + [small]
    stages = [dict() for _ in range(7)]

    def piece(item):
        total_rows = items[item][6]
        _, _, p_one, p_two = items[item][7]
        half, quarter, leaf = total_rows // 2, total_rows // 4, total_rows // 16
        at_one = pl.multiple_of(p_one * half, half)
        at_two = pl.multiple_of(at_one + p_two * quarter, quarter)
        return half, quarter, leaf, at_one, at_two

    def reduce_one(item):
        data, one = items[item][0], items[item][1]
        half, _, _, _, _ = piece(item)
        device, _, p_one, _ = items[item][7]
        other = pl.ds(pl.multiple_of((1 - p_one) * half, half), half)
        stages[0][item] = [links.send(data.at[other], one, device)]

    def reduce_two(item):
        data, one, two = items[item][:3]
        half, quarter, _, at_one, _ = piece(item)
        stages[0][item][0].wait_recv()
        mine = pl.ds(at_one, half)
        data[mine] = (data[mine].astype(F32) + one[...].astype(F32)).astype(data.dtype)
        _, device, _, p_two = items[item][7]
        other = pl.ds(pl.multiple_of(at_one + (1 - p_two) * quarter, quarter), quarter)
        stages[1][item] = [links.send(data.at[other], two, device)]

    def reduce_z(item):
        data, _, two, by_z = items[item][:4]
        _, quarter, leaf, _, at_two = piece(item)
        stages[1][item][0].wait_recv()
        mine = pl.ds(at_two, quarter)
        data[mine] = (data[mine].astype(F32) + two[...].astype(F32)).astype(data.dtype)
        stages[2][item] = [
            links.send(
                data.at[pl.ds(pl.multiple_of(at_two + ((zq + hop) % 4) * leaf, leaf), leaf)],
                by_z.at[hop - 1],
                zdev[hop],
            )
            for hop in range(1, 4)
        ]

    def spread_z(item):
        data, _, _, by_z, by_rest, done = items[item][:6]
        _, _, leaf, _, at_two = piece(item)
        for copy in stages[2][item]:
            copy.wait_recv()
        mine = pl.ds(pl.multiple_of(at_two + zq * leaf, leaf), leaf)
        total = data[mine].astype(F32)
        for hop in range(3):
            total += by_z[hop].astype(F32)
        if rest_count > 1:
            by_rest[0] = total.astype(data.dtype)
            copies = [
                links.send(by_rest.at[0], by_rest.at[hop], rdev[hop])
                for hop in range(1, rest_count)
            ]
            for copy in copies:
                copy.wait_recv()
            total = jnp.zeros(total.shape, F32)
            for owner in range(rest_count):
                total += by_rest[(rest - owner + rest_count) % rest_count].astype(F32)
        done[mine] = total.astype(done.dtype)
        stages[3][item] = [
            links.send(done.at[mine], done.at[mine], zdev[hop]) for hop in range(1, 4)
        ]

    def spread_two(item):
        done = items[item][5]
        _, quarter, _, _, at_two = piece(item)
        for copy in stages[3][item]:
            copy.wait_recv()
        mine = pl.ds(at_two, quarter)
        stages[4][item] = [links.send(done.at[mine], done.at[mine], items[item][7][1])]

    def spread_one(item):
        done = items[item][5]
        half, _, _, at_one, _ = piece(item)
        stages[4][item][0].wait_recv()
        mine = pl.ds(at_one, half)
        stages[5][item] = [links.send(done.at[mine], done.at[mine], items[item][7][0])]

    def finish(item):
        stages[5][item][0].wait_recv()
        if item < 4:
            stores.append(loads.start(s.attn.at[item], out_attn.at[item]))

    for half in range(2):
        at = slice(half * local, (half + 1) * local)
        total = mm(s.mixed_t[0], grad_branch[0, :, at]) + mm(
            s.mixed_t[1], grad_branch[1, :, at]
        )
        ar[0, at, :] = total.astype(BF16)
    reduce_one(0)
    for pair in range(pairs):
        attend_back(1, pair)
        attend_back(0, pair)
        weights_back(pair)
        reduce_one(1 + pair)
        if pair == 1:
            sum_a_until(3)
    s.rows_out[...] = rows_back(1).astype(BF16)
    rows_sib = links.send(s.rows_out, s.rows_in, sib)
    reduce_two(0)
    sum_b_until(ring)
    s.branch_own[...] = rows_back(0)
    reduce_two(1)
    reduce_z(0)
    rows_sib.wait_recv()

    def in_back(step, totals):
        at = pl.ds(pl.multiple_of(step * block, block), block)
        grads = (s.branch_own[at, :] + s.rows_in[at, :].astype(F32))
        unit_rows, scale = s.unit_one[at, :], s.scale_one[at, :]
        grad_mid[at, :] += norm_back(grads, vecs[0:1, :], unit_rows, scale)
        return (totals[0] + fold_rows(grads * unit_rows), totals[1] + fold_rows(grads))

    gain_one_sum, shift_one_sum = lax.fori_loop(0, blocks, in_back, (empty,) * 2)
    grad_in = grad_mid[...]
    high = grad_in.astype(BF16)
    low = (grad_in - high.astype(F32)).astype(BF16)
    placed = mm(pick[...], high) + mm(pick[...], low)
    s.own_tok[0] = placed[0:tok_rows]
    stores.append(loads.start(s.own_tok.at[0], out_tok.at[:, 0, :]))

    small_ref, small_own = s.small_full, s.small
    small_ref[...] = jnp.zeros(small_ref.shape, F32)
    part_width = small_ref.shape[1]
    parts = width // part_width
    for part in range(parts):
        small_ref[part * prompt_pad : part * prompt_pad + prompt_pad, :] = placed[
            tok_pad : tok_pad + prompt_pad, part * part_width : (part + 1) * part_width
        ]
    base = parts * prompt_pad
    sums = (gain_one_sum, shift_one_sum, out_bias_sum, gain_two_sum, shift_two_sum, fc2_bias_sum)
    for place, total in enumerate(sums):
        row = jnp.sum(total, axis=0, keepdims=True)
        for part in range(parts):
            at = base + place * parts + part
            small_ref[at : at + 1, :] = row[:, part * part_width : (part + 1) * part_width]
    base += len(sums) * parts
    for place in range(2):
        at = slice(2 * place * LANES, 2 * place * LANES + LANES)
        row = jnp.concatenate(
            [
                jnp.sum(
                    grads_pair[pair, 0, :, at].astype(F32) + grads_pair[pair, 1, :, at].astype(F32),
                    axis=0,
                    keepdims=True,
                )
                for pair in range(pairs)
            ],
            axis=1,
        )
        for head in range(2):
            chosen = row * (h if head == 1 else 1 - h).astype(F32)
            at = base + head * 4 + place * 2
            small_ref[at : at + 1, :] = chosen[:, 0:part_width]
            small_ref[at + 1 : at + 2, 0 : local - part_width] = chosen[:, part_width:local]
    theirs = pl.ds(pl.multiple_of((1 - h) * small_half, small_half), small_half)
    ours = pl.ds(pl.multiple_of(h * small_half, small_half), small_half)
    small_sib = links.send(small_ref.at[theirs], s.small_in.at[1], sib)
    small_sib.wait_recv()
    small_own[...] = small_ref[ours] + s.small_in[1]
    reduce_one(4)
    reduce_two(2)
    reduce_z(1)
    sum_a_until(ring)
    spread_z(0)
    reduce_two(3)
    reduce_z(2)
    sum_b_end()
    spread_z(1)
    spread_two(0)
    reduce_two(4)
    reduce_z(3)
    spread_z(2)
    spread_two(1)
    reduce_z(4)
    spread_one(0)
    spread_z(3)
    spread_z(4)
    spread_two(2)
    spread_one(1)
    part_sib[1, 1].wait_recv()
    cross[1].wait_recv()

    @pl.loop(0, blocks)
    def _(step):
        at = pl.ds(pl.multiple_of(step * block, block), block)
        row_ids = lax.broadcasted_iota(jnp.int32, (block, 1), 0) + step * block
        total = result[0, at, :] + part_in[1, 1, at, :].astype(F32) + cross_in[1, at, :].astype(F32)
        rows = middle[at, :] + (total + vecs[5:6, :])
        s.own_rows[0, at, :] = jnp.where(row_ids < limit, rows, 0.0).astype(BF16)

    stores.append(loads.start(s.own_rows, out_rows))
    spread_two(4)
    spread_two(3)
    spread_one(2)
    spread_one(4)
    spread_one(3)
    finish(0)
    finish(1)
    finish(4)
    final = s.small_out
    final[ours] = s.small_all[...]
    small_back = links.send(s.small_all, s.small_in.at[0], sib)
    finish(2)
    small_back.wait_recv()
    final[theirs] = s.small_in[0]
    final[base + 8 : base + 12, :] = jnp.where(h == 0, final[base : base + 4, :], final[base + 4 : base + 8, :])
    stores.append(loads.start(final, out_small))
    finish(3)
    links.drain()
    for copy in stores:
        copy.wait()


def finish_kernel(dims, *refs):
    it = iter(refs)
    rows_in, tok_in, attn_in, small_in, fc1_in, fc2_in, bias_in = (next(it) for _ in range(7))
    (
        layer_out, grad_tokens, grad_prompts, gain_one, shift_one, w_query, b_query, w_key,
        w_value, b_value, w_out, b_out, gain_two, shift_two, w_fc1, b_fc1, w_fc2, b_fc2,
    ) = (next(it) for _ in range(18))
    s = SimpleNamespace(**dict(zip(dims.finish, it)))
    width, local = dims.width, dims.local
    rows = w_fc1.shape[0]
    loads = Loads(s.load_sems)
    load_attn = [loads.start(attn_in.at[item], s.attn.at[item]) for item in range(4)]
    load_small = loads.start(small_in, s.small)
    load_bias = loads.start(bias_in, s.bias)
    passing = [(rows_in, s.rows, layer_out), (tok_in, s.tok, grad_tokens)]
    if rows == fc1_in.shape[0]:
        passing += [(fc1_in, s.fc1, w_fc1), (fc2_in, s.fc2, w_fc2)]
    passing = [(loads.start(source, held), held, target) for source, held, target in passing]
    stores = []
    if rows != fc1_in.shape[0]:
        for source, held, target in ((fc1_in, s.fc1, w_fc1), (fc2_in, s.fc2, w_fc2)):
            loads.start(source, held).wait()
            s.cut[...] = held[0:rows]
            loads.start(s.cut, target).wait()
    for item in range(4):
        load_attn[item].wait()
        if item == 0:
            s.wide[:, 0:local] = s.attn[0, 0:local].astype(F32)
            s.wide[:, local : 2 * local] = s.attn[0, local : 2 * local].astype(F32)
            stores.append(loads.start(s.wide, w_out))
            continue
        at = slice((item - 1) * LANES, item * LANES)
        for place in range(3):
            s.tall[place, :, at] = s.attn[item, :, place * LANES : (place + 1) * LANES].astype(F32)
    for place, target in enumerate((w_query, w_key, w_value)):
        stores.append(loads.start(s.tall.at[place], target))
    for load, held, target in passing:
        load.wait()
        stores.append(loads.start(held, target))
    load_small.wait()
    load_bias.wait()
    part_width = s.small.shape[1]
    parts = width // part_width
    for part in range(parts):
        at = slice(part * part_width, (part + 1) * part_width)
        s.prompts[:, at] = s.small[part * dims.prompt_pad : part * dims.prompt_pad + dims.prompt_rows]
    stores.append(loads.start(s.prompts, grad_prompts))
    base = parts * dims.prompt_pad
    for place, target in enumerate((gain_one, shift_one, b_out, gain_two, shift_two, b_fc2)):
        for part in range(parts):
            at = base + place * parts + part
            s.row[place : place + 1, part * part_width : (part + 1) * part_width] = s.small[at : at + 1]
        target[...] = s.row[place : place + 1, :].reshape(width)
    base += 6 * parts + 8
    for place, target in enumerate((b_query, b_value)):
        at = base + 2 * place
        s.row[6:7, 0:part_width] = s.small[at : at + 1]
        s.row[6:7, part_width : 2 * part_width] = s.small[at + 1 : at + 2]
        target[...] = s.row[6:7, 0:local].reshape(local)
    b_fc1[...] = s.bias[0:1, 0:rows].reshape(rows)
    for copy in stores:
        copy.wait()


def layer(dims, operands):
    seq, width, local = dims.seq, dims.width, dims.local
    n, ring, slots, rows_per = dims.n, dims.ring, dims.slots, dims.rows_per
    pairs = local // LANES
    chunk = dims.chunk_slots * rows_per
    rest_count = n // 16
    small_half = seq // 2
    part_width = 256
    copies = 6 * ring + 4 * ring + 40 + 5 * (10 + rest_count)
    vmem = pltpu.VMEM
    shared = 2 * rows_per
    scratch = dict(
        send_sems=pltpu.SemaphoreType.DMA((copies,)),
        recv_sems=pltpu.SemaphoreType.DMA((copies,)),
        w_all=vmem((slots, shared, width), BF16),
        b_all=vmem((slots, 8, LANES), F32),
        cot_all=vmem((4, seq, width), BF16),
        meta=vmem((2, 8, LANES), jnp.int32),
        load_sems=pltpu.SemaphoreType.DMA((36,)),
        kept=vmem((1, dims.patches), jnp.int32),
        tokens=vmem((1, dims.tok_rows, width), BF16),
        prompts=vmem((dims.prompt_rows, width), BF16),
        gain_one=vmem((width,), BF16),
        shift_one=vmem((width,), BF16),
        b_query=vmem((local,), BF16),
        b_value=vmem((local,), BF16),
        b_out=vmem((width,), BF16),
        gain_two=vmem((width,), BF16),
        shift_two=vmem((width,), BF16),
        b_fc1=vmem((dims.rows,), BF16),
        b_fc2=vmem((width,), BF16),
        vecs=vmem((8, width), F32),
        w_pair=vmem((pairs, width, 3 * LANES), BF16),
        wout=vmem((local, width), BF16),
        unit_one=vmem((seq, width), F32),
        unit_two=vmem((seq, width), F32),
        scale_one=vmem((seq, 1), F32),
        scale_two=vmem((seq, 1), F32),
        own_rows=vmem((1, seq, width), BF16),
        own_tok=vmem((1, dims.tok_rows, width), F32),
        own_fc1=vmem((rows_per, width), F32),
        own_fc2=vmem((rows_per, width), F32),
        own_bias=vmem((8, LANES), F32),
        attn=vmem((4, width, local), BF16),
        src=vmem((dims.tok_pad + dims.prompt_pad, width), BF16),
        pick=vmem((dims.tok_pad + dims.prompt_pad, seq), BF16),
        idx=vmem((8, seq), jnp.int32),
        stream=vmem((seq, width), F32),
        middle=vmem((seq, width), F32),
        n1=vmem((2, seq, width), BF16),
        n2=vmem((4, seq, width), BF16),
        q=vmem((2, pairs, seq, LANES), BF16),
        k=vmem((2, pairs, seq, LANES), BF16),
        v=vmem((2, pairs, seq, LANES), BF16),
        probs=vmem((4 * pairs, seq, seq), F32),
        mixed_t=vmem((2, local, seq), BF16),
        branch_out=vmem((seq, width), F32),
        branch_in=vmem((seq, width), F32),
        branch_own=vmem((seq, width), F32),
        hidden=vmem((slots // dims.chunk_slots, 4, seq, chunk), BF16),
        grad_before=vmem((4, seq, chunk), BF16),
        result=vmem((4, seq, width), F32),
        grad_two=vmem((4, seq, width), F32),
        part_out=vmem((2, 2, seq, width), BF16),
        part_in=vmem((2, 2, seq, width), BF16),
        cross_out=vmem((2, seq, width), BF16),
        cross_in=vmem((2, seq, width), BF16),
        g_all=vmem((slots, shared, width), BF16),
        gb_all=vmem((slots, 8, LANES), F32),
        ry=vmem((ring, rows_per, width), BF16),
        ry_last=vmem((rows_per, width), BF16),
        rb_out=vmem((ring, 2, rows_per, width), BF16),
        rb_in=vmem((ring, 2, rows_per, width), BF16),
        n1_t=vmem((width, 2 * seq), BF16),
        ryb=vmem((ring, 8, LANES), F32),
        rz_out=vmem((ring, rows_per, width), BF16),
        rzb_out=vmem((ring, 8, LANES), F32),
        rz_in=vmem((ring, rows_per, width), BF16),
        rzb_in=vmem((ring, 8, LANES), F32),
        grad_branch=vmem((2, seq, width), BF16),
        grad_mixed=vmem((2, pairs, seq, LANES), BF16),
        grads_pair=vmem((pairs, 2, seq, 3 * LANES), BF16),
        rows_out=vmem((seq, width), BF16),
        rows_in=vmem((seq, width), BF16),
        ar=vmem((4, width, local), BF16),
        ar_one=vmem((4, width // 2, local), BF16),
        ar_two=vmem((4, width // 4, local), BF16),
        ar_z=vmem((4, 3, width // 16, local), BF16),
        ar_rest=vmem((4, rest_count, width // 16, local), BF16),
        small_full=vmem((seq, part_width), F32),
        small_out=vmem((seq, part_width), F32),
        small_in=vmem((2, small_half, part_width), F32),
        small=vmem((small_half, part_width), F32),
        small_one=vmem((small_half // 2, part_width), F32),
        small_two=vmem((small_half // 4, part_width), F32),
        small_z=vmem((3, small_half // 16, part_width), F32),
        small_rest=vmem((rest_count, small_half // 16, part_width), F32),
        small_all=vmem((small_half, part_width), F32),
    )
    dims = SimpleNamespace(**vars(dims), scratch=tuple(scratch))
    anywhere = pl.BlockSpec(memory_space=pl.ANY)
    shape = jax.ShapeDtypeStruct
    return pl.pallas_call(
        functools.partial(layer_kernel, dims),
        out_shape=(
            shape((1, seq, width), BF16),
            shape((dims.tok_rows, 1, width), F32),
            shape((4, width, local), BF16),
            shape((seq, part_width), F32),
            shape((rows_per, width), F32),
            shape((rows_per, width), F32),
            shape((8, LANES), F32),
        ),
        in_specs=[pl.BlockSpec(memory_space=pltpu.SMEM)] + [anywhere] * (len(operands) - 1),
        out_specs=[anywhere] * 7,
        scratch_shapes=list(scratch.values()),
        compiler_params=pltpu.CompilerParams(
            collective_id=0, has_side_effects=True, vmem_limit_bytes=63 * 2**20
        ),
    )(*operands)


def finish(dims, results):
    seq, width, local, rows = dims.seq, dims.width, dims.local, dims.rows
    vmem = pltpu.VMEM
    scratch = dict(
        load_sems=pltpu.SemaphoreType.DMA((28,)),
        attn=vmem((4, width, local), BF16),
        wide=vmem((local, width), F32),
        tall=vmem((3, width, local), F32),
        small=vmem(results[3].shape, F32),
        bias=vmem((8, LANES), F32),
        prompts=vmem((dims.prompt_rows, width), F32),
        row=vmem((8, width), F32),
        rows=vmem((1, seq, width), BF16),
        tok=vmem((dims.tok_rows, 1, width), F32),
        fc1=vmem((dims.rows_per, width), F32),
        fc2=vmem((dims.rows_per, width), F32),
        cut=vmem((rows, width), F32),
    )
    dims = SimpleNamespace(**vars(dims), finish=tuple(scratch))
    anywhere = pl.BlockSpec(memory_space=pl.ANY)
    whole = pl.BlockSpec(memory_space=pltpu.VMEM)

    def out(*sizes, dtype=F32):
        return jax.ShapeDtypeStruct(sizes, dtype)

    shapes = (
        out(1, seq, width, dtype=BF16), out(dims.tok_rows, 1, width), out(dims.prompt_rows, width),
        out(width), out(width), out(width, local), out(local), out(width, local),
        out(width, local), out(local), out(local, width), out(width), out(width), out(width),
        out(rows, width), out(rows), out(rows, width), out(width),
    )
    return pl.pallas_call(
        functools.partial(finish_kernel, dims),
        out_shape=shapes,
        in_specs=[anywhere] * 7,
        out_specs=[whole if len(shape.shape) == 1 else anywhere for shape in shapes],
        scratch_shapes=list(scratch.values()),
        compiler_params=pltpu.CompilerParams(vmem_limit_bytes=60 * 2**20),
    )(*results)


def body(n, *arguments):
    (
        tokens, kept_index, kept_count, prompts, gain_one, shift_one, w_query, b_query, w_key,
        w_value, b_value, w_out, b_out, gain_two, shift_two, w_fc1, b_fc1, w_fc2, b_fc2, cotangent,
    ) = arguments
    seq, width = cotangent.shape[1:]
    local = w_query.shape[1]
    rows = w_fc1.shape[0]
    rows_per = round_up(rows, 16)
    ring = n // 4
    slots = 2 * ring
    halves = slots // 2
    chunk_slots = halves if (halves % 2 == 0 and halves * rows_per % LANES == 0) else slots
    tok_rows, prompt_rows = tokens.shape[1], prompts.shape[0]
    dims = SimpleNamespace(
        n=n, ring=ring, slots=slots, chunk_slots=chunk_slots, rows_per=rows_per, rows=rows, seq=seq,
        width=width, local=local, tok_rows=tok_rows, tok_pad=round_up(tok_rows, 16),
        prompt_rows=prompt_rows, prompt_pad=round_up(prompt_rows, 16),
        patches=kept_index.shape[1],
    )
    if rows_per != rows:
        spare = ((0, rows_per - rows), (0, 0))
        w_fc1, w_fc2 = jnp.pad(w_fc1, spare), jnp.pad(w_fc2, spare)
    operands = (
        kept_count, tokens, kept_index, prompts, w_fc1, w_fc2, cotangent, w_query, w_key, w_value,
        w_out, gain_one, shift_one, b_query, b_value, b_out, gain_two, shift_two, b_fc1, b_fc2,
    )
    outs = list(finish(dims, layer(dims, operands)))
    outs[1] = outs[1].transpose(1, 0, 2)
    return tuple(outs)


def solution(mesh):
    batch, head = mesh.axis_names
    both = (batch, head)
    placed = (
        P(both, None, None), P(both, None), P(both), P(), P(), P(), P(None, head), P(head),
        P(None, head), P(None, head), P(head), P(head, None), P(), P(), P(),
        P(both, None), P(both), P(both, None), P(), P(both, None, None),
    )
    return jax.shard_map(
        functools.partial(body, mesh.shape[batch]),
        mesh=mesh,
        in_specs=placed,
        out_specs=(
            P(both, None, None), P(both, None, None), P(), P(), P(), P(None, head), P(head),
            P(None, head), P(None, head), P(head), P(head, None), P(), P(), P(),
            P(both, None), P(both), P(both, None), P(),
        ),
        check_vma=False,
    )
```

```python
import functools
from types import SimpleNamespace

import jax
import jax.numpy as jnp
from jax import lax
from jax.experimental import pallas as pl
from jax.experimental.pallas import tpu as pltpu
from jax.sharding import PartitionSpec as P

MESH = pl.DeviceIdType.MESH
HEAD_DIM = 64
EPSILON = 1e-06
LANES = 128
BF16 = jnp.bfloat16
F32 = jnp.float32


def round_up(value, step):
    return -(-value // step) * step


def mm(left, right):
    return lax.dot_general(left, right, (((1,), (0,)), ((), ())), preferred_element_type=F32)


def mm_nt(left, right):
    return lax.dot_general(left, right, (((1,), (1,)), ((), ())), preferred_element_type=F32)


def mm_tn(left, right):
    return lax.dot_general(left, right, (((0,), (0,)), ((), ())), preferred_element_type=F32)


def fold_rows(rows):
    count, width = rows.shape
    return jnp.sum(rows.reshape(count // 8, 8, width), axis=0)


def normalise(rows):
    width = rows.shape[1]
    centre = jnp.sum(rows, axis=1, keepdims=True) * (1.0 / width)
    centred = rows - centre
    spread = jnp.sum(centred * centred, axis=1, keepdims=True) * (1.0 / width)
    scale = lax.rsqrt(spread + EPSILON)
    return centred * scale, scale


def norm_back(grad_rows, gain_row, unit_rows, scale):
    width = grad_rows.shape[1]
    scaled = grad_rows * gain_row
    mean_one = jnp.sum(scaled, axis=1, keepdims=True) * (1.0 / width)
    mean_two = jnp.sum(scaled * unit_rows, axis=1, keepdims=True) * (1.0 / width)
    return scale * (scaled - mean_one - unit_rows * mean_two)


GELU_A = 0.7978845608028654
GELU_B = 0.044715


def gelu_both(value):
    square = value * value
    bend = jnp.tanh(value * (GELU_A + (GELU_A * GELU_B) * square))
    half = 0.5 + 0.5 * bend
    slope = half + (0.5 * value) * (1.0 - bend * bend) * (
        GELU_A + (3.0 * GELU_A * GELU_B) * square
    )
    return value * half, slope


VECTORS = (
    "gain_one", "shift_one", "b_query", "b_value", "b_out", "gain_two", "shift_two", "b_fc1", "b_fc2",
)


LATE_SUM = (8, 1)
REDUCE_ORDER = (
    (0, 0), (-1, 0), (3, 0), (-2, 0), (5, 0), (1, 0), (-3, 0), (4, 0), (7, 0), (3, 1), (0, 1),
    (5, 1), (2, 0), (1, 1), (3, 2), (0, 2), (4, 1), (5, 2), (1, 2), (3, 3), (-4, 0), (7, 1),
    (6, 0), (0, 3), (1, 3), (7, 2), (4, 2), (2, 1), (3, 4), (-5, 0), (1, 4), (5, 3), (0, 4),
    (6, 1), (-6, 0), (7, 3), (2, 2), (-7, 0), (4, 3), (8, 0), (3, 5), (1, 5), (5, 4), (7, 4),
    (6, 2), (-8, 0), (8, 1), (2, 3), (0, 5), (6, 3), (5, 5), (4, 4), (8, 2), (2, 4), (7, 5),
    (6, 4), (3, 6), (4, 5), (8, 3), (2, 5), (7, 6), (8, 4), (5, 6), (6, 5), (0, 6), (4, 6), (8, 5),
    (6, 6), (1, 6), (2, 6), (8, 6),
)


class Loads:
    def __init__(self, sems):
        self.sems = sems
        self.count = 0

    def start(self, source, target):
        copy = pltpu.make_async_copy(source, target, self.sems.at[self.count])
        copy.start()
        self.count += 1
        return copy


class Links:
    def __init__(self, send_sems, recv_sems):
        self.send_sems = send_sems
        self.recv_sems = recv_sems
        self.copies = []

    def send(self, source, target, device):
        place = len(self.copies)
        copy = pltpu.make_async_remote_copy(
            src_ref=source,
            dst_ref=target,
            send_sem=self.send_sems.at[place],
            recv_sem=self.recv_sems.at[place],
            device_id=device,
            device_id_type=MESH,
        )
        copy.start()
        self.copies.append(copy)
        return copy

    def drain(self):
        for copy in self.copies:
            copy.wait_send()


def layer_kernel(dims, *refs):
    it = iter(refs)
    count_ref = next(it)
    tokens, kept, prompts, fc1, fc2, cot = (next(it) for _ in range(6))
    weights_in = [next(it) for _ in range(4)]
    vectors_in = [next(it) for _ in range(9)]
    out_rows, out_tok, out_attn, out_small, out_fc1, out_fc2, out_bias = (
        next(it) for _ in range(7)
    )
    s = SimpleNamespace(**dict(zip(dims.scratch, it)))
    w_pair, wout = s.w_pair, s.wout
    vecs = s.vecs
    seq, width, local = dims.seq, dims.width, dims.local
    pairs = local // LANES
    rows_per = dims.rows_per
    n, ring, slots = dims.n, dims.ring, dims.slots
    chunk_slots = dims.chunk_slots
    chunk = chunk_slots * rows_per
    chunks = slots // chunk_slots
    tok_rows, tok_pad, prompt_pad = dims.tok_rows, dims.tok_pad, dims.prompt_pad
    prompt_rows, patches = dims.prompt_rows, dims.patches
    rest_count = n // 16
    score_scale = HEAD_DIM**-0.5
    block = 32
    blocks = seq // block

    b = lax.axis_index("batch")
    h = lax.axis_index("head")
    bx = b % 2
    by = (b // 2) % 2
    zz = b // 4
    sib = (b, 1 - h)
    xdev = (b + 1 - 2 * bx, h)
    ydev = (b + 2 - 4 * by, h)
    corner = b % 4
    ring_next = (((zz + 1) % ring) * 4 + corner, h)
    ring_prev = (((zz + ring - 1) % ring) * 4 + corner, h)
    zq = zz % 4
    zdev = [((zz - zq + (zq + hop) % 4) * 4 + corner, h) for hop in range(4)]
    rest = b // 16
    rdev = [(((rest + hop) % rest_count) * 16 + b % 16, h) for hop in range(rest_count)]
    one_dev = (xdev[0] * (1 - h) + ydev[0] * h, h)
    two_dev = (ydev[0] * (1 - h) + xdev[0] * h, h)
    p_one = bx * (1 - h) + by * h
    p_two = by * (1 - h) + bx * h

    partners = [sib, xdev, ydev] + zdev[1:]
    if ring > 4:
        partners += [ring_next, ring_prev] + rdev[1:]
    barrier = pltpu.get_barrier_semaphore()
    for partner in partners:
        pl.semaphore_signal(barrier, inc=1, device_id=partner, device_id_type=MESH)

    links = Links(s.send_sems, s.recv_sems)

    w_all, b_all, cot_all = s.w_all, s.b_all, s.cot_all
    loads = Loads(s.load_sems)
    load_kept = loads.start(kept, s.kept)
    load_fc = [
        loads.start(fc1, w_all.at[0, pl.ds(0, rows_per)]),
        loads.start(fc2, w_all.at[0, pl.ds(rows_per, rows_per)]),
    ]
    load_cot = loads.start(cot.at[0], cot_all.at[0])
    load_rows = [loads.start(tokens, s.tokens), loads.start(prompts, s.prompts)]
    load_vectors = [loads.start(ref, getattr(s, name)) for ref, name in zip(vectors_in, VECTORS)]
    load_weights = [loads.start(weights_in[3], wout)]
    for pair in range(pairs):
        for place in range(3):
            load_weights.append(
                loads.start(
                    weights_in[place].at[:, pl.ds(pair * LANES, LANES)],
                    w_pair.at[pair, :, pl.ds(place * LANES, LANES)],
                )
            )

    limit = count_ref[0] + (1 + prompt_rows)
    src, pick = s.src, s.pick
    s.meta[0] = jnp.broadcast_to(limit, (8, LANES))
    s.idx[...] = jnp.zeros((8, seq), jnp.int32)
    src[tok_rows - tok_rows % 16 : tok_pad] = jnp.zeros((tok_pad - tok_rows + tok_rows % 16, width), BF16)
    src[tok_pad:] = jnp.zeros((prompt_pad, width), BF16)
    vecs[...] = jnp.zeros(vecs.shape, F32)
    load_kept.wait()
    s.idx[0:1, 0:patches] = s.kept[...]
    shifted = pltpu.roll(s.idx[...], 1 + prompt_rows, axis=1)[0:1, :]
    spot = lax.broadcasted_iota(jnp.int32, (1, seq), 1)
    wanted = jnp.where(
        spot < 1 + prompt_rows,
        jnp.where(spot == 0, 0, tok_pad - 1 + spot),
        jnp.where(spot < limit, shifted + 1, -1),
    )
    pick[...] = jnp.where(
        lax.broadcasted_iota(jnp.int32, pick.shape, 0) == wanted, 1.0, 0.0
    ).astype(BF16)
    for copy in load_vectors:
        copy.wait()
    for place, name in enumerate(("gain_one", "shift_one", "b_out", "gain_two", "shift_two", "b_fc2")):
        vecs[place : place + 1, :] = getattr(s, name)[...].astype(F32).reshape(1, width)
    vecs[6:7, 0:local] = s.b_query[...].astype(F32).reshape(1, local)
    vecs[6:7, local : 2 * local] = s.b_value[...].astype(F32).reshape(1, local)
    bias_rows = s.b_fc1.shape[0]
    vecs[7:8, 0:bias_rows] = s.b_fc1[...].astype(F32).reshape(1, bias_rows)
    b_all[0] = jnp.broadcast_to(vecs[7:8, 0:LANES], (8, LANES))
    load_cot.wait()

    @pl.loop(0, blocks, unroll=4)
    def _(step):
        at = pl.ds(pl.multiple_of(step * block, block), block)
        row_ids = lax.broadcasted_iota(jnp.int32, (block, 1), 0) + step * block
        rows = cot_all[0, at, :].astype(F32)
        cot_all[0, at, :] = jnp.where(row_ids < limit, rows, 0.0).astype(BF16)

    for copy in load_rows:
        copy.wait()
    src[0:tok_rows, :] = s.tokens[0]
    src[tok_pad : tok_pad + prompt_rows, :] = s.prompts[...]
    stream = s.stream
    stream[...] = mm_tn(pick[...], src[...])

    n1 = s.n1

    @pl.loop(0, blocks, unroll=4)
    def _(step):
        at = pl.ds(pl.multiple_of(step * block, block), block)
        unit_rows, s.scale_one[at, :] = normalise(stream[at, :])
        s.unit_one[at, :] = unit_rows
        n1[0, at, :] = (unit_rows * vecs[0:1, :] + vecs[1:2, :]).astype(BF16)

    for copy in load_fc:
        copy.wait()
    pl.semaphore_wait(barrier, len(partners))

    gather_ring, gather_y = {}, {}

    def gather_step(distance, kind):
        if distance > 0:
            for copy in gather_ring[distance, kind]:
                copy.wait_recv()
        rows = pl.ds(kind * rows_per, rows_per)
        mine = 2 * distance

        def hand_on(slot, device):
            copies = [links.send(w_all.at[mine, rows], w_all.at[slot, rows], device)]
            if kind == 0:
                copies.append(links.send(b_all.at[mine], b_all.at[slot], device))
            return copies

        if distance + 1 < ring:
            gather_ring[distance + 1, kind] = hand_on(mine + 2, ring_next)
        gather_y[distance, kind] = hand_on(mine + 1, ydev)

    gather_done = [0]

    def gather_until(distance, kind):
        while gather_done[0] <= min(2 * distance + kind, 2 * ring - 1):
            gather_step(gather_done[0] // 2, gather_done[0] % 2)
            gather_done[0] += 1

    n1_sib = links.send(n1.at[0], n1.at[1], sib)
    gather_until(0, 1)
    cot_x = links.send(cot_all.at[0], cot_all.at[2], xdev)
    cot_sib = links.send(cot_all.at[0], cot_all.at[1], sib)
    meta_sib = links.send(s.meta.at[0], s.meta.at[1], sib)


    def project(image):
        rows = n1[image]
        for pair in range(pairs):
            found = mm(rows, w_pair[pair])
            at = slice(pair * LANES, (pair + 1) * LANES)
            s.q[image, pair] = (found[:, 0:LANES] + vecs[6:7, at]).astype(BF16)
            s.k[image, pair] = found[:, LANES : 2 * LANES].astype(BF16)
            at = slice(local + pair * LANES, local + (pair + 1) * LANES)
            s.v[image, pair] = (found[:, 2 * LANES :] + vecs[6:7, at]).astype(BF16)

    lane_ids = lax.broadcasted_iota(jnp.int32, (1, LANES), 1)
    lane_half = [
        jnp.where(lane_ids // HEAD_DIM == half, 1.0, 0.0).astype(BF16) for half in range(2)
    ]
    lane_scaled = [
        jnp.where(lane_ids // HEAD_DIM == half, score_scale, 0.0).astype(BF16) for half in range(2)
    ]
    lane_spare = [
        jnp.where(lane_ids == (1 - half) * HEAD_DIM, 1.0, 0.0).astype(BF16) for half in range(2)
    ]
    key_ids = lax.broadcasted_iota(jnp.int32, (seq, 1), 0)

    def attend(image, first, last):
        key_bias = jnp.where(key_ids < s.meta[image, 0:1, 0:1], 0.0, -1e30).astype(BF16)

        for pair in range(first, last):
            queries, keys = s.q[image, pair], s.k[image, pair]
            values_t = s.v[image, pair].T
            for half in range(2):
                scores = mm_nt(
                    keys * lane_half[half] + key_bias * lane_spare[half],
                    queries * lane_scaled[half] + lane_spare[half],
                )
                weights = jnp.exp(scores - jnp.max(scores, axis=0, keepdims=True))
                probs = weights * (1.0 / jnp.sum(weights, axis=0, keepdims=True))
                s.probs[image * 2 * pairs + pair * 2 + half] = probs
                mixed_t = mm(values_t[half * HEAD_DIM : (half + 1) * HEAD_DIM], probs.astype(BF16))
                at = pl.ds(pair * LANES + half * HEAD_DIM, HEAD_DIM)
                s.mixed_t[image, at, :] = mixed_t.astype(BF16)

    for copy in load_weights:
        copy.wait()
    project(0)
    n1_sib.wait_recv()
    meta_sib.wait_recv()
    project(1)
    attend(1, 0, pairs)
    s.branch_out[...] = mm_tn(s.mixed_t[1], wout[...])
    branch_sib = links.send(s.branch_out, s.branch_in, sib)
    gather_until(1, 0)
    attend(0, 0, pairs)
    gather_until(1, 1)
    s.branch_own[...] = mm_tn(s.mixed_t[0], wout[...])
    branch_sib.wait_recv()
    middle, n2 = s.middle, s.n2

    @pl.loop(0, blocks, unroll=4)
    def _(step):
        at = pl.ds(pl.multiple_of(step * block, block), block)
        rows = stream[at, :] + (s.branch_own[at, :] + s.branch_in[at, :] + vecs[2:3, :])
        middle[at, :] = rows
        unit_rows, s.scale_two[at, :] = normalise(rows)
        s.unit_two[at, :] = unit_rows
        n2[0, at, :] = (unit_rows * vecs[3:4, :] + vecs[4:5, :]).astype(BF16)

    n2_x = links.send(n2.at[0], n2.at[2], xdev)
    n2_sib = links.send(n2.at[0], n2.at[1], sib)
    gather_until(2, 0)
    cot_x.wait_recv()
    cot_far = links.send(cot_all.at[2], cot_all.at[3], sib)
    hidden_all, before_all = s.hidden, s.grad_before
    result, grad_two = s.result, s.grad_two
    unpack = jnp.where(
        lax.broadcasted_iota(jnp.int32, (LANES, chunk), 1) % rows_per
        == lax.broadcasted_iota(jnp.int32, (LANES, chunk), 0),
        1.0,
        0.0,
    )
    owner_of = (
        lax.broadcasted_iota(jnp.int32, (chunk_slots, chunk), 1) // rows_per
        == lax.broadcasted_iota(jnp.int32, (chunk_slots, chunk), 0)
    )

    def feed_spans(part):
        span = slice(part * chunk_slots, (part + 1) * chunk_slots)
        return (
            w_all[span, 0:rows_per].reshape(chunk, width),
            w_all[span, rows_per : 2 * rows_per].reshape(chunk, width),
        )

    def feed(part, images, totals):
        span = slice(part * chunk_slots, (part + 1) * chunk_slots)
        tiles = b_all[span, 0, :].astype(BF16)
        bias_row = jnp.sum(
            jnp.where(owner_of, mm(tiles, unpack.astype(BF16)), 0.0), axis=0, keepdims=True
        )
        up, down = feed_spans(part)
        for image in images:
            before = mm_nt(n2[image], up) + bias_row
            hidden, slope = gelu_both(before)
            hidden_all[part, image] = hidden.astype(BF16)
            grad_before = (mm_nt(cot_all[image], down) * slope).astype(BF16)
            before_all[image] = grad_before
            if part == 0:
                grad_two[image] = mm(grad_before, up)
            else:
                grad_two[image] += mm(grad_before, up)
            totals += fold_rows(grad_before.astype(F32))
        return totals

    def feed_result(part):
        @pl.loop(0, 4)
        def _(image):
            _, down = feed_spans(part)
            if part == 0:
                result[image] = mm(hidden_all[part, image], down)
            else:
                result[image] += mm(hidden_all[part, image], down)

    g_all, gb_all = s.g_all, s.gb_all

    def feed_weights(part, bias_total):
        first = part * chunk_slots
        span = slice(first, first + chunk_slots)

        for left, right, base in ((before_all, n2, 0), (hidden_all.at[part], cot_all, rows_per)):
            total = jnp.zeros((chunk, width), F32)
            for image in range(4):
                total += mm_tn(left[image], right[image])
            g_all[span, base : base + rows_per] = (
                total.astype(BF16).reshape(chunk_slots, rows_per, width)
            )
        bias_row = jnp.sum(bias_total, axis=0, keepdims=True)
        spread = jnp.where(owner_of, jnp.broadcast_to(bias_row, owner_of.shape), 0.0)
        high = spread.astype(BF16)
        low = (spread - high.astype(F32)).astype(BF16)
        packed = mm_nt(high, unpack.astype(BF16)) + mm_nt(low, unpack.astype(BF16))
        for slot in range(chunk_slots):
            gb_all[first + slot] = jnp.broadcast_to(packed[slot : slot + 1], (8, LANES))

    order = list(range(1, ring)) + [0]
    stores = []
    sum_y, sum_ring, sum_both, sum_last = {}, {}, {}, []
    first_rows, second_rows = pl.ds(0, rows_per), pl.ds(rows_per, rows_per)

    def sum_send_y(distance):
        slot = 2 * distance + 1
        sum_y[distance] = [
            links.send(g_all.at[slot, first_rows], s.ry.at[distance], ydev),
            links.send(gb_all.at[slot], s.ryb.at[distance], ydev),
        ]

    def sum_a_step(distance):
        for copy in sum_y[distance]:
            copy.wait_recv()
        mine = 2 * distance
        total = g_all[mine, 0:rows_per].astype(F32) + s.ry[distance].astype(F32)
        bias = gb_all[mine] + s.ryb[distance]
        if distance != 1:
            before = (distance + ring - 1) % ring
            for copy in sum_ring[before]:
                copy.wait_recv()
            total += s.rz_in[before].astype(F32)
            bias += s.rzb_in[before]
        if distance == 0:
            s.own_fc1[...] = total
            s.own_bias[...] = bias
            stores.append(loads.start(s.own_fc1, out_fc1))
            stores.append(loads.start(s.own_bias, out_bias))
        else:
            s.rz_out[distance] = total.astype(BF16)
            s.rzb_out[distance] = bias
            sum_ring[distance] = [
                links.send(s.rz_out.at[distance], s.rz_in.at[distance], ring_next),
                links.send(s.rzb_out.at[distance], s.rzb_in.at[distance], ring_next),
            ]

    def sum_b_step(distance):
        if distance == 1:
            source = g_all.at[pl.ds(2, 2), second_rows]
            sum_both[1] = links.send(source, s.rb_in.at[1], ring_next)
            return
        before = (distance + ring - 1) % ring
        sum_both[before].wait_recv()
        for line in range(2):
            total = g_all[2 * distance + line, rows_per:].astype(F32) + s.rb_in[before, line].astype(F32)
            if distance == 0 and line == 0:
                s.own_fc2[...] = total
            else:
                s.rb_out[distance, line] = total.astype(BF16)
        if distance == 0:
            sum_last.append(links.send(s.rb_out.at[0, 1], s.ry_last, ydev))
        else:
            sum_both[distance] = links.send(s.rb_out.at[distance], s.rb_in.at[distance], ring_next)

    def sum_b_end():
        sum_last[0].wait_recv()
        s.own_fc2[...] += s.ry_last[...].astype(F32)
        stores.append(loads.start(s.own_fc2, out_fc2))

    sums_done = [0, 1]

    def sum_a_until(steps):
        while sums_done[0] < min(steps, ring):
            sum_a_step(order[sums_done[0]])
            sums_done[0] += 1

    def sum_b_until(steps):
        while sums_done[1] < min(steps, ring):
            sum_b_step(order[sums_done[1]])
            sums_done[1] += 1

    def gather_wait(part):
        per = chunk_slots // 2
        gather_until((part + 1) * per - 1, 1)
        for distance in range(part * per, (part + 1) * per):
            for kind in range(2):
                for copy in gather_y[distance, kind]:
                    copy.wait_recv()

    part_out, part_in = s.part_out, s.part_in
    cross_out, cross_in = s.cross_out, s.cross_in
    part_sib, cross = {}, {}

    def hand_part(kind, place):
        total = (grad_two, result)[kind]
        part_out[kind, place] = total[(3, 1)[place]].astype(BF16)
        part_sib[kind, place] = links.send(part_out.at[kind, place], part_in.at[kind, place], sib)

    def hand_cross(kind):
        total = (grad_two, result)[kind]
        part_sib[kind, 0].wait_recv()
        cross_out[kind] = (total[2] + part_in[kind, 0].astype(F32)).astype(BF16)
        cross[kind] = links.send(cross_out.at[kind], cross_in.at[kind], xdev)

    gather_until(2, 1)
    gather_wait(0)
    n2_sib.wait_recv()
    cot_sib.wait_recv()
    no_bias = jnp.zeros((8, chunk), F32)
    bias_total = feed(0, (0, 1), no_bias)
    gather_until(ring - 1, 0)
    n2_x.wait_recv()
    n2_far = links.send(n2.at[2], n2.at[3], sib)
    gather_until(ring - 1, 1)
    cot_far.wait_recv()
    bias_total = feed(0, (2,), bias_total)
    n2_far.wait_recv()
    bias_total = feed(0, (3,), bias_total)
    feed_weights(0, bias_total)
    sum_b_step(1)
    for distance in range(1, chunk_slots // 2):
        sum_send_y(distance)
    feed_result(0)
    if chunks == 2:
        gather_wait(1)
        bias_total = feed(1, (3,), no_bias)
        hand_part(0, 0)
        bias_total = feed(1, (2,), bias_total)
    else:
        hand_part(0, 0)
    hand_cross(0)
    if chunks == 2:
        bias_total = feed(1, (0, 1), bias_total)
    hand_part(0, 1)
    sum_a_until(1)
    if chunks == 2:
        feed_weights(1, bias_total)
    for distance in range(chunk_slots // 2, ring):
        sum_send_y(distance)
    sum_send_y(0)
    sum_b_until(2)
    if chunks == 2:
        feed_result(1)
    hand_part(1, 0)
    hand_part(1, 1)
    hand_cross(1)
    for image in range(2):
        s.n1_t[:, image * seq : (image + 1) * seq] = n1[image].T
    sum_a_until(2)
    part_sib[0, 1].wait_recv()
    cross[0].wait_recv()
    grad_mid, grad_branch = stream, s.grad_branch

    def mid_back(step, totals):
        at = pl.ds(pl.multiple_of(step * block, block), block)
        grads = (
            grad_two[0, at, :] + part_in[0, 1, at, :].astype(F32) + cross_in[0, at, :].astype(F32)
        )
        unit_rows, scale = s.unit_two[at, :], s.scale_two[at, :]
        passed = cot_all[0, at, :].astype(F32)
        mid = passed + norm_back(grads, vecs[3:4, :], unit_rows, scale)
        grad_mid[at, :] = mid
        low = mid.astype(BF16)
        grad_branch[0, at, :] = low
        return (
            totals[0] + fold_rows(grads * unit_rows),
            totals[1] + fold_rows(grads),
            totals[2] + fold_rows(low.astype(F32)),
            totals[3] + fold_rows(passed),
        )

    empty = jnp.zeros((8, width), F32)
    gain_two_sum, shift_two_sum, out_bias_sum, fc2_bias_sum = lax.fori_loop(
        0, blocks, mid_back, (empty,) * 4, unroll=4
    )
    branch_back = links.send(grad_branch.at[0], grad_branch.at[1], sib)

    def mixed_back(image):
        grads = mm_nt(grad_branch[image], wout[...])
        for pair in range(pairs):
            s.grad_mixed[image, pair] = grads[:, pair * LANES : (pair + 1) * LANES].astype(BF16)

    grads_pair = s.grads_pair

    def attend_back(image, pair):
        queries, keys = s.q[image, pair], s.k[image, pair]
        values, grads = s.v[image, pair], s.grad_mixed[image, pair]
        keys_t = (keys * score_scale).T
        grad_values = jnp.zeros((seq, LANES), F32)
        grad_keys = jnp.zeros((seq, LANES), F32)
        grad_queries = []
        for half in range(2):
            probs = s.probs[image * 2 * pairs + pair * 2 + half]
            grads_half = grads * lane_half[half]
            grad_values += mm(probs.astype(BF16), grads_half)
            grad_probs = mm_nt(values, grads_half)
            inner = jnp.sum(grad_probs * probs, axis=0, keepdims=True)
            grad_scores = (probs * (grad_probs - inner)).astype(BF16)
            grad_keys += mm(grad_scores, queries * lane_scaled[half])
            grad_queries.append(
                mm(keys_t[half * HEAD_DIM : (half + 1) * HEAD_DIM], grad_scores)
            )
        grad_query = jnp.concatenate(grad_queries, axis=0).T
        for place, value in enumerate(
            (grad_query, grad_keys, grad_values)
        ):
            grads_pair[pair, image, :, place * LANES : (place + 1) * LANES] = value.astype(BF16)

    def rows_back(image):
        total = mm_nt(grads_pair[0, image], w_pair[0])
        for pair in range(1, pairs):
            total += mm_nt(grads_pair[pair, image], w_pair[pair])
        return total

    def weights_back(pair):
        both = grads_pair[pair].reshape(2 * seq, 3 * LANES)
        for base in range(0, width, 256):
            rows = slice(base, base + 256)
            ar[1 + pair, rows, :] = mm(s.n1_t[rows, :], both).astype(BF16)

    mixed_back(0)
    attend_back(0, 0)
    branch_back.wait_recv()
    mixed_back(1)

    ar = s.ar
    by_core = (one_dev, two_dev, p_one, p_two)
    cuts = [(array, lanes) for array in range(4) for lanes in (pl.ds(0, 256), pl.ds(256, local - 256))]
    flat = [
        (ar.at[array, :, lanes], s.ar_one.at[array, :, lanes], s.ar_two.at[array, :, lanes],
         s.ar_z.at[array, :, :, lanes], s.ar_rest.at[array, :, :, lanes], s.attn.at[array, :, lanes],
         width, by_core)
        for array, lanes in cuts
    ]
    small_half = seq // 2
    small = (s.small, s.small_one, s.small_two, s.small_z, s.small_rest,
             s.small_all, small_half, by_core)
    items = flat + [small]
    stages = [dict() for _ in range(7)]

    def piece(item):
        total_rows = items[item][6]
        _, _, p_one, p_two = items[item][7]
        half, quarter, leaf = total_rows // 2, total_rows // 4, total_rows // 16
        at_one = pl.multiple_of(p_one * half, half)
        at_two = pl.multiple_of(at_one + p_two * quarter, quarter)
        return half, quarter, leaf, at_one, at_two

    def reduce_one(item):
        data, one = items[item][0], items[item][1]
        half, _, _, _, _ = piece(item)
        device, _, p_one, _ = items[item][7]
        other = pl.ds(pl.multiple_of((1 - p_one) * half, half), half)
        stages[0][item] = [links.send(data.at[other], one, device)]

    def reduce_two(item):
        data, one, two = items[item][:3]
        half, quarter, _, at_one, _ = piece(item)
        stages[0][item][0].wait_recv()
        mine = pl.ds(at_one, half)
        data[mine] = (data[mine].astype(F32) + one[...].astype(F32)).astype(data.dtype)
        _, device, _, p_two = items[item][7]
        other = pl.ds(pl.multiple_of(at_one + (1 - p_two) * quarter, quarter), quarter)
        stages[1][item] = [links.send(data.at[other], two, device)]

    def reduce_z(item):
        data, _, two, by_z = items[item][:4]
        _, quarter, leaf, _, at_two = piece(item)
        stages[1][item][0].wait_recv()
        mine = pl.ds(at_two, quarter)
        data[mine] = (data[mine].astype(F32) + two[...].astype(F32)).astype(data.dtype)
        stages[2][item] = [
            links.send(
                data.at[pl.ds(pl.multiple_of(at_two + ((zq + hop) % 4) * leaf, leaf), leaf)],
                by_z.at[hop - 1],
                zdev[hop],
            )
            for hop in range(1, 4)
        ]

    def spread_z(item):
        data, _, _, by_z, by_rest, done = items[item][:6]
        _, _, leaf, _, at_two = piece(item)
        for copy in stages[2][item]:
            copy.wait_recv()
        mine = pl.ds(pl.multiple_of(at_two + zq * leaf, leaf), leaf)
        total = data[mine].astype(F32)
        for hop in range(3):
            total += by_z[hop].astype(F32)
        if rest_count > 1:
            by_rest[0] = total.astype(data.dtype)
            copies = [
                links.send(by_rest.at[0], by_rest.at[hop], rdev[hop])
                for hop in range(1, rest_count)
            ]
            for copy in copies:
                copy.wait_recv()
            total = jnp.zeros(total.shape, F32)
            for owner in range(rest_count):
                total += by_rest[(rest - owner + rest_count) % rest_count].astype(F32)
        done[mine] = total.astype(done.dtype)
        stages[3][item] = [
            links.send(done.at[mine], done.at[mine], zdev[hop]) for hop in range(1, 4)
        ]

    def spread_two(item):
        done = items[item][5]
        _, quarter, _, _, at_two = piece(item)
        for copy in stages[3][item]:
            copy.wait_recv()
        mine = pl.ds(at_two, quarter)
        stages[4][item] = [links.send(done.at[mine], done.at[mine], items[item][7][1])]

    def spread_one(item):
        done = items[item][5]
        half, _, _, at_one, _ = piece(item)
        stages[4][item][0].wait_recv()
        mine = pl.ds(at_one, half)
        stages[5][item] = [links.send(done.at[mine], done.at[mine], items[item][7][0])]

    def finish(item):
        stages[5][item][0].wait_recv()
        if item < len(cuts):
            array, lanes = cuts[item]
            stores.append(loads.start(s.attn.at[array, :, lanes], out_attn.at[array, :, lanes]))

    for half in range(2):
        at = slice(half * local, (half + 1) * local)
        total = mm(s.mixed_t[0], grad_branch[0, :, at]) + mm(
            s.mixed_t[1], grad_branch[1, :, at]
        )
        ar[0, at, :] = total.astype(BF16)
    def out_back():
        part_sib[1, 1].wait_recv()
        cross[1].wait_recv()

        @pl.loop(0, blocks, unroll=4)
        def _(step):
            at = pl.ds(pl.multiple_of(step * block, block), block)
            row_ids = lax.broadcasted_iota(jnp.int32, (block, 1), 0) + step * block
            total = result[0, at, :] + part_in[1, 1, at, :].astype(F32) + cross_in[1, at, :].astype(F32)
            rows = middle[at, :] + (total + vecs[5:6, :])
            s.own_rows[0, at, :] = jnp.where(row_ids < limit, rows, 0.0).astype(BF16)

        stores.append(loads.start(s.own_rows, out_rows))

    def pair_back(pair):
        if pair == 0:
            sum_b_until(3)
        attend_back(1, pair)
        if pair > 0:
            attend_back(0, pair)
        weights_back(pair)
        if pair == 1:
            sum_a_until(3)

    held = SimpleNamespace()

    def rows_hand():
        s.rows_out[...] = rows_back(1).astype(BF16)
        held.rows_sib = links.send(s.rows_out, s.rows_in, sib)

    def rows_keep():
        s.branch_own[...] = rows_back(0)

    def norm_one_back():
        held.rows_sib.wait_recv()

        def in_back(step, totals):
            at = pl.ds(pl.multiple_of(step * block, block), block)
            grads = (s.branch_own[at, :] + s.rows_in[at, :].astype(F32))
            unit_rows, scale = s.unit_one[at, :], s.scale_one[at, :]
            grad_mid[at, :] += norm_back(grads, vecs[0:1, :], unit_rows, scale)
            return (totals[0] + fold_rows(grads * unit_rows), totals[1] + fold_rows(grads))

        held.sums = lax.fori_loop(0, blocks, in_back, (empty,) * 2, unroll=4)
        sum_a_until(ring)

    theirs = pl.ds(pl.multiple_of((1 - h) * small_half, small_half), small_half)
    ours = pl.ds(pl.multiple_of(h * small_half, small_half), small_half)
    small_ref, small_own = s.small_full, s.small
    small_base = (width // small_ref.shape[1]) * prompt_pad + 6 * (width // small_ref.shape[1])

    def place_small():
        gain_one_sum, shift_one_sum = held.sums
        grad_in = grad_mid[...]
        high = grad_in.astype(BF16)
        low = (grad_in - high.astype(F32)).astype(BF16)
        placed = mm(pick[...], high) + mm(pick[...], low)
        s.own_tok[0] = placed[0:tok_rows]
        stores.append(loads.start(s.own_tok.at[0], out_tok.at[:, 0, :]))

        small_ref[...] = jnp.zeros(small_ref.shape, F32)
        part_width = small_ref.shape[1]
        parts = width // part_width
        for part in range(parts):
            small_ref[part * prompt_pad : part * prompt_pad + prompt_pad, :] = placed[
                tok_pad : tok_pad + prompt_pad, part * part_width : (part + 1) * part_width
            ]
        base = parts * prompt_pad
        sums = (gain_one_sum, shift_one_sum, out_bias_sum, gain_two_sum, shift_two_sum, fc2_bias_sum)
        for place, total in enumerate(sums):
            row = jnp.sum(total, axis=0, keepdims=True)
            for part in range(parts):
                at = base + place * parts + part
                small_ref[at : at + 1, :] = row[:, part * part_width : (part + 1) * part_width]
        base += len(sums) * parts
        for place in range(2):
            at = slice(2 * place * LANES, 2 * place * LANES + LANES)
            row = jnp.concatenate(
                [
                    jnp.sum(
                        grads_pair[pair, 0, :, at].astype(F32) + grads_pair[pair, 1, :, at].astype(F32),
                        axis=0,
                        keepdims=True,
                    )
                    for pair in range(pairs)
                ],
                axis=1,
            )
            for head in range(2):
                chosen = row * (h if head == 1 else 1 - h).astype(F32)
                at = base + head * 4 + place * 2
                small_ref[at : at + 1, :] = chosen[:, 0:part_width]
                small_ref[at + 1 : at + 2, 0 : local - part_width] = chosen[:, part_width:local]
        held.small_sib = links.send(small_ref.at[theirs], s.small_in.at[1], sib)
        sum_b_until(ring)

    def reduce_small():
        held.small_sib.wait_recv()
        small_own[...] = small_ref[ours] + s.small_in[1]

    blocks_beside = [
        functools.partial(pair_back, 0), functools.partial(pair_back, 1), functools.partial(pair_back, 2),
        rows_hand, rows_keep, norm_one_back, place_small, out_back,
    ]
    steps = [reduce_one, reduce_two, reduce_z, spread_z, spread_two, spread_one, finish]
    for item, stage in REDUCE_ORDER:
        if item < 0:
            blocks_beside[-1 - item]()
        else:
            if stage == 0 and item == len(cuts):
                reduce_small()
            steps[stage](item)
            if (item, stage) == LATE_SUM:
                sum_b_end()
    final = s.small_out
    final[ours] = s.small_all[...]
    small_back = links.send(s.small_all, s.small_in.at[0], sib)
    small_back.wait_recv()
    final[theirs] = s.small_in[0]
    final[small_base + 8 : small_base + 12, :] = jnp.where(
        h == 0, final[small_base : small_base + 4, :], final[small_base + 4 : small_base + 8, :]
    )
    stores.append(loads.start(final, out_small))
    links.drain()
    for copy in stores:
        copy.wait()


def finish_kernel(dims, *refs):
    it = iter(refs)
    rows_in, tok_in, attn_in, small_in, fc1_in, fc2_in, bias_in = (next(it) for _ in range(7))
    (
        layer_out, grad_tokens, grad_prompts, gain_one, shift_one, w_query, b_query, w_key,
        w_value, b_value, w_out, b_out, gain_two, shift_two, w_fc1, b_fc1, w_fc2, b_fc2,
    ) = (next(it) for _ in range(18))
    s = SimpleNamespace(**dict(zip(dims.finish, it)))
    width, local = dims.width, dims.local
    rows = w_fc1.shape[0]
    loads = Loads(s.load_sems)
    load_small = loads.start(small_in, s.small)
    load_bias = loads.start(bias_in, s.bias)
    load_attn = [loads.start(attn_in.at[array], s.attn.at[array]) for array in (1, 2, 3, 0)]
    passing = [(rows_in, s.rows, layer_out), (tok_in, s.tok, grad_tokens)]
    whole_shards = rows == fc1_in.shape[0]
    if whole_shards:
        passing += [(fc1_in, s.fc1, w_fc1), (fc2_in, s.fc2, w_fc2)]
    passing = [(loads.start(source, held), held, target) for source, held, target in passing]
    stores = []
    load_small.wait()
    load_bias.wait()
    part_width = s.small.shape[1]
    parts = width // part_width
    for part in range(parts):
        at = slice(part * part_width, (part + 1) * part_width)
        s.prompts[:, at] = s.small[part * dims.prompt_pad : part * dims.prompt_pad + dims.prompt_rows]
    stores.append(loads.start(s.prompts, grad_prompts))
    base = parts * dims.prompt_pad
    for place, target in enumerate((gain_one, shift_one, b_out, gain_two, shift_two, b_fc2)):
        for part in range(parts):
            at = base + place * parts + part
            s.row[place : place + 1, part * part_width : (part + 1) * part_width] = s.small[at : at + 1]
        s.flat[place, :] = s.row[place : place + 1, :].reshape(width)
        stores.append(loads.start(s.flat.at[place], target))
    base += 6 * parts + 8
    for place, target in enumerate((b_query, b_value)):
        at = base + 2 * place
        s.row[6:7, 0:part_width] = s.small[at : at + 1]
        s.row[6:7, part_width : 2 * part_width] = s.small[at + 1 : at + 2]
        s.half_flat[place, :] = s.row[6:7, 0:local].reshape(local)
        stores.append(loads.start(s.half_flat.at[place], target))
    b_fc1[...] = s.bias[0:1, 0:rows].reshape(rows)
    for pair in range(3):
        load_attn[pair].wait()
        at = slice(pair * LANES, (pair + 1) * LANES)
        for place, target in enumerate((w_query, w_key, w_value)):
            s.tall[place, :, at] = s.attn[1 + pair, :, place * LANES : (place + 1) * LANES].astype(F32)
            stores.append(loads.start(s.tall.at[place, :, pl.ds(pair * LANES, LANES)], target.at[:, pl.ds(pair * LANES, LANES)]))
    load_attn[3].wait()
    s.wide[:, 0:local] = s.attn[0, 0:local].astype(F32)
    s.wide[:, local : 2 * local] = s.attn[0, local : 2 * local].astype(F32)
    stores.append(loads.start(s.wide, w_out))
    for load, held, target in passing:
        load.wait()
        stores.append(loads.start(held, target))
    if not whole_shards:
        for source, held, target in ((fc1_in, s.fc1, w_fc1), (fc2_in, s.fc2, w_fc2)):
            loads.start(source, held).wait()
            s.cut[...] = held[0:rows]
            loads.start(s.cut, target).wait()
    for copy in stores:
        copy.wait()


def layer(dims, operands):
    seq, width, local = dims.seq, dims.width, dims.local
    n, ring, slots, rows_per = dims.n, dims.ring, dims.slots, dims.rows_per
    pairs = local // LANES
    chunk = dims.chunk_slots * rows_per
    rest_count = n // 16
    small_half = seq // 2
    part_width = 256
    copies = 11 * ring + 64 + 10 * 4 + 9 * (rest_count - 1)
    vmem = pltpu.VMEM
    shared = 2 * rows_per
    scratch = dict(
        send_sems=pltpu.SemaphoreType.DMA((copies,)),
        recv_sems=pltpu.SemaphoreType.DMA((copies,)),
        w_all=vmem((slots, shared, width), BF16),
        b_all=vmem((slots, 8, LANES), F32),
        cot_all=vmem((4, seq, width), BF16),
        meta=vmem((2, 8, LANES), jnp.int32),
        load_sems=pltpu.SemaphoreType.DMA((39,)),
        kept=vmem((1, dims.patches), jnp.int32),
        tokens=vmem((1, dims.tok_rows, width), BF16),
        prompts=vmem((dims.prompt_rows, width), BF16),
        gain_one=vmem((width,), BF16),
        shift_one=vmem((width,), BF16),
        b_query=vmem((local,), BF16),
        b_value=vmem((local,), BF16),
        b_out=vmem((width,), BF16),
        gain_two=vmem((width,), BF16),
        shift_two=vmem((width,), BF16),
        b_fc1=vmem((dims.rows,), BF16),
        b_fc2=vmem((width,), BF16),
        vecs=vmem((8, width), F32),
        w_pair=vmem((pairs, width, 3 * LANES), BF16),
        wout=vmem((local, width), BF16),
        unit_one=vmem((seq, width), F32),
        unit_two=vmem((seq, width), F32),
        scale_one=vmem((seq, 1), F32),
        scale_two=vmem((seq, 1), F32),
        own_rows=vmem((1, seq, width), BF16),
        own_tok=vmem((1, dims.tok_rows, width), F32),
        own_fc1=vmem((rows_per, width), F32),
        own_fc2=vmem((rows_per, width), F32),
        own_bias=vmem((8, LANES), F32),
        attn=vmem((4, width, local), BF16),
        src=vmem((dims.tok_pad + dims.prompt_pad, width), BF16),
        pick=vmem((dims.tok_pad + dims.prompt_pad, seq), BF16),
        idx=vmem((8, seq), jnp.int32),
        stream=vmem((seq, width), F32),
        middle=vmem((seq, width), F32),
        n1=vmem((2, seq, width), BF16),
        n2=vmem((4, seq, width), BF16),
        q=vmem((2, pairs, seq, LANES), BF16),
        k=vmem((2, pairs, seq, LANES), BF16),
        v=vmem((2, pairs, seq, LANES), BF16),
        probs=vmem((4 * pairs, seq, seq), F32),
        mixed_t=vmem((2, local, seq), BF16),
        branch_out=vmem((seq, width), F32),
        branch_in=vmem((seq, width), F32),
        branch_own=vmem((seq, width), F32),
        hidden=vmem((slots // dims.chunk_slots, 4, seq, chunk), BF16),
        grad_before=vmem((4, seq, chunk), BF16),
        result=vmem((4, seq, width), F32),
        grad_two=vmem((4, seq, width), F32),
        part_out=vmem((2, 2, seq, width), BF16),
        part_in=vmem((2, 2, seq, width), BF16),
        cross_out=vmem((2, seq, width), BF16),
        cross_in=vmem((2, seq, width), BF16),
        g_all=vmem((slots, shared, width), BF16),
        gb_all=vmem((slots, 8, LANES), F32),
        ry=vmem((ring, rows_per, width), BF16),
        ry_last=vmem((rows_per, width), BF16),
        rb_out=vmem((ring, 2, rows_per, width), BF16),
        rb_in=vmem((ring, 2, rows_per, width), BF16),
        n1_t=vmem((width, 2 * seq), BF16),
        ryb=vmem((ring, 8, LANES), F32),
        rz_out=vmem((ring, rows_per, width), BF16),
        rzb_out=vmem((ring, 8, LANES), F32),
        rz_in=vmem((ring, rows_per, width), BF16),
        rzb_in=vmem((ring, 8, LANES), F32),
        grad_branch=vmem((2, seq, width), BF16),
        grad_mixed=vmem((2, pairs, seq, LANES), BF16),
        grads_pair=vmem((pairs, 2, seq, 3 * LANES), BF16),
        rows_out=vmem((seq, width), BF16),
        rows_in=vmem((seq, width), BF16),
        ar=vmem((4, width, local), BF16),
        ar_one=vmem((4, width // 2, local), BF16),
        ar_two=vmem((4, width // 4, local), BF16),
        ar_z=vmem((4, 3, width // 16, local), BF16),
        ar_rest=vmem((4, rest_count, width // 16, local), BF16),
        small_full=vmem((seq, part_width), F32),
        small_out=vmem((seq, part_width), F32),
        small_in=vmem((2, small_half, part_width), F32),
        small=vmem((small_half, part_width), F32),
        small_one=vmem((small_half // 2, part_width), F32),
        small_two=vmem((small_half // 4, part_width), F32),
        small_z=vmem((3, small_half // 16, part_width), F32),
        small_rest=vmem((rest_count, small_half // 16, part_width), F32),
        small_all=vmem((small_half, part_width), F32),
    )
    dims = SimpleNamespace(**vars(dims), scratch=tuple(scratch))
    anywhere = pl.BlockSpec(memory_space=pl.ANY)
    shape = jax.ShapeDtypeStruct
    return pl.pallas_call(
        functools.partial(layer_kernel, dims),
        out_shape=(
            shape((1, seq, width), BF16),
            shape((dims.tok_rows, 1, width), F32),
            shape((4, width, local), BF16),
            shape((seq, part_width), F32),
            shape((rows_per, width), F32),
            shape((rows_per, width), F32),
            shape((8, LANES), F32),
        ),
        in_specs=[pl.BlockSpec(memory_space=pltpu.SMEM)] + [anywhere] * (len(operands) - 1),
        out_specs=[anywhere] * 7,
        scratch_shapes=list(scratch.values()),
        compiler_params=pltpu.CompilerParams(
            collective_id=0, has_side_effects=True, vmem_limit_bytes=63 * 2**20
        ),
    )(*operands)


def finish(dims, results):
    seq, width, local, rows = dims.seq, dims.width, dims.local, dims.rows
    vmem = pltpu.VMEM
    scratch = dict(
        load_sems=pltpu.SemaphoreType.DMA((36,)),
        attn=vmem((4, width, local), BF16),
        wide=vmem((local, width), F32),
        tall=vmem((3, width, local), F32),
        small=vmem(results[3].shape, F32),
        bias=vmem((8, LANES), F32),
        prompts=vmem((dims.prompt_rows, width), F32),
        row=vmem((8, width), F32),
        flat=vmem((6, width), F32),
        half_flat=vmem((2, local), F32),
        rows=vmem((1, seq, width), BF16),
        tok=vmem((dims.tok_rows, 1, width), F32),
        fc1=vmem((dims.rows_per, width), F32),
        fc2=vmem((dims.rows_per, width), F32),
        cut=vmem((rows, width), F32),
    )
    dims = SimpleNamespace(**vars(dims), finish=tuple(scratch))
    anywhere = pl.BlockSpec(memory_space=pl.ANY)
    whole = pl.BlockSpec(memory_space=pltpu.VMEM)

    def out(*sizes, dtype=F32):
        return jax.ShapeDtypeStruct(sizes, dtype)

    shapes = (
        out(1, seq, width, dtype=BF16), out(dims.tok_rows, 1, width), out(dims.prompt_rows, width),
        out(width), out(width), out(width, local), out(local), out(width, local),
        out(width, local), out(local), out(local, width), out(width), out(width), out(width),
        out(rows, width), out(rows), out(rows, width), out(width),
    )
    return pl.pallas_call(
        functools.partial(finish_kernel, dims),
        out_shape=shapes,
        in_specs=[anywhere] * 7,
        out_specs=[whole if place == 15 else anywhere for place in range(len(shapes))],
        scratch_shapes=list(scratch.values()),
        compiler_params=pltpu.CompilerParams(vmem_limit_bytes=60 * 2**20),
    )(*results)


def body(n, *arguments):
    (
        tokens, kept_index, kept_count, prompts, gain_one, shift_one, w_query, b_query, w_key,
        w_value, b_value, w_out, b_out, gain_two, shift_two, w_fc1, b_fc1, w_fc2, b_fc2, cotangent,
    ) = arguments
    seq, width = cotangent.shape[1:]
    local = w_query.shape[1]
    rows = w_fc1.shape[0]
    rows_per = round_up(rows, 16)
    ring = n // 4
    slots = 2 * ring
    halves = slots // 2
    chunk_slots = halves if (halves % 2 == 0 and halves * rows_per % LANES == 0) else slots
    tok_rows, prompt_rows = tokens.shape[1], prompts.shape[0]
    dims = SimpleNamespace(
        n=n, ring=ring, slots=slots, chunk_slots=chunk_slots, rows_per=rows_per, rows=rows, seq=seq,
        width=width, local=local, tok_rows=tok_rows, tok_pad=round_up(tok_rows, 16),
        prompt_rows=prompt_rows, prompt_pad=round_up(prompt_rows, 16),
        patches=kept_index.shape[1],
    )
    if rows_per != rows:
        spare = ((0, rows_per - rows), (0, 0))
        w_fc1, w_fc2 = jnp.pad(w_fc1, spare), jnp.pad(w_fc2, spare)
    operands = (
        kept_count, tokens, kept_index, prompts, w_fc1, w_fc2, cotangent, w_query, w_key, w_value,
        w_out, gain_one, shift_one, b_query, b_value, b_out, gain_two, shift_two, b_fc1, b_fc2,
    )
    outs = list(finish(dims, layer(dims, operands)))
    outs[1] = outs[1].transpose(1, 0, 2)
    return tuple(outs)


def solution(mesh):
    batch, head = mesh.axis_names
    both = (batch, head)
    placed = (
        P(both, None, None), P(both, None), P(both), P(), P(), P(), P(None, head), P(head),
        P(None, head), P(None, head), P(head), P(head, None), P(), P(), P(),
        P(both, None), P(both), P(both, None), P(), P(both, None, None),
    )
    return jax.shard_map(
        functools.partial(body, mesh.shape[batch]),
        mesh=mesh,
        in_specs=placed,
        out_specs=(
            P(both, None, None), P(both, None, None), P(), P(), P(), P(None, head), P(head),
            P(None, head), P(None, head), P(head), P(head, None), P(), P(), P(),
            P(both, None), P(both), P(both, None), P(),
        ),
        check_vma=False,
    )
```

```python
import functools
from types import SimpleNamespace

import jax
import jax.numpy as jnp
from jax import lax
from jax.experimental import pallas as pl
from jax.experimental.pallas import tpu as pltpu
from jax.sharding import PartitionSpec as P

MESH = pl.DeviceIdType.MESH
HEAD_DIM = 64
EPSILON = 1e-06
LANES = 128
BF16 = jnp.bfloat16
F32 = jnp.float32


def round_up(value, step):
    return -(-value // step) * step


def mm(left, right):
    return lax.dot_general(left, right, (((1,), (0,)), ((), ())), preferred_element_type=F32)


def mm_nt(left, right):
    return lax.dot_general(left, right, (((1,), (1,)), ((), ())), preferred_element_type=F32)


def mm_tn(left, right):
    return lax.dot_general(left, right, (((0,), (0,)), ((), ())), preferred_element_type=F32)


def fold_rows(rows):
    count, width = rows.shape
    return jnp.sum(rows.reshape(count // 8, 8, width), axis=0)


def normalise(rows):
    width = rows.shape[1]
    centre = jnp.sum(rows, axis=1, keepdims=True) * (1.0 / width)
    centred = rows - centre
    spread = jnp.sum(centred * centred, axis=1, keepdims=True) * (1.0 / width)
    scale = lax.rsqrt(spread + EPSILON)
    return centred * scale, scale


def norm_back(grad_rows, gain_row, unit_rows, scale):
    width = grad_rows.shape[1]
    scaled = grad_rows * gain_row
    mean_one = jnp.sum(scaled, axis=1, keepdims=True) * (1.0 / width)
    mean_two = jnp.sum(scaled * unit_rows, axis=1, keepdims=True) * (1.0 / width)
    return scale * (scaled - mean_one - unit_rows * mean_two)


GELU_A = 0.7978845608028654
GELU_B = 0.044715


def gelu_both(value):
    square = value * value
    bend = jnp.tanh(value * (GELU_A + (GELU_A * GELU_B) * square))
    half = 0.5 + 0.5 * bend
    slope = half + (0.5 * value) * (1.0 - bend * bend) * (
        GELU_A + (3.0 * GELU_A * GELU_B) * square
    )
    return value * half, slope


VECTORS = (
    "gain_one", "shift_one", "b_query", "b_value", "b_out", "gain_two", "shift_two", "b_fc1", "b_fc2",
)


LATE_SUM = (8, 1)
REDUCE_ORDER = (
    (0, 0), (-1, 0), (3, 0), (-2, 0), (5, 0), (1, 0), (-3, 0), (4, 0), (7, 0), (3, 1), (0, 1),
    (5, 1), (2, 0), (1, 1), (3, 2), (0, 2), (4, 1), (5, 2), (1, 2), (3, 3), (-4, 0), (7, 1),
    (6, 0), (0, 3), (1, 3), (7, 2), (4, 2), (2, 1), (3, 4), (-5, 0), (1, 4), (5, 3), (0, 4),
    (6, 1), (-6, 0), (7, 3), (2, 2), (-7, 0), (4, 3), (8, 0), (3, 5), (1, 5), (5, 4), (7, 4),
    (6, 2), (-8, 0), (8, 1), (2, 3), (0, 5), (6, 3), (5, 5), (4, 4), (8, 2), (2, 4), (7, 5),
    (6, 4), (3, 6), (4, 5), (8, 3), (2, 5), (7, 6), (8, 4), (5, 6), (6, 5), (0, 6), (4, 6), (8, 5),
    (6, 6), (1, 6), (2, 6), (8, 6),
)


class Once:
    def __init__(self, wait):
        self.pending = wait

    def wait(self):
        if self.pending is not None:
            self.pending()
            self.pending = None


class Loads:
    def __init__(self, sems, depth):
        self.sems = sems
        self.depth = depth
        self.copies = []

    def take(self):
        place = len(self.copies)
        if place >= self.depth:
            self.copies[place - self.depth].wait()
        return self.sems.at[place % self.depth]

    def start(self, source, target):
        copy = pltpu.make_async_copy(source, target, self.take())
        copy.start()
        self.copies.append(Once(copy.wait))
        return self.copies[-1]

    def start_parts(self, pieces, whole):
        sem = self.take()
        for source, target in pieces:
            pltpu.make_async_copy(source, target, sem).start()
        self.copies.append(Once(pltpu.make_async_copy(whole, whole, sem).wait))
        return self.copies[-1]


class Links:
    def __init__(self, send_sems, recv_sems, depth):
        self.send_sems = send_sems
        self.recv_sems = recv_sems
        self.depth = depth
        self.sends = []
        self.arrivals = 0

    def copy(self, source, target, device, arrival):
        place = len(self.sends)
        if place >= self.depth:
            self.sends[place - self.depth].wait()
        copy = pltpu.make_async_remote_copy(
            src_ref=source,
            dst_ref=target,
            send_sem=self.send_sems.at[place % self.depth],
            recv_sem=self.recv_sems.at[arrival],
            device_id=device,
            device_id_type=MESH,
        )
        copy.start()
        self.sends.append(Once(copy.wait_send))
        return copy

    def send(self, source, target, device):
        copy = self.copy(source, target, device, self.arrivals)
        self.arrivals += 1
        return copy

    def send_parts(self, pieces, whole):
        arrival = self.arrivals
        self.arrivals += 1
        for source, target, device in pieces:
            self.copy(source, target, device, arrival)
        return pltpu.make_async_remote_copy(
            src_ref=whole,
            dst_ref=whole,
            send_sem=self.send_sems.at[0],
            recv_sem=self.recv_sems.at[arrival],
            device_id=device,
            device_id_type=MESH,
        )

    def drain(self):
        for copy in self.sends:
            copy.wait()


def layer_kernel(dims, *refs):
    it = iter(refs)
    count_ref = next(it)
    tokens, kept, prompts, fc1, fc2, cot = (next(it) for _ in range(6))
    weights_in = [next(it) for _ in range(4)]
    vectors_in = [next(it) for _ in range(9)]
    out_rows, out_tok, out_attn, out_small, out_fc1, out_fc2, out_bias = (
        next(it) for _ in range(7)
    )
    s = SimpleNamespace(**dict(zip(dims.scratch, it)))
    w_pair, wout = s.w_pair, s.wout
    vecs = s.vecs
    seq, width, local = dims.seq, dims.width, dims.local
    pairs = local // LANES
    rows_per = dims.rows_per
    n, ring, slots = dims.n, dims.ring, dims.slots
    chunk_slots = dims.chunk_slots
    chunk = chunk_slots * rows_per
    chunks = slots // chunk_slots
    tok_rows, tok_pad, prompt_pad = dims.tok_rows, dims.tok_pad, dims.prompt_pad
    prompt_rows, patches = dims.prompt_rows, dims.patches
    rest_count = n // 16
    score_scale = HEAD_DIM**-0.5
    block = 32
    blocks = seq // block

    b = lax.axis_index("batch")
    h = lax.axis_index("head")
    bx = b % 2
    by = (b // 2) % 2
    zz = b // 4
    sib = (b, 1 - h)
    xdev = (b + 1 - 2 * bx, h)
    ydev = (b + 2 - 4 * by, h)
    corner = b % 4
    ring_next = (((zz + 1) % ring) * 4 + corner, h)
    ring_prev = (((zz + ring - 1) % ring) * 4 + corner, h)
    zq = zz % 4
    zdev = [((zz - zq + (zq + hop) % 4) * 4 + corner, h) for hop in range(4)]
    rest = b // 16
    rdev = [(((rest + hop) % rest_count) * 16 + b % 16, h) for hop in range(rest_count)]
    one_dev = (xdev[0] * (1 - h) + ydev[0] * h, h)
    two_dev = (ydev[0] * (1 - h) + xdev[0] * h, h)
    p_one = bx * (1 - h) + by * h
    p_two = by * (1 - h) + bx * h

    partners = [sib, xdev, ydev] + zdev[1:]
    if ring > 4:
        partners += [ring_next, ring_prev] + rdev[1:]
    barrier = pltpu.get_barrier_semaphore()
    for partner in partners:
        pl.semaphore_signal(barrier, inc=1, device_id=partner, device_id_type=MESH)

    links = Links(s.send_sems, s.recv_sems, dims.send_depth)

    w_all, b_all, cot_all = s.w_all, s.b_all, s.cot_all
    loads = Loads(s.load_sems, dims.load_depth)
    load_kept = loads.start(kept, s.kept)
    load_fc = [
        loads.start(fc1, w_all.at[0, pl.ds(0, rows_per)]),
        loads.start(fc2, w_all.at[0, pl.ds(rows_per, rows_per)]),
    ]
    load_cot = loads.start(cot.at[0], cot_all.at[0])
    load_rows = [loads.start(tokens, s.tokens), loads.start(prompts, s.prompts)]
    load_vectors = [loads.start(ref, getattr(s, name)) for ref, name in zip(vectors_in, VECTORS)]
    load_weights = [
        loads.start(weights_in[3], wout),
        loads.start_parts(
            [
                (
                    weights_in[place].at[:, pl.ds(pair * LANES, LANES)],
                    w_pair.at[pair, :, pl.ds(place * LANES, LANES)],
                )
                for pair in range(pairs)
                for place in range(3)
            ],
            w_pair,
        ),
    ]

    limit = count_ref[0] + (1 + prompt_rows)
    src, pick = s.src, s.pick
    s.meta[0] = jnp.broadcast_to(limit, (8, LANES))
    s.idx[...] = jnp.zeros((8, seq), jnp.int32)
    src[tok_rows - tok_rows % 16 : tok_pad] = jnp.zeros((tok_pad - tok_rows + tok_rows % 16, width), BF16)
    src[tok_pad:] = jnp.zeros((prompt_pad, width), BF16)
    vecs[...] = jnp.zeros(vecs.shape, F32)
    load_kept.wait()
    s.idx[0:1, 0:patches] = s.kept[...]
    shifted = pltpu.roll(s.idx[...], 1 + prompt_rows, axis=1)[0:1, :]
    spot = lax.broadcasted_iota(jnp.int32, (1, seq), 1)
    wanted = jnp.where(
        spot < 1 + prompt_rows,
        jnp.where(spot == 0, 0, tok_pad - 1 + spot),
        jnp.where(spot < limit, shifted + 1, -1),
    )
    pick[...] = jnp.where(
        lax.broadcasted_iota(jnp.int32, pick.shape, 0) == wanted, 1.0, 0.0
    ).astype(BF16)
    for copy in load_vectors:
        copy.wait()
    for place, name in enumerate(("gain_one", "shift_one", "b_out", "gain_two", "shift_two", "b_fc2")):
        vecs[place : place + 1, :] = getattr(s, name)[...].astype(F32).reshape(1, width)
    vecs[6:7, 0:local] = s.b_query[...].astype(F32).reshape(1, local)
    vecs[6:7, local : 2 * local] = s.b_value[...].astype(F32).reshape(1, local)
    bias_rows = s.b_fc1.shape[0]
    vecs[7:8, 0:bias_rows] = s.b_fc1[...].astype(F32).reshape(1, bias_rows)
    b_all[0] = jnp.broadcast_to(vecs[7:8, 0:LANES], (8, LANES))
    load_cot.wait()

    @pl.loop(0, blocks, unroll=4)
    def _(step):
        at = pl.ds(pl.multiple_of(step * block, block), block)
        row_ids = lax.broadcasted_iota(jnp.int32, (block, 1), 0) + step * block
        rows = cot_all[0, at, :].astype(F32)
        cot_all[0, at, :] = jnp.where(row_ids < limit, rows, 0.0).astype(BF16)

    for copy in load_rows:
        copy.wait()
    src[0:tok_rows, :] = s.tokens[0]
    src[tok_pad : tok_pad + prompt_rows, :] = s.prompts[...]
    stream = s.stream
    stream[...] = mm_tn(pick[...], src[...])

    n1 = s.n1

    @pl.loop(0, blocks, unroll=4)
    def _(step):
        at = pl.ds(pl.multiple_of(step * block, block), block)
        unit_rows, s.scale_one[at, :] = normalise(stream[at, :])
        s.unit_one[at, :] = unit_rows
        n1[0, at, :] = (unit_rows * vecs[0:1, :] + vecs[1:2, :]).astype(BF16)

    for copy in load_fc:
        copy.wait()
    pl.semaphore_wait(barrier, len(partners))

    gather_ring, gather_y = {}, {}

    def gather_step(distance, kind):
        if distance > 0:
            for copy in gather_ring[distance, kind]:
                copy.wait_recv()
        rows = pl.ds(kind * rows_per, rows_per)
        mine = 2 * distance

        def hand_on(slot, device):
            copies = [links.send(w_all.at[mine, rows], w_all.at[slot, rows], device)]
            if kind == 0:
                copies.append(links.send(b_all.at[mine], b_all.at[slot], device))
            return copies

        if distance + 1 < ring:
            gather_ring[distance + 1, kind] = hand_on(mine + 2, ring_next)
        gather_y[distance, kind] = hand_on(mine + 1, ydev)

    gather_done = [0]

    def gather_until(distance, kind):
        while gather_done[0] <= min(2 * distance + kind, 2 * ring - 1):
            gather_step(gather_done[0] // 2, gather_done[0] % 2)
            gather_done[0] += 1

    n1_sib = links.send(n1.at[0], n1.at[1], sib)
    gather_until(0, 1)
    cot_x = links.send(cot_all.at[0], cot_all.at[2], xdev)
    cot_sib = links.send(cot_all.at[0], cot_all.at[1], sib)
    meta_sib = links.send(s.meta.at[0], s.meta.at[1], sib)


    def project(image):
        rows = n1[image]
        for pair in range(pairs):
            found = mm(rows, w_pair[pair])
            at = slice(pair * LANES, (pair + 1) * LANES)
            s.q[image, pair] = (found[:, 0:LANES] + vecs[6:7, at]).astype(BF16)
            s.k[image, pair] = found[:, LANES : 2 * LANES].astype(BF16)
            at = slice(local + pair * LANES, local + (pair + 1) * LANES)
            s.v[image, pair] = (found[:, 2 * LANES :] + vecs[6:7, at]).astype(BF16)

    lane_ids = lax.broadcasted_iota(jnp.int32, (1, LANES), 1)
    lane_half = [
        jnp.where(lane_ids // HEAD_DIM == half, 1.0, 0.0).astype(BF16) for half in range(2)
    ]
    lane_scaled = [
        jnp.where(lane_ids // HEAD_DIM == half, score_scale, 0.0).astype(BF16) for half in range(2)
    ]
    lane_spare = [
        jnp.where(lane_ids == (1 - half) * HEAD_DIM, 1.0, 0.0).astype(BF16) for half in range(2)
    ]
    key_ids = lax.broadcasted_iota(jnp.int32, (seq, 1), 0)

    def attend(image, first, last):
        key_bias = jnp.where(key_ids < s.meta[image, 0:1, 0:1], 0.0, -1e30).astype(BF16)

        for pair in range(first, last):
            queries, keys = s.q[image, pair], s.k[image, pair]
            values_t = s.v[image, pair].T
            for half in range(2):
                scores = mm_nt(
                    keys * lane_half[half] + key_bias * lane_spare[half],
                    queries * lane_scaled[half] + lane_spare[half],
                )
                weights = jnp.exp(scores - jnp.max(scores, axis=0, keepdims=True))
                probs = weights * (1.0 / jnp.sum(weights, axis=0, keepdims=True))
                s.probs[image * 2 * pairs + pair * 2 + half] = probs
                mixed_t = mm(values_t[half * HEAD_DIM : (half + 1) * HEAD_DIM], probs.astype(BF16))
                at = pl.ds(pair * LANES + half * HEAD_DIM, HEAD_DIM)
                s.mixed_t[image, at, :] = mixed_t.astype(BF16)

    for copy in load_weights:
        copy.wait()
    project(0)
    n1_sib.wait_recv()
    meta_sib.wait_recv()
    project(1)
    attend(1, 0, pairs)
    s.branch_out[...] = mm_tn(s.mixed_t[1], wout[...])
    branch_sib = links.send(s.branch_out, s.branch_in, sib)
    gather_until(1, 0)
    attend(0, 0, pairs)
    gather_until(1, 1)
    s.branch_own[...] = mm_tn(s.mixed_t[0], wout[...])
    branch_sib.wait_recv()
    middle, n2 = s.middle, s.n2

    @pl.loop(0, blocks, unroll=4)
    def _(step):
        at = pl.ds(pl.multiple_of(step * block, block), block)
        rows = stream[at, :] + (s.branch_own[at, :] + s.branch_in[at, :] + vecs[2:3, :])
        middle[at, :] = rows
        unit_rows, s.scale_two[at, :] = normalise(rows)
        s.unit_two[at, :] = unit_rows
        n2[0, at, :] = (unit_rows * vecs[3:4, :] + vecs[4:5, :]).astype(BF16)

    n2_x = links.send(n2.at[0], n2.at[2], xdev)
    n2_sib = links.send(n2.at[0], n2.at[1], sib)
    gather_until(2, 0)
    cot_x.wait_recv()
    cot_far = links.send(cot_all.at[2], cot_all.at[3], sib)
    hidden_all, before_all = s.hidden, s.grad_before
    result, grad_two = s.result, s.grad_two
    unpack = jnp.where(
        lax.broadcasted_iota(jnp.int32, (LANES, chunk), 1) % rows_per
        == lax.broadcasted_iota(jnp.int32, (LANES, chunk), 0),
        1.0,
        0.0,
    )
    owner_of = (
        lax.broadcasted_iota(jnp.int32, (chunk_slots, chunk), 1) // rows_per
        == lax.broadcasted_iota(jnp.int32, (chunk_slots, chunk), 0)
    )

    def feed_spans(part):
        span = slice(part * chunk_slots, (part + 1) * chunk_slots)
        return (
            w_all[span, 0:rows_per].reshape(chunk, width),
            w_all[span, rows_per : 2 * rows_per].reshape(chunk, width),
        )

    def feed(part, images, totals):
        span = slice(part * chunk_slots, (part + 1) * chunk_slots)
        tiles = b_all[span, 0, :].astype(BF16)
        bias_row = jnp.sum(
            jnp.where(owner_of, mm(tiles, unpack.astype(BF16)), 0.0), axis=0, keepdims=True
        )
        up, down = feed_spans(part)
        for image in images:
            before = mm_nt(n2[image], up) + bias_row
            hidden, slope = gelu_both(before)
            hidden_all[part, image] = hidden.astype(BF16)
            grad_before = (mm_nt(cot_all[image], down) * slope).astype(BF16)
            before_all[image] = grad_before
            if part == 0:
                grad_two[image] = mm(grad_before, up)
            else:
                grad_two[image] += mm(grad_before, up)
            totals += fold_rows(grad_before.astype(F32))
        return totals

    def feed_result(part):
        @pl.loop(0, 4)
        def _(image):
            _, down = feed_spans(part)
            if part == 0:
                result[image] = mm(hidden_all[part, image], down)
            else:
                result[image] += mm(hidden_all[part, image], down)

    g_all, gb_all = s.g_all, s.gb_all

    def feed_weights(part, bias_total):
        first = part * chunk_slots
        span = slice(first, first + chunk_slots)

        for left, right, base in ((before_all, n2, 0), (hidden_all.at[part], cot_all, rows_per)):
            total = jnp.zeros((chunk, width), F32)
            for image in range(4):
                total += mm_tn(left[image], right[image])
            g_all[span, base : base + rows_per] = (
                total.astype(BF16).reshape(chunk_slots, rows_per, width)
            )
        bias_row = jnp.sum(bias_total, axis=0, keepdims=True)
        spread = jnp.where(owner_of, jnp.broadcast_to(bias_row, owner_of.shape), 0.0)
        high = spread.astype(BF16)
        low = (spread - high.astype(F32)).astype(BF16)
        packed = mm_nt(high, unpack.astype(BF16)) + mm_nt(low, unpack.astype(BF16))
        for slot in range(chunk_slots):
            gb_all[first + slot] = jnp.broadcast_to(packed[slot : slot + 1], (8, LANES))

    order = list(range(1, ring)) + [0]
    stores = []
    sum_y, sum_ring, sum_both, sum_last = {}, {}, {}, []
    first_rows, second_rows = pl.ds(0, rows_per), pl.ds(rows_per, rows_per)

    def sum_send_y(distance):
        slot = 2 * distance + 1
        sum_y[distance] = [
            links.send(g_all.at[slot, first_rows], s.ry.at[distance], ydev),
            links.send(gb_all.at[slot], s.ryb.at[distance], ydev),
        ]

    def sum_a_step(distance):
        for copy in sum_y[distance]:
            copy.wait_recv()
        mine = 2 * distance
        total = g_all[mine, 0:rows_per].astype(F32) + s.ry[distance].astype(F32)
        bias = gb_all[mine] + s.ryb[distance]
        if distance != 1:
            before = (distance + ring - 1) % ring
            for copy in sum_ring[before]:
                copy.wait_recv()
            total += s.rz_in[before].astype(F32)
            bias += s.rzb_in[before]
        if distance == 0:
            s.own_fc1[...] = total
            s.own_bias[...] = bias
            stores.append(loads.start(s.own_fc1, out_fc1))
            stores.append(loads.start(s.own_bias, out_bias))
        else:
            s.rz_out[distance] = total.astype(BF16)
            s.rzb_out[distance] = bias
            sum_ring[distance] = [
                links.send(s.rz_out.at[distance], s.rz_in.at[distance], ring_next),
                links.send(s.rzb_out.at[distance], s.rzb_in.at[distance], ring_next),
            ]

    def sum_b_step(distance):
        if distance == 1:
            source = g_all.at[pl.ds(2, 2), second_rows]
            sum_both[1] = links.send(source, s.rb_in.at[1], ring_next)
            return
        before = (distance + ring - 1) % ring
        sum_both[before].wait_recv()
        for line in range(2):
            total = g_all[2 * distance + line, rows_per:].astype(F32) + s.rb_in[before, line].astype(F32)
            if distance == 0 and line == 0:
                s.own_fc2[...] = total
            else:
                s.rb_out[distance, line] = total.astype(BF16)
        if distance == 0:
            sum_last.append(links.send(s.rb_out.at[0, 1], s.ry_last, ydev))
        else:
            sum_both[distance] = links.send(s.rb_out.at[distance], s.rb_in.at[distance], ring_next)

    def sum_b_end():
        sum_last[0].wait_recv()
        s.own_fc2[...] += s.ry_last[...].astype(F32)
        stores.append(loads.start(s.own_fc2, out_fc2))

    sums_done = [0, 1]

    def sum_a_until(steps):
        while sums_done[0] < min(steps, ring):
            sum_a_step(order[sums_done[0]])
            sums_done[0] += 1

    def sum_b_until(steps):
        while sums_done[1] < min(steps, ring):
            sum_b_step(order[sums_done[1]])
            sums_done[1] += 1

    def gather_wait(part):
        per = chunk_slots // 2
        gather_until((part + 1) * per - 1, 1)
        for distance in range(part * per, (part + 1) * per):
            for kind in range(2):
                for copy in gather_y[distance, kind]:
                    copy.wait_recv()

    part_out, part_in = s.part_out, s.part_in
    cross_out, cross_in = s.cross_out, s.cross_in
    part_sib, cross = {}, {}

    def hand_part(kind, place):
        total = (grad_two, result)[kind]
        part_out[kind, place] = total[(3, 1)[place]].astype(BF16)
        part_sib[kind, place] = links.send(part_out.at[kind, place], part_in.at[kind, place], sib)

    def hand_cross(kind):
        total = (grad_two, result)[kind]
        part_sib[kind, 0].wait_recv()
        cross_out[kind] = (total[2] + part_in[kind, 0].astype(F32)).astype(BF16)
        cross[kind] = links.send(cross_out.at[kind], cross_in.at[kind], xdev)

    gather_until(2, 1)
    gather_wait(0)
    n2_sib.wait_recv()
    cot_sib.wait_recv()
    no_bias = jnp.zeros((8, chunk), F32)
    bias_total = feed(0, (0, 1), no_bias)
    gather_until(ring - 1, 0)
    n2_x.wait_recv()
    n2_far = links.send(n2.at[2], n2.at[3], sib)
    gather_until(ring - 1, 1)
    cot_far.wait_recv()
    bias_total = feed(0, (2,), bias_total)
    n2_far.wait_recv()
    bias_total = feed(0, (3,), bias_total)
    feed_weights(0, bias_total)
    sum_b_step(1)
    for distance in range(1, chunk_slots // 2):
        sum_send_y(distance)
    feed_result(0)
    if chunks == 2:
        gather_wait(1)
        bias_total = feed(1, (3,), no_bias)
        hand_part(0, 0)
        bias_total = feed(1, (2,), bias_total)
    else:
        hand_part(0, 0)
    hand_cross(0)
    if chunks == 2:
        bias_total = feed(1, (0, 1), bias_total)
    hand_part(0, 1)
    sum_a_until(1)
    if chunks == 2:
        feed_weights(1, bias_total)
    for distance in range(chunk_slots // 2, ring):
        sum_send_y(distance)
    sum_send_y(0)
    sum_b_until(2)
    if chunks == 2:
        feed_result(1)
    hand_part(1, 0)
    hand_part(1, 1)
    hand_cross(1)
    for image in range(2):
        s.n1_t[:, image * seq : (image + 1) * seq] = n1[image].T
    sum_a_until(2)
    part_sib[0, 1].wait_recv()
    cross[0].wait_recv()
    grad_mid, grad_branch = stream, s.grad_branch

    def mid_back(step, totals):
        at = pl.ds(pl.multiple_of(step * block, block), block)
        grads = (
            grad_two[0, at, :] + part_in[0, 1, at, :].astype(F32) + cross_in[0, at, :].astype(F32)
        )
        unit_rows, scale = s.unit_two[at, :], s.scale_two[at, :]
        passed = cot_all[0, at, :].astype(F32)
        mid = passed + norm_back(grads, vecs[3:4, :], unit_rows, scale)
        grad_mid[at, :] = mid
        low = mid.astype(BF16)
        grad_branch[0, at, :] = low
        return (
            totals[0] + fold_rows(grads * unit_rows),
            totals[1] + fold_rows(grads),
            totals[2] + fold_rows(low.astype(F32)),
            totals[3] + fold_rows(passed),
        )

    empty = jnp.zeros((8, width), F32)
    gain_two_sum, shift_two_sum, out_bias_sum, fc2_bias_sum = lax.fori_loop(
        0, blocks, mid_back, (empty,) * 4, unroll=4
    )
    branch_back = links.send(grad_branch.at[0], grad_branch.at[1], sib)

    def mixed_back(image):
        grads = mm_nt(grad_branch[image], wout[...])
        for pair in range(pairs):
            s.grad_mixed[image, pair] = grads[:, pair * LANES : (pair + 1) * LANES].astype(BF16)

    grads_pair = s.grads_pair

    def attend_back(image, pair):
        queries, keys = s.q[image, pair], s.k[image, pair]
        values, grads = s.v[image, pair], s.grad_mixed[image, pair]
        keys_t = (keys * score_scale).T
        grad_values = jnp.zeros((seq, LANES), F32)
        grad_keys = jnp.zeros((seq, LANES), F32)
        grad_queries = []
        for half in range(2):
            probs = s.probs[image * 2 * pairs + pair * 2 + half]
            grads_half = grads * lane_half[half]
            grad_values += mm(probs.astype(BF16), grads_half)
            grad_probs = mm_nt(values, grads_half)
            inner = jnp.sum(grad_probs * probs, axis=0, keepdims=True)
            grad_scores = (probs * (grad_probs - inner)).astype(BF16)
            grad_keys += mm(grad_scores, queries * lane_scaled[half])
            grad_queries.append(
                mm(keys_t[half * HEAD_DIM : (half + 1) * HEAD_DIM], grad_scores)
            )
        grad_query = jnp.concatenate(grad_queries, axis=0).T
        for place, value in enumerate(
            (grad_query, grad_keys, grad_values)
        ):
            grads_pair[pair, image, :, place * LANES : (place + 1) * LANES] = value.astype(BF16)

    def rows_back(image):
        total = mm_nt(grads_pair[0, image], w_pair[0])
        for pair in range(1, pairs):
            total += mm_nt(grads_pair[pair, image], w_pair[pair])
        return total

    def weights_back(pair):
        both = grads_pair[pair].reshape(2 * seq, 3 * LANES)
        for base in range(0, width, 256):
            rows = slice(base, base + 256)
            ar[1 + pair, rows, :] = mm(s.n1_t[rows, :], both).astype(BF16)

    mixed_back(0)
    attend_back(0, 0)
    branch_back.wait_recv()
    mixed_back(1)

    ar = s.ar
    by_core = (one_dev, two_dev, p_one, p_two)
    cuts = [(array, lanes) for array in range(4) for lanes in (pl.ds(0, 256), pl.ds(256, local - 256))]
    flat = [
        (ar.at[array, :, lanes], s.ar_one.at[array, :, lanes], s.ar_two.at[array, :, lanes],
         s.ar_z.at[array, :, :, lanes], s.ar_rest.at[array, :, :, lanes], s.attn.at[array, :, lanes],
         width, by_core)
        for array, lanes in cuts
    ]
    small_half = seq // 2
    small = (s.small, s.small_one, s.small_two, s.small_z, s.small_rest,
             s.small_all, small_half, by_core)
    items = flat + [small]
    stages = [dict() for _ in range(7)]

    def piece(item):
        total_rows = items[item][6]
        _, _, p_one, p_two = items[item][7]
        half, quarter, leaf = total_rows // 2, total_rows // 4, total_rows // 16
        at_one = pl.multiple_of(p_one * half, half)
        at_two = pl.multiple_of(at_one + p_two * quarter, quarter)
        return half, quarter, leaf, at_one, at_two

    def reduce_one(item):
        data, one = items[item][0], items[item][1]
        half, _, _, _, _ = piece(item)
        device, _, p_one, _ = items[item][7]
        other = pl.ds(pl.multiple_of((1 - p_one) * half, half), half)
        stages[0][item] = [links.send(data.at[other], one, device)]

    def reduce_two(item):
        data, one, two = items[item][:3]
        half, quarter, _, at_one, _ = piece(item)
        stages[0][item][0].wait_recv()
        mine = pl.ds(at_one, half)
        data[mine] = (data[mine].astype(F32) + one[...].astype(F32)).astype(data.dtype)
        _, device, _, p_two = items[item][7]
        other = pl.ds(pl.multiple_of(at_one + (1 - p_two) * quarter, quarter), quarter)
        stages[1][item] = [links.send(data.at[other], two, device)]

    def reduce_z(item):
        data, _, two, by_z = items[item][:4]
        _, quarter, leaf, _, at_two = piece(item)
        stages[1][item][0].wait_recv()
        mine = pl.ds(at_two, quarter)
        data[mine] = (data[mine].astype(F32) + two[...].astype(F32)).astype(data.dtype)
        stages[2][item] = links.send_parts(
            [
                (
                    data.at[pl.ds(pl.multiple_of(at_two + ((zq + hop) % 4) * leaf, leaf), leaf)],
                    by_z.at[hop - 1],
                    zdev[hop],
                )
                for hop in range(1, 4)
            ],
            by_z,
        )

    def spread_z(item):
        data, _, _, by_z, by_rest, done = items[item][:6]
        _, _, leaf, _, at_two = piece(item)
        stages[2][item].wait_recv()
        mine = pl.ds(pl.multiple_of(at_two + zq * leaf, leaf), leaf)
        total = data[mine].astype(F32)
        for hop in range(3):
            total += by_z[hop].astype(F32)
        if rest_count > 1:
            by_rest[0] = total.astype(data.dtype)
            copies = [
                links.send(by_rest.at[0], by_rest.at[hop], rdev[hop])
                for hop in range(1, rest_count)
            ]
            for copy in copies:
                copy.wait_recv()
            total = jnp.zeros(total.shape, F32)
            for owner in range(rest_count):
                total += by_rest[(rest - owner + rest_count) % rest_count].astype(F32)
        done[mine] = total.astype(done.dtype)
        stages[3][item] = links.send_parts(
            [(done.at[mine], done.at[mine], zdev[hop]) for hop in range(1, 4)],
            done.at[pl.ds(0, 3 * leaf)],
        )

    def spread_two(item):
        done = items[item][5]
        _, quarter, _, _, at_two = piece(item)
        stages[3][item].wait_recv()
        mine = pl.ds(at_two, quarter)
        stages[4][item] = [links.send(done.at[mine], done.at[mine], items[item][7][1])]

    def spread_one(item):
        done = items[item][5]
        half, _, _, at_one, _ = piece(item)
        stages[4][item][0].wait_recv()
        mine = pl.ds(at_one, half)
        stages[5][item] = [links.send(done.at[mine], done.at[mine], items[item][7][0])]

    def finish(item):
        stages[5][item][0].wait_recv()
        if item < len(cuts):
            array, lanes = cuts[item]
            stores.append(loads.start(s.attn.at[array, :, lanes], out_attn.at[array, :, lanes]))

    for half in range(2):
        at = slice(half * local, (half + 1) * local)
        total = mm(s.mixed_t[0], grad_branch[0, :, at]) + mm(
            s.mixed_t[1], grad_branch[1, :, at]
        )
        ar[0, at, :] = total.astype(BF16)
    def out_back():
        part_sib[1, 1].wait_recv()
        cross[1].wait_recv()

        @pl.loop(0, blocks, unroll=4)
        def _(step):
            at = pl.ds(pl.multiple_of(step * block, block), block)
            row_ids = lax.broadcasted_iota(jnp.int32, (block, 1), 0) + step * block
            total = result[0, at, :] + part_in[1, 1, at, :].astype(F32) + cross_in[1, at, :].astype(F32)
            rows = middle[at, :] + (total + vecs[5:6, :])
            s.own_rows[0, at, :] = jnp.where(row_ids < limit, rows, 0.0).astype(BF16)

        stores.append(loads.start(s.own_rows, out_rows))

    def pair_back(pair):
        if pair == 0:
            sum_b_until(3)
        attend_back(1, pair)
        if pair > 0:
            attend_back(0, pair)
        weights_back(pair)
        if pair == 1:
            sum_a_until(3)

    held = SimpleNamespace()

    def rows_hand():
        s.rows_out[...] = rows_back(1).astype(BF16)
        held.rows_sib = links.send(s.rows_out, s.rows_in, sib)

    def rows_keep():
        s.branch_own[...] = rows_back(0)

    def norm_one_back():
        held.rows_sib.wait_recv()

        def in_back(step, totals):
            at = pl.ds(pl.multiple_of(step * block, block), block)
            grads = (s.branch_own[at, :] + s.rows_in[at, :].astype(F32))
            unit_rows, scale = s.unit_one[at, :], s.scale_one[at, :]
            grad_mid[at, :] += norm_back(grads, vecs[0:1, :], unit_rows, scale)
            return (totals[0] + fold_rows(grads * unit_rows), totals[1] + fold_rows(grads))

        held.sums = lax.fori_loop(0, blocks, in_back, (empty,) * 2, unroll=4)
        sum_a_until(ring)

    theirs = pl.ds(pl.multiple_of((1 - h) * small_half, small_half), small_half)
    ours = pl.ds(pl.multiple_of(h * small_half, small_half), small_half)
    small_ref, small_own = s.small_full, s.small
    small_base = (width // small_ref.shape[1]) * prompt_pad + 6 * (width // small_ref.shape[1])

    def place_small():
        gain_one_sum, shift_one_sum = held.sums
        grad_in = grad_mid[...]
        high = grad_in.astype(BF16)
        low = (grad_in - high.astype(F32)).astype(BF16)
        placed = mm(pick[...], high) + mm(pick[...], low)
        s.own_tok[0] = placed[0:tok_rows]
        stores.append(loads.start(s.own_tok.at[0], out_tok.at[:, 0, :]))

        small_ref[...] = jnp.zeros(small_ref.shape, F32)
        part_width = small_ref.shape[1]
        parts = width // part_width
        for part in range(parts):
            small_ref[part * prompt_pad : part * prompt_pad + prompt_pad, :] = placed[
                tok_pad : tok_pad + prompt_pad, part * part_width : (part + 1) * part_width
            ]
        base = parts * prompt_pad
        sums = (gain_one_sum, shift_one_sum, out_bias_sum, gain_two_sum, shift_two_sum, fc2_bias_sum)
        for place, total in enumerate(sums):
            row = jnp.sum(total, axis=0, keepdims=True)
            for part in range(parts):
                at = base + place * parts + part
                small_ref[at : at + 1, :] = row[:, part * part_width : (part + 1) * part_width]
        base += len(sums) * parts
        for place in range(2):
            at = slice(2 * place * LANES, 2 * place * LANES + LANES)
            row = jnp.concatenate(
                [
                    jnp.sum(
                        grads_pair[pair, 0, :, at].astype(F32) + grads_pair[pair, 1, :, at].astype(F32),
                        axis=0,
                        keepdims=True,
                    )
                    for pair in range(pairs)
                ],
                axis=1,
            )
            for head in range(2):
                chosen = row * (h if head == 1 else 1 - h).astype(F32)
                at = base + head * 4 + place * 2
                small_ref[at : at + 1, :] = chosen[:, 0:part_width]
                small_ref[at + 1 : at + 2, 0 : local - part_width] = chosen[:, part_width:local]
        held.small_sib = links.send(small_ref.at[theirs], s.small_in.at[1], sib)
        sum_b_until(ring)

    def reduce_small():
        held.small_sib.wait_recv()
        small_own[...] = small_ref[ours] + s.small_in[1]

    blocks_beside = [
        functools.partial(pair_back, 0), functools.partial(pair_back, 1), functools.partial(pair_back, 2),
        rows_hand, rows_keep, norm_one_back, place_small, out_back,
    ]
    steps = [reduce_one, reduce_two, reduce_z, spread_z, spread_two, spread_one, finish]
    for item, stage in REDUCE_ORDER:
        if item < 0:
            blocks_beside[-1 - item]()
        else:
            if stage == 0 and item == len(cuts):
                reduce_small()
            steps[stage](item)
            if (item, stage) == LATE_SUM:
                sum_b_end()
    final = s.small_out
    final[ours] = s.small_all[...]
    small_back = links.send(s.small_all, s.small_in.at[0], sib)
    small_back.wait_recv()
    final[theirs] = s.small_in[0]
    final[small_base + 8 : small_base + 12, :] = jnp.where(
        h == 0, final[small_base : small_base + 4, :], final[small_base + 4 : small_base + 8, :]
    )
    stores.append(loads.start(final, out_small))
    links.drain()
    for copy in stores:
        copy.wait()


def finish_kernel(dims, *refs):
    it = iter(refs)
    rows_in, tok_in, attn_in, small_in, fc1_in, fc2_in, bias_in = (next(it) for _ in range(7))
    (
        layer_out, grad_tokens, grad_prompts, gain_one, shift_one, w_query, b_query, w_key,
        w_value, b_value, w_out, b_out, gain_two, shift_two, w_fc1, b_fc1, w_fc2, b_fc2,
    ) = (next(it) for _ in range(18))
    s = SimpleNamespace(**dict(zip(dims.finish, it)))
    width, local = dims.width, dims.local
    rows = w_fc1.shape[0]
    loads = Loads(s.load_sems, dims.finish_depth)
    load_small = loads.start(small_in, s.small)
    load_bias = loads.start(bias_in, s.bias)
    load_attn = [loads.start(attn_in.at[array], s.attn.at[array]) for array in (1, 2, 3, 0)]
    passing = [(rows_in, s.rows, layer_out), (tok_in, s.tok, grad_tokens)]
    whole_shards = rows == fc1_in.shape[0]
    if whole_shards:
        passing += [(fc1_in, s.fc1, w_fc1), (fc2_in, s.fc2, w_fc2)]
    passing = [(loads.start(source, held), held, target) for source, held, target in passing]
    stores = []
    load_small.wait()
    load_bias.wait()
    part_width = s.small.shape[1]
    parts = width // part_width
    for part in range(parts):
        at = slice(part * part_width, (part + 1) * part_width)
        s.prompts[:, at] = s.small[part * dims.prompt_pad : part * dims.prompt_pad + dims.prompt_rows]
    stores.append(loads.start(s.prompts, grad_prompts))
    base = parts * dims.prompt_pad
    for place, target in enumerate((gain_one, shift_one, b_out, gain_two, shift_two, b_fc2)):
        for part in range(parts):
            at = base + place * parts + part
            s.row[place : place + 1, part * part_width : (part + 1) * part_width] = s.small[at : at + 1]
        s.flat[place, :] = s.row[place : place + 1, :].reshape(width)
        stores.append(loads.start(s.flat.at[place], target))
    base += 6 * parts + 8
    for place, target in enumerate((b_query, b_value)):
        at = base + 2 * place
        s.row[6:7, 0:part_width] = s.small[at : at + 1]
        s.row[6:7, part_width : 2 * part_width] = s.small[at + 1 : at + 2]
        s.half_flat[place, :] = s.row[6:7, 0:local].reshape(local)
        stores.append(loads.start(s.half_flat.at[place], target))
    b_fc1[...] = s.bias[0:1, 0:rows].reshape(rows)
    for pair in range(3):
        load_attn[pair].wait()
        at = slice(pair * LANES, (pair + 1) * LANES)
        for place, target in enumerate((w_query, w_key, w_value)):
            s.tall[place, :, at] = s.attn[1 + pair, :, place * LANES : (place + 1) * LANES].astype(F32)
            stores.append(loads.start(s.tall.at[place, :, pl.ds(pair * LANES, LANES)], target.at[:, pl.ds(pair * LANES, LANES)]))
    load_attn[3].wait()
    s.wide[:, 0:local] = s.attn[0, 0:local].astype(F32)
    s.wide[:, local : 2 * local] = s.attn[0, local : 2 * local].astype(F32)
    stores.append(loads.start(s.wide, w_out))
    for load, held, target in passing:
        load.wait()
        stores.append(loads.start(held, target))
    if not whole_shards:
        for source, held, target in ((fc1_in, s.fc1, w_fc1), (fc2_in, s.fc2, w_fc2)):
            loads.start(source, held).wait()
            s.cut[...] = held[0:rows]
            loads.start(s.cut, target).wait()
    for copy in stores:
        copy.wait()


def layer(dims, operands):
    seq, width, local = dims.seq, dims.width, dims.local
    n, ring, slots, rows_per = dims.n, dims.ring, dims.slots, dims.rows_per
    pairs = local // LANES
    chunk = dims.chunk_slots * rows_per
    rest_count = n // 16
    small_half = seq // 2
    part_width = 256
    arrivals = 11 * ring + 68 + 9 * (rest_count - 1)
    vmem = pltpu.VMEM
    shared = 2 * rows_per
    scratch = dict(
        send_sems=pltpu.SemaphoreType.DMA((dims.send_depth,)),
        recv_sems=pltpu.SemaphoreType.DMA((arrivals,)),
        w_all=vmem((slots, shared, width), BF16),
        b_all=vmem((slots, 8, LANES), F32),
        cot_all=vmem((4, seq, width), BF16),
        meta=vmem((2, 8, LANES), jnp.int32),
        load_sems=pltpu.SemaphoreType.DMA((dims.load_depth,)),
        kept=vmem((1, dims.patches), jnp.int32),
        tokens=vmem((1, dims.tok_rows, width), BF16),
        prompts=vmem((dims.prompt_rows, width), BF16),
        gain_one=vmem((width,), BF16),
        shift_one=vmem((width,), BF16),
        b_query=vmem((local,), BF16),
        b_value=vmem((local,), BF16),
        b_out=vmem((width,), BF16),
        gain_two=vmem((width,), BF16),
        shift_two=vmem((width,), BF16),
        b_fc1=vmem((dims.rows,), BF16),
        b_fc2=vmem((width,), BF16),
        vecs=vmem((8, width), F32),
        w_pair=vmem((pairs, width, 3 * LANES), BF16),
        wout=vmem((local, width), BF16),
        unit_one=vmem((seq, width), F32),
        unit_two=vmem((seq, width), F32),
        scale_one=vmem((seq, 1), F32),
        scale_two=vmem((seq, 1), F32),
        own_rows=vmem((1, seq, width), BF16),
        own_tok=vmem((1, dims.tok_rows, width), F32),
        own_fc1=vmem((rows_per, width), F32),
        own_fc2=vmem((rows_per, width), F32),
        own_bias=vmem((8, LANES), F32),
        attn=vmem((4, width, local), BF16),
        src=vmem((dims.tok_pad + dims.prompt_pad, width), BF16),
        pick=vmem((dims.tok_pad + dims.prompt_pad, seq), BF16),
        idx=vmem((8, seq), jnp.int32),
        stream=vmem((seq, width), F32),
        middle=vmem((seq, width), F32),
        n1=vmem((2, seq, width), BF16),
        n2=vmem((4, seq, width), BF16),
        q=vmem((2, pairs, seq, LANES), BF16),
        k=vmem((2, pairs, seq, LANES), BF16),
        v=vmem((2, pairs, seq, LANES), BF16),
        probs=vmem((4 * pairs, seq, seq), F32),
        mixed_t=vmem((2, local, seq), BF16),
        branch_out=vmem((seq, width), F32),
        branch_in=vmem((seq, width), F32),
        branch_own=vmem((seq, width), F32),
        hidden=vmem((slots // dims.chunk_slots, 4, seq, chunk), BF16),
        grad_before=vmem((4, seq, chunk), BF16),
        result=vmem((4, seq, width), F32),
        grad_two=vmem((4, seq, width), F32),
        part_out=vmem((2, 2, seq, width), BF16),
        part_in=vmem((2, 2, seq, width), BF16),
        cross_out=vmem((2, seq, width), BF16),
        cross_in=vmem((2, seq, width), BF16),
        g_all=vmem((slots, shared, width), BF16),
        gb_all=vmem((slots, 8, LANES), F32),
        ry=vmem((ring, rows_per, width), BF16),
        ry_last=vmem((rows_per, width), BF16),
        rb_out=vmem((ring, 2, rows_per, width), BF16),
        rb_in=vmem((ring, 2, rows_per, width), BF16),
        n1_t=vmem((width, 2 * seq), BF16),
        ryb=vmem((ring, 8, LANES), F32),
        rz_out=vmem((ring, rows_per, width), BF16),
        rzb_out=vmem((ring, 8, LANES), F32),
        rz_in=vmem((ring, rows_per, width), BF16),
        rzb_in=vmem((ring, 8, LANES), F32),
        grad_branch=vmem((2, seq, width), BF16),
        grad_mixed=vmem((2, pairs, seq, LANES), BF16),
        grads_pair=vmem((pairs, 2, seq, 3 * LANES), BF16),
        rows_out=vmem((seq, width), BF16),
        rows_in=vmem((seq, width), BF16),
        ar=vmem((4, width, local), BF16),
        ar_one=vmem((4, width // 2, local), BF16),
        ar_two=vmem((4, width // 4, local), BF16),
        ar_z=vmem((4, 3, width // 16, local), BF16),
        ar_rest=vmem((4, rest_count, width // 16, local), BF16),
        small_full=vmem((seq, part_width), F32),
        small_out=vmem((seq, part_width), F32),
        small_in=vmem((2, small_half, part_width), F32),
        small=vmem((small_half, part_width), F32),
        small_one=vmem((small_half // 2, part_width), F32),
        small_two=vmem((small_half // 4, part_width), F32),
        small_z=vmem((3, small_half // 16, part_width), F32),
        small_rest=vmem((rest_count, small_half // 16, part_width), F32),
        small_all=vmem((small_half, part_width), F32),
    )
    dims = SimpleNamespace(**vars(dims), scratch=tuple(scratch))
    anywhere = pl.BlockSpec(memory_space=pl.ANY)
    shape = jax.ShapeDtypeStruct
    return pl.pallas_call(
        functools.partial(layer_kernel, dims),
        out_shape=(
            shape((1, seq, width), BF16),
            shape((dims.tok_rows, 1, width), F32),
            shape((4, width, local), BF16),
            shape((seq, part_width), F32),
            shape((rows_per, width), F32),
            shape((rows_per, width), F32),
            shape((8, LANES), F32),
        ),
        in_specs=[pl.BlockSpec(memory_space=pltpu.SMEM)] + [anywhere] * (len(operands) - 1),
        out_specs=[anywhere] * 7,
        scratch_shapes=list(scratch.values()),
        compiler_params=pltpu.CompilerParams(
            collective_id=0, has_side_effects=True, vmem_limit_bytes=63 * 2**20
        ),
    )(*operands)


def finish(dims, results):
    seq, width, local, rows = dims.seq, dims.width, dims.local, dims.rows
    vmem = pltpu.VMEM
    scratch = dict(
        load_sems=pltpu.SemaphoreType.DMA((dims.finish_depth,)),
        attn=vmem((4, width, local), BF16),
        wide=vmem((local, width), F32),
        tall=vmem((3, width, local), F32),
        small=vmem(results[3].shape, F32),
        bias=vmem((8, LANES), F32),
        prompts=vmem((dims.prompt_rows, width), F32),
        row=vmem((8, width), F32),
        flat=vmem((6, width), F32),
        half_flat=vmem((2, local), F32),
        rows=vmem((1, seq, width), BF16),
        tok=vmem((dims.tok_rows, 1, width), F32),
        fc1=vmem((dims.rows_per, width), F32),
        fc2=vmem((dims.rows_per, width), F32),
        cut=vmem((rows, width), F32),
    )
    dims = SimpleNamespace(**vars(dims), finish=tuple(scratch))
    anywhere = pl.BlockSpec(memory_space=pl.ANY)
    whole = pl.BlockSpec(memory_space=pltpu.VMEM)

    def out(*sizes, dtype=F32):
        return jax.ShapeDtypeStruct(sizes, dtype)

    shapes = (
        out(1, seq, width, dtype=BF16), out(dims.tok_rows, 1, width), out(dims.prompt_rows, width),
        out(width), out(width), out(width, local), out(local), out(width, local),
        out(width, local), out(local), out(local, width), out(width), out(width), out(width),
        out(rows, width), out(rows), out(rows, width), out(width),
    )
    return pl.pallas_call(
        functools.partial(finish_kernel, dims),
        out_shape=shapes,
        in_specs=[anywhere] * 7,
        out_specs=[whole if place == 15 else anywhere for place in range(len(shapes))],
        scratch_shapes=list(scratch.values()),
        compiler_params=pltpu.CompilerParams(vmem_limit_bytes=60 * 2**20),
    )(*results)


def body(n, *arguments):
    (
        tokens, kept_index, kept_count, prompts, gain_one, shift_one, w_query, b_query, w_key,
        w_value, b_value, w_out, b_out, gain_two, shift_two, w_fc1, b_fc1, w_fc2, b_fc2, cotangent,
    ) = arguments
    seq, width = cotangent.shape[1:]
    local = w_query.shape[1]
    rows = w_fc1.shape[0]
    rows_per = round_up(rows, 16)
    ring = n // 4
    slots = 2 * ring
    halves = slots // 2
    chunk_slots = halves if (halves % 2 == 0 and halves * rows_per % LANES == 0) else slots
    tok_rows, prompt_rows = tokens.shape[1], prompts.shape[0]
    dims = SimpleNamespace(
        n=n, ring=ring, slots=slots, chunk_slots=chunk_slots, rows_per=rows_per, rows=rows, seq=seq,
        width=width, local=local, tok_rows=tok_rows, tok_pad=round_up(tok_rows, 16),
        prompt_rows=prompt_rows, prompt_pad=round_up(prompt_rows, 16),
        patches=kept_index.shape[1], send_depth=32, load_depth=17, finish_depth=32,
    )
    if rows_per != rows:
        spare = ((0, rows_per - rows), (0, 0))
        w_fc1, w_fc2 = jnp.pad(w_fc1, spare), jnp.pad(w_fc2, spare)
    operands = (
        kept_count, tokens, kept_index, prompts, w_fc1, w_fc2, cotangent, w_query, w_key, w_value,
        w_out, gain_one, shift_one, b_query, b_value, b_out, gain_two, shift_two, b_fc1, b_fc2,
    )
    outs = list(finish(dims, layer(dims, operands)))
    outs[1] = outs[1].transpose(1, 0, 2)
    return tuple(outs)


def solution(mesh):
    batch, head = mesh.axis_names
    both = (batch, head)
    placed = (
        P(both, None, None), P(both, None), P(both), P(), P(), P(), P(None, head), P(head),
        P(None, head), P(None, head), P(head), P(head, None), P(), P(), P(),
        P(both, None), P(both), P(both, None), P(), P(both, None, None),
    )
    return jax.shard_map(
        functools.partial(body, mesh.shape[batch]),
        mesh=mesh,
        in_specs=placed,
        out_specs=(
            P(both, None, None), P(both, None, None), P(), P(), P(), P(None, head), P(head),
            P(None, head), P(None, head), P(head), P(head, None), P(), P(), P(),
            P(both, None), P(both), P(both, None), P(),
        ),
        check_vma=False,
    )
```

```python
import functools
from types import SimpleNamespace

import jax
import jax.numpy as jnp
from jax import lax
from jax.experimental import pallas as pl
from jax.experimental.pallas import tpu as pltpu
from jax.sharding import PartitionSpec as P

MESH = pl.DeviceIdType.MESH
HEAD_DIM = 64
EPSILON = 1e-06
LANES = 128
BF16 = jnp.bfloat16
F32 = jnp.float32


def round_up(value, step):
    return -(-value // step) * step


def mm(left, right):
    return lax.dot_general(left, right, (((1,), (0,)), ((), ())), preferred_element_type=F32)


def mm_nt(left, right):
    return lax.dot_general(left, right, (((1,), (1,)), ((), ())), preferred_element_type=F32)


def mm_tn(left, right):
    return lax.dot_general(left, right, (((0,), (0,)), ((), ())), preferred_element_type=F32)


def fold_rows(rows):
    count, width = rows.shape
    return jnp.sum(rows.reshape(count // 8, 8, width), axis=0)


def normalise(rows):
    width = rows.shape[1]
    centre = jnp.sum(rows, axis=1, keepdims=True) * (1.0 / width)
    centred = rows - centre
    spread = jnp.sum(centred * centred, axis=1, keepdims=True) * (1.0 / width)
    scale = lax.rsqrt(spread + EPSILON)
    return centred * scale, scale


def norm_back(grad_rows, gain_row, unit_rows, scale):
    width = grad_rows.shape[1]
    scaled = grad_rows * gain_row
    mean_one = jnp.sum(scaled, axis=1, keepdims=True) * (1.0 / width)
    mean_two = jnp.sum(scaled * unit_rows, axis=1, keepdims=True) * (1.0 / width)
    return scale * (scaled - mean_one - unit_rows * mean_two)


GELU_A = 0.7978845608028654
GELU_B = 0.044715


def gelu_both(value):
    square = value * value
    bend = jnp.tanh(value * (GELU_A + (GELU_A * GELU_B) * square))
    half = 0.5 + 0.5 * bend
    slope = half + (0.5 * value) * (1.0 - bend * bend) * (
        GELU_A + (3.0 * GELU_A * GELU_B) * square
    )
    return value * half, slope


VECTORS = (
    "gain_one", "shift_one", "b_query", "b_value", "b_out", "gain_two", "shift_two", "b_fc1", "b_fc2",
)


LATE_SUM = (8, 3)
REDUCE_ORDER = (
    (0, 0), (-1, 0), (3, 0), (-2, 0), (5, 0), (1, 0), (-3, 0), (4, 0), (7, 0), (3, 1), (0, 1),
    (5, 1), (2, 0), (1, 1), (3, 2), (0, 2), (4, 1), (5, 2), (1, 2), (3, 3), (-4, 0), (7, 1),
    (6, 0), (0, 3), (1, 3), (7, 2), (4, 2), (2, 1), (3, 4), (-5, 0), (1, 4), (5, 3), (0, 4),
    (6, 1), (-6, 0), (7, 3), (2, 2), (-7, 0), (4, 3), (8, 0), (3, 5), (1, 5), (5, 4), (7, 4),
    (6, 2), (-8, 0), (8, 1), (2, 3), (0, 5), (6, 3), (5, 5), (4, 4), (8, 2), (2, 4), (7, 5),
    (8, 3), (6, 4), (3, 6), (4, 5), (2, 5), (8, 4), (7, 6), (5, 6), (6, 5), (8, 5), (0, 6), (4, 6),
    (8, 6), (6, 6), (1, 6), (2, 6),
)


class Once:
    def __init__(self, wait):
        self.pending = wait

    def wait(self):
        if self.pending is not None:
            self.pending()
            self.pending = None


class Loads:
    def __init__(self, sems, depth):
        self.sems = sems
        self.depth = depth
        self.copies = []

    def take(self):
        place = len(self.copies)
        if place >= self.depth:
            self.copies[place - self.depth].wait()
        return self.sems.at[place % self.depth]

    def start(self, source, target):
        copy = pltpu.make_async_copy(source, target, self.take())
        copy.start()
        self.copies.append(Once(copy.wait))
        return self.copies[-1]

    def start_parts(self, pieces, whole):
        sem = self.take()
        for source, target in pieces:
            pltpu.make_async_copy(source, target, sem).start()
        self.copies.append(Once(pltpu.make_async_copy(whole, whole, sem).wait))
        return self.copies[-1]


class Links:
    def __init__(self, send_sems, recv_sems, depth):
        self.send_sems = send_sems
        self.recv_sems = recv_sems
        self.depth = depth
        self.sends = []
        self.arrivals = 0
        self.spare = []

    def copy(self, source, target, device, arrival):
        place = len(self.sends)
        if place >= self.depth:
            self.sends[place - self.depth].wait()
        copy = pltpu.make_async_remote_copy(
            src_ref=source,
            dst_ref=target,
            send_sem=self.send_sems.at[place % self.depth],
            recv_sem=self.recv_sems.at[arrival],
            device_id=device,
            device_id_type=MESH,
        )
        copy.start()
        self.sends.append(Once(copy.wait_send))
        return copy

    def send(self, source, target, device, again=False):
        if again and self.spare:
            return self.copy(source, target, device, self.spare.pop(0))
        copy = self.copy(source, target, device, self.arrivals)
        self.arrivals += 1
        return copy

    def send_parts(self, pieces, whole):
        arrival = self.arrivals
        self.arrivals += 1
        for source, target, device in pieces:
            self.copy(source, target, device, arrival)
        return pltpu.make_async_remote_copy(
            src_ref=whole,
            dst_ref=whole,
            send_sem=self.send_sems.at[0],
            recv_sem=self.recv_sems.at[arrival],
            device_id=device,
            device_id_type=MESH,
        )

    def drain(self):
        for copy in self.sends:
            copy.wait()


def layer_kernel(dims, *refs):
    it = iter(refs)
    count_ref = next(it)
    tokens, kept, prompts, fc1, fc2, cot = (next(it) for _ in range(6))
    weights_in = [next(it) for _ in range(4)]
    vectors_in = [next(it) for _ in range(9)]
    out_rows, out_tok, out_attn, out_small, out_fc1, out_fc2, out_bias = (
        next(it) for _ in range(7)
    )
    s = SimpleNamespace(**dict(zip(dims.scratch, it)))
    w_pair, wout = s.w_pair, s.wout
    vecs = s.vecs
    seq, width, local = dims.seq, dims.width, dims.local
    pairs = local // LANES
    rows_per = dims.rows_per
    n, ring, slots = dims.n, dims.ring, dims.slots
    chunk_slots = dims.chunk_slots
    chunk = chunk_slots * rows_per
    chunks = slots // chunk_slots
    tok_rows, tok_pad, prompt_pad = dims.tok_rows, dims.tok_pad, dims.prompt_pad
    prompt_rows, patches = dims.prompt_rows, dims.patches
    rest_count = n // 16
    score_scale = HEAD_DIM**-0.5
    block = 32
    blocks = seq // block

    b = lax.axis_index("batch")
    h = lax.axis_index("head")
    bx = b % 2
    by = (b // 2) % 2
    zz = b // 4
    sib = (b, 1 - h)
    xdev = (b + 1 - 2 * bx, h)
    ydev = (b + 2 - 4 * by, h)
    corner = b % 4
    ring_next = (((zz + 1) % ring) * 4 + corner, h)
    ring_prev = (((zz + ring - 1) % ring) * 4 + corner, h)
    zq = zz % 4
    zdev = [((zz - zq + (zq + hop) % 4) * 4 + corner, h) for hop in range(4)]
    rest = b // 16
    rdev = [(((rest + hop) % rest_count) * 16 + b % 16, h) for hop in range(rest_count)]
    one_dev = (xdev[0] * (1 - h) + ydev[0] * h, h)
    two_dev = (ydev[0] * (1 - h) + xdev[0] * h, h)
    p_one = bx * (1 - h) + by * h
    p_two = by * (1 - h) + bx * h

    partners = [sib, xdev, ydev] + zdev[1:]
    if ring > 4:
        partners += [ring_next, ring_prev] + rdev[1:]
    barrier = pltpu.get_barrier_semaphore()
    for partner in partners:
        pl.semaphore_signal(barrier, inc=1, device_id=partner, device_id_type=MESH)

    links = Links(s.send_sems, s.recv_sems, dims.send_depth)

    w_all, b_all, cot_all = s.w_all, s.b_all, s.cot_all
    loads = Loads(s.load_sems, dims.load_depth)
    load_kept = loads.start(kept, s.kept)
    load_fc = [
        loads.start(fc1, w_all.at[0, pl.ds(0, rows_per)]),
        loads.start(fc2, w_all.at[0, pl.ds(rows_per, rows_per)]),
    ]
    load_cot = loads.start(cot.at[0], cot_all.at[0])
    load_rows = [loads.start(tokens, s.tokens), loads.start(prompts, s.prompts)]
    load_vectors = [loads.start(ref, getattr(s, name)) for ref, name in zip(vectors_in, VECTORS)]
    load_weights = [
        loads.start(weights_in[3], wout),
        loads.start_parts(
            [
                (
                    weights_in[place].at[:, pl.ds(pair * LANES, LANES)],
                    w_pair.at[pair, :, pl.ds(place * LANES, LANES)],
                )
                for pair in range(pairs)
                for place in range(3)
            ],
            w_pair,
        ),
    ]

    limit = count_ref[0] + (1 + prompt_rows)
    src, pick = s.src, s.pick
    s.meta[0] = jnp.broadcast_to(limit, (8, LANES))
    s.idx[...] = jnp.zeros((8, seq), jnp.int32)
    src[tok_rows - tok_rows % 16 : tok_pad] = jnp.zeros((tok_pad - tok_rows + tok_rows % 16, width), BF16)
    src[tok_pad:] = jnp.zeros((prompt_pad, width), BF16)
    vecs[...] = jnp.zeros(vecs.shape, F32)
    load_kept.wait()
    s.idx[0:1, 0:patches] = s.kept[...]
    shifted = pltpu.roll(s.idx[...], 1 + prompt_rows, axis=1)[0:1, :]
    spot = lax.broadcasted_iota(jnp.int32, (1, seq), 1)
    wanted = jnp.where(
        spot < 1 + prompt_rows,
        jnp.where(spot == 0, 0, tok_pad - 1 + spot),
        jnp.where(spot < limit, shifted + 1, -1),
    )
    pick[...] = jnp.where(
        lax.broadcasted_iota(jnp.int32, pick.shape, 0) == wanted, 1.0, 0.0
    ).astype(BF16)
    for copy in load_vectors:
        copy.wait()
    for place, name in enumerate(("gain_one", "shift_one", "b_out", "gain_two", "shift_two", "b_fc2")):
        vecs[place : place + 1, :] = getattr(s, name)[...].astype(F32).reshape(1, width)
    vecs[6:7, 0:local] = s.b_query[...].astype(F32).reshape(1, local)
    vecs[6:7, local : 2 * local] = s.b_value[...].astype(F32).reshape(1, local)
    bias_rows = s.b_fc1.shape[0]
    vecs[7:8, 0:bias_rows] = s.b_fc1[...].astype(F32).reshape(1, bias_rows)
    b_all[0] = jnp.broadcast_to(vecs[7:8, 0:LANES], (8, LANES))
    load_cot.wait()

    @pl.loop(0, blocks, unroll=4)
    def _(step):
        at = pl.ds(pl.multiple_of(step * block, block), block)
        row_ids = lax.broadcasted_iota(jnp.int32, (block, 1), 0) + step * block
        rows = cot_all[0, at, :].astype(F32)
        cot_all[0, at, :] = jnp.where(row_ids < limit, rows, 0.0).astype(BF16)

    for copy in load_rows:
        copy.wait()
    src[0:tok_rows, :] = s.tokens[0]
    src[tok_pad : tok_pad + prompt_rows, :] = s.prompts[...]
    stream = s.stream
    stream[...] = mm_tn(pick[...], src[...])

    n1 = s.n1

    @pl.loop(0, blocks, unroll=4)
    def _(step):
        at = pl.ds(pl.multiple_of(step * block, block), block)
        unit_rows, s.scale_one[at, :] = normalise(stream[at, :])
        s.unit_one[at, :] = unit_rows
        n1[0, at, :] = (unit_rows * vecs[0:1, :] + vecs[1:2, :]).astype(BF16)

    for copy in load_fc:
        copy.wait()
    pl.semaphore_wait(barrier, len(partners))

    gather_ring, gather_y = {}, {}

    def gather_step(distance, kind):
        if distance > 0:
            for copy in gather_ring[distance, kind]:
                copy.wait_recv()
        rows = pl.ds(kind * rows_per, rows_per)
        mine = 2 * distance

        def hand_on(slot, device):
            copies = [links.send(w_all.at[mine, rows], w_all.at[slot, rows], device)]
            if kind == 0:
                copies.append(links.send(b_all.at[mine], b_all.at[slot], device))
            return copies

        if distance + 1 < ring:
            gather_ring[distance + 1, kind] = hand_on(mine + 2, ring_next)
        gather_y[distance, kind] = hand_on(mine + 1, ydev)

    gather_done = [0]

    def gather_until(distance, kind):
        while gather_done[0] <= min(2 * distance + kind, 2 * ring - 1):
            gather_step(gather_done[0] // 2, gather_done[0] % 2)
            gather_done[0] += 1

    n1_sib = links.send(n1.at[0], n1.at[1], sib)
    gather_until(0, 1)
    cot_x = links.send(cot_all.at[0], cot_all.at[2], xdev)
    cot_sib = links.send(cot_all.at[0], cot_all.at[1], sib)
    meta_sib = links.send(s.meta.at[0], s.meta.at[1], sib)


    def project(image):
        rows = n1[image]
        for pair in range(pairs):
            found = mm(rows, w_pair[pair])
            at = slice(pair * LANES, (pair + 1) * LANES)
            s.q[image, pair] = (found[:, 0:LANES] + vecs[6:7, at]).astype(BF16)
            s.k[image, pair] = found[:, LANES : 2 * LANES].astype(BF16)
            at = slice(local + pair * LANES, local + (pair + 1) * LANES)
            s.v[image, pair] = (found[:, 2 * LANES :] + vecs[6:7, at]).astype(BF16)

    lane_ids = lax.broadcasted_iota(jnp.int32, (1, LANES), 1)
    lane_half = [
        jnp.where(lane_ids // HEAD_DIM == half, 1.0, 0.0).astype(BF16) for half in range(2)
    ]
    lane_scaled = [
        jnp.where(lane_ids // HEAD_DIM == half, score_scale, 0.0).astype(BF16) for half in range(2)
    ]
    lane_spare = [
        jnp.where(lane_ids == (1 - half) * HEAD_DIM, 1.0, 0.0).astype(BF16) for half in range(2)
    ]
    key_ids = lax.broadcasted_iota(jnp.int32, (seq, 1), 0)

    def attend(image, first, last):
        key_bias = jnp.where(key_ids < s.meta[image, 0:1, 0:1], 0.0, -1e30).astype(BF16)

        for pair in range(first, last):
            queries, keys = s.q[image, pair], s.k[image, pair]
            values_t = s.v[image, pair].T
            for half in range(2):
                scores = mm_nt(
                    keys * lane_half[half] + key_bias * lane_spare[half],
                    queries * lane_scaled[half] + lane_spare[half],
                )
                weights = jnp.exp(scores - jnp.max(scores, axis=0, keepdims=True))
                probs = weights * (1.0 / jnp.sum(weights, axis=0, keepdims=True))
                s.probs[image * 2 * pairs + pair * 2 + half] = probs
                mixed_t = mm(values_t[half * HEAD_DIM : (half + 1) * HEAD_DIM], probs.astype(BF16))
                at = pl.ds(pair * LANES + half * HEAD_DIM, HEAD_DIM)
                s.mixed_t[image, at, :] = mixed_t.astype(BF16)

    for copy in load_weights:
        copy.wait()
    project(0)
    n1_sib.wait_recv()
    meta_sib.wait_recv()
    project(1)
    attend(1, 0, pairs)
    s.branch_out[...] = mm_tn(s.mixed_t[1], wout[...])
    branch_sib = links.send(s.branch_out, s.branch_in, sib)
    gather_until(1, 0)
    attend(0, 0, pairs)
    gather_until(1, 1)
    s.branch_own[...] = mm_tn(s.mixed_t[0], wout[...])
    branch_sib.wait_recv()
    middle, n2 = s.middle, s.n2

    @pl.loop(0, blocks, unroll=4)
    def _(step):
        at = pl.ds(pl.multiple_of(step * block, block), block)
        rows = stream[at, :] + (s.branch_own[at, :] + s.branch_in[at, :] + vecs[2:3, :])
        middle[at, :] = rows
        unit_rows, s.scale_two[at, :] = normalise(rows)
        s.unit_two[at, :] = unit_rows
        n2[0, at, :] = (unit_rows * vecs[3:4, :] + vecs[4:5, :]).astype(BF16)

    n2_x = links.send(n2.at[0], n2.at[2], xdev)
    n2_sib = links.send(n2.at[0], n2.at[1], sib)
    gather_until(2, 0)
    cot_x.wait_recv()
    cot_far = links.send(cot_all.at[2], cot_all.at[3], sib)
    hidden_all, before_all = s.hidden, s.grad_before
    result, grad_two = s.result, s.grad_two
    unpack = jnp.where(
        lax.broadcasted_iota(jnp.int32, (LANES, chunk), 1) % rows_per
        == lax.broadcasted_iota(jnp.int32, (LANES, chunk), 0),
        1.0,
        0.0,
    )
    owner_of = (
        lax.broadcasted_iota(jnp.int32, (chunk_slots, chunk), 1) // rows_per
        == lax.broadcasted_iota(jnp.int32, (chunk_slots, chunk), 0)
    )

    def feed_spans(part):
        span = slice(part * chunk_slots, (part + 1) * chunk_slots)
        return (
            w_all[span, 0:rows_per].reshape(chunk, width),
            w_all[span, rows_per : 2 * rows_per].reshape(chunk, width),
        )

    def feed(part, images, totals):
        span = slice(part * chunk_slots, (part + 1) * chunk_slots)
        tiles = b_all[span, 0, :].astype(BF16)
        bias_row = jnp.sum(
            jnp.where(owner_of, mm(tiles, unpack.astype(BF16)), 0.0), axis=0, keepdims=True
        )
        up, down = feed_spans(part)
        for image in images:
            before = mm_nt(n2[image], up) + bias_row
            hidden, slope = gelu_both(before)
            hidden_all[part, image] = hidden.astype(BF16)
            grad_before = (mm_nt(cot_all[image], down) * slope).astype(BF16)
            before_all[image] = grad_before
            if part == 0:
                grad_two[image] = mm(grad_before, up)
            else:
                grad_two[image] += mm(grad_before, up)
            totals += fold_rows(grad_before.astype(F32))
        return totals

    def feed_result(part):
        @pl.loop(0, 4)
        def _(image):
            _, down = feed_spans(part)
            if part == 0:
                result[image] = mm(hidden_all[part, image], down)
            else:
                result[image] += mm(hidden_all[part, image], down)

    g_all, gb_all = s.g_all, s.gb_all

    def feed_weights(part, bias_total):
        first = part * chunk_slots
        span = slice(first, first + chunk_slots)

        for left, right, base in ((before_all, n2, 0), (hidden_all.at[part], cot_all, rows_per)):
            total = jnp.zeros((chunk, width), F32)
            for image in range(4):
                total += mm_tn(left[image], right[image])
            g_all[span, base : base + rows_per] = (
                total.astype(BF16).reshape(chunk_slots, rows_per, width)
            )
        bias_row = jnp.sum(bias_total, axis=0, keepdims=True)
        spread = jnp.where(owner_of, jnp.broadcast_to(bias_row, owner_of.shape), 0.0)
        high = spread.astype(BF16)
        low = (spread - high.astype(F32)).astype(BF16)
        packed = mm_nt(high, unpack.astype(BF16)) + mm_nt(low, unpack.astype(BF16))
        for slot in range(chunk_slots):
            gb_all[first + slot] = jnp.broadcast_to(packed[slot : slot + 1], (8, LANES))

    order = list(range(1, ring)) + [0]
    stores = []
    sum_y, sum_ring, sum_both, sum_last = {}, {}, {}, []
    first_rows, second_rows = pl.ds(0, rows_per), pl.ds(rows_per, rows_per)

    def sum_send_y(distance):
        slot = 2 * distance + 1
        sum_y[distance] = [
            links.send(g_all.at[slot, first_rows], s.ry.at[distance], ydev),
            links.send(gb_all.at[slot], s.ryb.at[distance], ydev),
        ]

    def sum_a_step(distance):
        for copy in sum_y[distance]:
            copy.wait_recv()
        mine = 2 * distance
        total = g_all[mine, 0:rows_per].astype(F32) + s.ry[distance].astype(F32)
        bias = gb_all[mine] + s.ryb[distance]
        if distance != 1:
            before = (distance + ring - 1) % ring
            for copy in sum_ring[before]:
                copy.wait_recv()
            total += s.rz_in[before].astype(F32)
            bias += s.rzb_in[before]
        if distance == 0:
            s.own_fc1[...] = total
            s.own_bias[...] = bias
            stores.append(loads.start(s.own_fc1, out_fc1))
            stores.append(loads.start(s.own_bias, out_bias))
        else:
            s.rz_out[distance] = total.astype(BF16)
            s.rzb_out[distance] = bias
            sum_ring[distance] = [
                links.send(s.rz_out.at[distance], s.rz_in.at[distance], ring_next),
                links.send(s.rzb_out.at[distance], s.rzb_in.at[distance], ring_next),
            ]

    def sum_b_step(distance):
        if distance == 1:
            source = g_all.at[pl.ds(2, 2), second_rows]
            sum_both[1] = links.send(source, s.rb_in.at[1], ring_next)
            return
        before = (distance + ring - 1) % ring
        sum_both[before].wait_recv()
        for line in range(2):
            total = g_all[2 * distance + line, rows_per:].astype(F32) + s.rb_in[before, line].astype(F32)
            if distance == 0 and line == 0:
                s.own_fc2[...] = total
            else:
                s.rb_out[distance, line] = total.astype(BF16)
        if distance == 0:
            sum_last.append(links.send(s.rb_out.at[0, 1], s.ry_last, ydev))
        else:
            sum_both[distance] = links.send(s.rb_out.at[distance], s.rb_in.at[distance], ring_next)

    def sum_b_end():
        sum_last[0].wait_recv()
        s.own_fc2[...] += s.ry_last[...].astype(F32)
        stores.append(loads.start(s.own_fc2, out_fc2))

    sums_done = [0, 1]

    def sum_a_until(steps):
        while sums_done[0] < min(steps, ring):
            sum_a_step(order[sums_done[0]])
            sums_done[0] += 1

    def sum_b_until(steps):
        while sums_done[1] < min(steps, ring):
            sum_b_step(order[sums_done[1]])
            sums_done[1] += 1

    def gather_wait(part):
        per = chunk_slots // 2
        gather_until((part + 1) * per - 1, 1)
        for distance in range(part * per, (part + 1) * per):
            for kind in range(2):
                for copy in gather_y[distance, kind]:
                    copy.wait_recv()

    part_out, part_in = s.part_out, s.part_in
    cross_out, cross_in = s.cross_out, s.cross_in
    part_sib, cross = {}, {}

    def hand_part(kind, place):
        total = (grad_two, result)[kind]
        part_out[kind, place] = total[(3, 1)[place]].astype(BF16)
        part_sib[kind, place] = links.send(part_out.at[kind, place], part_in.at[kind, place], sib)

    def hand_cross(kind):
        total = (grad_two, result)[kind]
        part_sib[kind, 0].wait_recv()
        cross_out[kind] = (total[2] + part_in[kind, 0].astype(F32)).astype(BF16)
        cross[kind] = links.send(cross_out.at[kind], cross_in.at[kind], xdev)

    gather_until(2, 1)
    gather_wait(0)
    n2_sib.wait_recv()
    cot_sib.wait_recv()
    no_bias = jnp.zeros((8, chunk), F32)
    bias_total = feed(0, (0, 1), no_bias)
    gather_until(ring - 1, 0)
    n2_x.wait_recv()
    n2_far = links.send(n2.at[2], n2.at[3], sib)
    gather_until(ring - 1, 1)
    cot_far.wait_recv()
    bias_total = feed(0, (2,), bias_total)
    n2_far.wait_recv()
    bias_total = feed(0, (3,), bias_total)
    early = links.arrivals
    feed_weights(0, bias_total)
    sum_b_step(1)
    for distance in range(1, chunk_slots // 2):
        sum_send_y(distance)
    feed_result(0)
    if chunks == 2:
        gather_wait(1)
        bias_total = feed(1, (3,), no_bias)
        hand_part(0, 0)
        bias_total = feed(1, (2,), bias_total)
    else:
        hand_part(0, 0)
    hand_cross(0)
    if chunks == 2:
        bias_total = feed(1, (0, 1), bias_total)
    hand_part(0, 1)
    sum_a_until(1)
    if chunks == 2:
        feed_weights(1, bias_total)
    for distance in range(chunk_slots // 2, ring):
        sum_send_y(distance)
    sum_send_y(0)
    sum_b_until(2)
    if chunks == 2:
        feed_result(1)
    hand_part(1, 0)
    hand_part(1, 1)
    hand_cross(1)
    for image in range(2):
        s.n1_t[:, image * seq : (image + 1) * seq] = n1[image].T
    sum_a_until(2)
    part_sib[0, 1].wait_recv()
    cross[0].wait_recv()
    grad_mid, grad_branch = stream, s.grad_branch

    def mid_back(step, totals):
        at = pl.ds(pl.multiple_of(step * block, block), block)
        grads = (
            grad_two[0, at, :] + part_in[0, 1, at, :].astype(F32) + cross_in[0, at, :].astype(F32)
        )
        unit_rows, scale = s.unit_two[at, :], s.scale_two[at, :]
        passed = cot_all[0, at, :].astype(F32)
        mid = passed + norm_back(grads, vecs[3:4, :], unit_rows, scale)
        grad_mid[at, :] = mid
        low = mid.astype(BF16)
        grad_branch[0, at, :] = low
        return (
            totals[0] + fold_rows(grads * unit_rows),
            totals[1] + fold_rows(grads),
            totals[2] + fold_rows(low.astype(F32)),
            totals[3] + fold_rows(passed),
        )

    empty = jnp.zeros((8, width), F32)
    gain_two_sum, shift_two_sum, out_bias_sum, fc2_bias_sum = lax.fori_loop(
        0, blocks, mid_back, (empty,) * 4, unroll=4
    )
    branch_back = links.send(grad_branch.at[0], grad_branch.at[1], sib)

    def mixed_back(image):
        grads = mm_nt(grad_branch[image], wout[...])
        for pair in range(pairs):
            s.grad_mixed[image, pair] = grads[:, pair * LANES : (pair + 1) * LANES].astype(BF16)

    grads_pair = s.grads_pair

    def attend_back(image, pair):
        queries, keys = s.q[image, pair], s.k[image, pair]
        values, grads = s.v[image, pair], s.grad_mixed[image, pair]
        keys_t = (keys * score_scale).T
        grad_values = jnp.zeros((seq, LANES), F32)
        grad_keys = jnp.zeros((seq, LANES), F32)
        grad_queries = []
        for half in range(2):
            probs = s.probs[image * 2 * pairs + pair * 2 + half]
            grads_half = grads * lane_half[half]
            grad_values += mm(probs.astype(BF16), grads_half)
            grad_probs = mm_nt(values, grads_half)
            inner = jnp.sum(grad_probs * probs, axis=0, keepdims=True)
            grad_scores = (probs * (grad_probs - inner)).astype(BF16)
            grad_keys += mm(grad_scores, queries * lane_scaled[half])
            grad_queries.append(
                mm(keys_t[half * HEAD_DIM : (half + 1) * HEAD_DIM], grad_scores)
            )
        grad_query = jnp.concatenate(grad_queries, axis=0).T
        for place, value in enumerate(
            (grad_query, grad_keys, grad_values)
        ):
            grads_pair[pair, image, :, place * LANES : (place + 1) * LANES] = value.astype(BF16)

    def rows_back(image):
        total = mm_nt(grads_pair[0, image], w_pair[0])
        for pair in range(1, pairs):
            total += mm_nt(grads_pair[pair, image], w_pair[pair])
        return total

    def weights_back(pair):
        both = grads_pair[pair].reshape(2 * seq, 3 * LANES)
        for base in range(0, width, 256):
            rows = slice(base, base + 256)
            ar[1 + pair, rows, :] = mm(s.n1_t[rows, :], both).astype(BF16)

    mixed_back(0)
    attend_back(0, 0)
    branch_back.wait_recv()
    mixed_back(1)

    ar = s.ar
    by_core = (one_dev, two_dev, p_one, p_two)
    cuts = [(array, lanes) for array in range(4) for lanes in (pl.ds(0, 256), pl.ds(256, local - 256))]
    flat = [
        (ar.at[array, :, lanes], s.ar_one.at[array, :, lanes], s.ar_two.at[array, :, lanes],
         s.ar_z.at[array, :, :, lanes], s.ar_rest.at[array, :, :, lanes], s.attn.at[array, :, lanes],
         width, by_core)
        for array, lanes in cuts
    ]
    small_half = seq // 2
    small = (s.small, s.small_one, s.small_two, s.small_z, s.small_rest,
             s.small_all, small_half, by_core)
    items = flat + [small]
    stages = [dict() for _ in range(7)]

    def piece(item):
        total_rows = items[item][6]
        _, _, p_one, p_two = items[item][7]
        half, quarter, leaf = total_rows // 2, total_rows // 4, total_rows // 16
        at_one = pl.multiple_of(p_one * half, half)
        at_two = pl.multiple_of(at_one + p_two * quarter, quarter)
        return half, quarter, leaf, at_one, at_two

    def reduce_one(item):
        data, one = items[item][0], items[item][1]
        half, _, _, _, _ = piece(item)
        device, _, p_one, _ = items[item][7]
        other = pl.ds(pl.multiple_of((1 - p_one) * half, half), half)
        stages[0][item] = [links.send(data.at[other], one, device, again=True)]

    def reduce_two(item):
        data, one, two = items[item][:3]
        half, quarter, _, at_one, _ = piece(item)
        stages[0][item][0].wait_recv()
        mine = pl.ds(at_one, half)
        data[mine] = (data[mine].astype(F32) + one[...].astype(F32)).astype(data.dtype)
        _, device, _, p_two = items[item][7]
        other = pl.ds(pl.multiple_of(at_one + (1 - p_two) * quarter, quarter), quarter)
        stages[1][item] = [links.send(data.at[other], two, device, again=True)]

    def reduce_z(item):
        data, _, two, by_z = items[item][:4]
        _, quarter, leaf, _, at_two = piece(item)
        stages[1][item][0].wait_recv()
        mine = pl.ds(at_two, quarter)
        data[mine] = (data[mine].astype(F32) + two[...].astype(F32)).astype(data.dtype)
        stages[2][item] = links.send_parts(
            [
                (
                    data.at[pl.ds(pl.multiple_of(at_two + ((zq + hop) % 4) * leaf, leaf), leaf)],
                    by_z.at[hop - 1],
                    zdev[hop],
                )
                for hop in range(1, 4)
            ],
            by_z,
        )

    def spread_z(item):
        data, _, _, by_z, by_rest, done = items[item][:6]
        _, _, leaf, _, at_two = piece(item)
        stages[2][item].wait_recv()
        mine = pl.ds(pl.multiple_of(at_two + zq * leaf, leaf), leaf)
        total = data[mine].astype(F32)
        for hop in range(3):
            total += by_z[hop].astype(F32)
        if rest_count > 1:
            by_rest[0] = total.astype(data.dtype)
            copies = [
                links.send(by_rest.at[0], by_rest.at[hop], rdev[hop])
                for hop in range(1, rest_count)
            ]
            for copy in copies:
                copy.wait_recv()
            total = jnp.zeros(total.shape, F32)
            for owner in range(rest_count):
                total += by_rest[(rest - owner + rest_count) % rest_count].astype(F32)
        done[mine] = total.astype(done.dtype)
        stages[3][item] = links.send_parts(
            [(done.at[mine], done.at[mine], zdev[hop]) for hop in range(1, 4)],
            done.at[pl.ds(0, 3 * leaf)],
        )

    def spread_two(item):
        done = items[item][5]
        _, quarter, _, _, at_two = piece(item)
        stages[3][item].wait_recv()
        mine = pl.ds(at_two, quarter)
        stages[4][item] = [links.send(done.at[mine], done.at[mine], items[item][7][1], again=True)]

    def spread_one(item):
        done = items[item][5]
        half, _, _, at_one, _ = piece(item)
        stages[4][item][0].wait_recv()
        mine = pl.ds(at_one, half)
        stages[5][item] = [links.send(done.at[mine], done.at[mine], items[item][7][0], again=True)]

    def finish(item):
        stages[5][item][0].wait_recv()
        if item < len(cuts):
            array, lanes = cuts[item]
            stores.append(loads.start(s.attn.at[array, :, lanes], out_attn.at[array, :, lanes]))

    for half in range(2):
        at = slice(half * local, (half + 1) * local)
        total = mm(s.mixed_t[0], grad_branch[0, :, at]) + mm(
            s.mixed_t[1], grad_branch[1, :, at]
        )
        ar[0, at, :] = total.astype(BF16)
    links.spare = list(range(early))
    def out_back():
        part_sib[1, 1].wait_recv()
        cross[1].wait_recv()

        @pl.loop(0, blocks, unroll=4)
        def _(step):
            at = pl.ds(pl.multiple_of(step * block, block), block)
            row_ids = lax.broadcasted_iota(jnp.int32, (block, 1), 0) + step * block
            total = result[0, at, :] + part_in[1, 1, at, :].astype(F32) + cross_in[1, at, :].astype(F32)
            rows = middle[at, :] + (total + vecs[5:6, :])
            s.own_rows[0, at, :] = jnp.where(row_ids < limit, rows, 0.0).astype(BF16)

        stores.append(loads.start(s.own_rows, out_rows))

    def pair_back(pair):
        if pair == 0:
            sum_b_until(3)
        attend_back(1, pair)
        if pair > 0:
            attend_back(0, pair)
        weights_back(pair)
        if pair == 1:
            sum_a_until(3)

    held = SimpleNamespace()

    def rows_hand():
        s.rows_out[...] = rows_back(1).astype(BF16)
        held.rows_sib = links.send(s.rows_out, s.rows_in, sib)

    def rows_keep():
        s.branch_own[...] = rows_back(0)

    def norm_one_back():
        held.rows_sib.wait_recv()

        def in_back(step, totals):
            at = pl.ds(pl.multiple_of(step * block, block), block)
            grads = (s.branch_own[at, :] + s.rows_in[at, :].astype(F32))
            unit_rows, scale = s.unit_one[at, :], s.scale_one[at, :]
            grad_mid[at, :] += norm_back(grads, vecs[0:1, :], unit_rows, scale)
            return (totals[0] + fold_rows(grads * unit_rows), totals[1] + fold_rows(grads))

        held.sums = lax.fori_loop(0, blocks, in_back, (empty,) * 2, unroll=4)

    theirs = pl.ds(pl.multiple_of((1 - h) * small_half, small_half), small_half)
    ours = pl.ds(pl.multiple_of(h * small_half, small_half), small_half)
    small_ref, small_own = s.small_full, s.small
    small_base = (width // small_ref.shape[1]) * prompt_pad + 6 * (width // small_ref.shape[1])

    def place_small():
        gain_one_sum, shift_one_sum = held.sums
        grad_in = grad_mid[...]
        high = grad_in.astype(BF16)
        low = (grad_in - high.astype(F32)).astype(BF16)
        placed = mm(pick[...], high) + mm(pick[...], low)
        s.own_tok[0] = placed[0:tok_rows]
        stores.append(loads.start(s.own_tok.at[0], out_tok.at[:, 0, :]))

        small_ref[...] = jnp.zeros(small_ref.shape, F32)
        part_width = small_ref.shape[1]
        parts = width // part_width
        for part in range(parts):
            small_ref[part * prompt_pad : part * prompt_pad + prompt_pad, :] = placed[
                tok_pad : tok_pad + prompt_pad, part * part_width : (part + 1) * part_width
            ]
        base = parts * prompt_pad
        sums = (gain_one_sum, shift_one_sum, out_bias_sum, gain_two_sum, shift_two_sum, fc2_bias_sum)
        for place, total in enumerate(sums):
            row = jnp.sum(total, axis=0, keepdims=True)
            for part in range(parts):
                at = base + place * parts + part
                small_ref[at : at + 1, :] = row[:, part * part_width : (part + 1) * part_width]
        base += len(sums) * parts
        for place in range(2):
            at = slice(2 * place * LANES, 2 * place * LANES + LANES)
            row = jnp.concatenate(
                [
                    jnp.sum(
                        grads_pair[pair, 0, :, at].astype(F32) + grads_pair[pair, 1, :, at].astype(F32),
                        axis=0,
                        keepdims=True,
                    )
                    for pair in range(pairs)
                ],
                axis=1,
            )
            for head in range(2):
                chosen = row * (h if head == 1 else 1 - h).astype(F32)
                at = base + head * 4 + place * 2
                small_ref[at : at + 1, :] = chosen[:, 0:part_width]
                small_ref[at + 1 : at + 2, 0 : local - part_width] = chosen[:, part_width:local]
        held.small_sib = links.send(small_ref.at[theirs], s.small_in.at[1], sib)
        sum_a_until(ring)
        sum_b_until(ring)

    def reduce_small():
        held.small_sib.wait_recv()
        small_own[...] = small_ref[ours] + s.small_in[1]

    final = s.small_out

    def hand_small():
        final[ours] = s.small_all[...]
        held.small_back = links.send(s.small_all, s.small_in.at[0], sib)

    blocks_beside = [
        functools.partial(pair_back, 0), functools.partial(pair_back, 1), functools.partial(pair_back, 2),
        rows_hand, rows_keep, norm_one_back, place_small, out_back,
    ]
    steps = [reduce_one, reduce_two, reduce_z, spread_z, spread_two, spread_one, finish]
    for item, stage in REDUCE_ORDER:
        if item < 0:
            blocks_beside[-1 - item]()
        else:
            if stage == 0 and item == len(cuts):
                reduce_small()
            steps[stage](item)
            if (item, stage) == LATE_SUM:
                sum_b_end()
            if (item, stage) == (len(cuts), len(steps) - 1):
                hand_small()
    held.small_back.wait_recv()
    final[theirs] = s.small_in[0]
    final[small_base + 8 : small_base + 12, :] = jnp.where(
        h == 0, final[small_base : small_base + 4, :], final[small_base + 4 : small_base + 8, :]
    )
    stores.append(loads.start(final, out_small))
    links.drain()
    for copy in stores:
        copy.wait()


def finish_kernel(dims, *refs):
    it = iter(refs)
    rows_in, tok_in, attn_in, small_in, fc1_in, fc2_in, bias_in = (next(it) for _ in range(7))
    (
        layer_out, grad_tokens, grad_prompts, gain_one, shift_one, w_query, b_query, w_key,
        w_value, b_value, w_out, b_out, gain_two, shift_two, w_fc1, b_fc1, w_fc2, b_fc2,
    ) = (next(it) for _ in range(18))
    s = SimpleNamespace(**dict(zip(dims.finish, it)))
    width, local = dims.width, dims.local
    rows = w_fc1.shape[0]
    loads = Loads(s.load_sems, dims.finish_depth)
    whole_shards = rows == fc1_in.shape[0]
    passing = [(tok_in, s.tok, grad_tokens), (rows_in, s.rows, layer_out)]
    if whole_shards:
        passing += [(fc1_in, s.fc1, w_fc1), (fc2_in, s.fc2, w_fc2)]
    passing = [(loads.start(source, held), held, target) for source, held, target in passing]
    load_attn = [loads.start(attn_in.at[array], s.attn.at[array]) for array in (1, 2, 3, 0)]
    load_small = loads.start(small_in, s.small)
    load_bias = loads.start(bias_in, s.bias)
    stores = []
    for load, held, target in passing:
        load.wait()
        stores.append(loads.start(held, target))
    for pair in range(3):
        load_attn[pair].wait()
        at = slice(pair * LANES, (pair + 1) * LANES)
        for place, target in enumerate((w_query, w_key, w_value)):
            s.tall[place, :, at] = s.attn[1 + pair, :, place * LANES : (place + 1) * LANES].astype(F32)
            stores.append(loads.start(s.tall.at[place, :, pl.ds(pair * LANES, LANES)], target.at[:, pl.ds(pair * LANES, LANES)]))
    load_attn[3].wait()
    s.wide[:, 0:local] = s.attn[0, 0:local].astype(F32)
    s.wide[:, local : 2 * local] = s.attn[0, local : 2 * local].astype(F32)
    stores.append(loads.start(s.wide, w_out))
    load_small.wait()
    load_bias.wait()
    part_width = s.small.shape[1]
    parts = width // part_width
    for part in range(parts):
        at = slice(part * part_width, (part + 1) * part_width)
        s.prompts[:, at] = s.small[part * dims.prompt_pad : part * dims.prompt_pad + dims.prompt_rows]
    stores.append(loads.start(s.prompts, grad_prompts))
    base = parts * dims.prompt_pad
    for place, target in enumerate((gain_one, shift_one, b_out, gain_two, shift_two, b_fc2)):
        for part in range(parts):
            at = base + place * parts + part
            s.row[place : place + 1, part * part_width : (part + 1) * part_width] = s.small[at : at + 1]
        s.flat[place, :] = s.row[place : place + 1, :].reshape(width)
        stores.append(loads.start(s.flat.at[place], target))
    base += 6 * parts + 8
    for place, target in enumerate((b_query, b_value)):
        at = base + 2 * place
        s.row[6:7, 0:part_width] = s.small[at : at + 1]
        s.row[6:7, part_width : 2 * part_width] = s.small[at + 1 : at + 2]
        s.half_flat[place, :] = s.row[6:7, 0:local].reshape(local)
        stores.append(loads.start(s.half_flat.at[place], target))
    b_fc1[...] = s.bias[0:1, 0:rows].reshape(rows)
    if not whole_shards:
        for source, held, target in ((fc1_in, s.fc1, w_fc1), (fc2_in, s.fc2, w_fc2)):
            loads.start(source, held).wait()
            s.cut[...] = held[0:rows]
            loads.start(s.cut, target).wait()
    for copy in stores:
        copy.wait()


def layer(dims, operands):
    seq, width, local = dims.seq, dims.width, dims.local
    n, ring, slots, rows_per = dims.n, dims.ring, dims.slots, dims.rows_per
    pairs = local // LANES
    chunk = dims.chunk_slots * rows_per
    rest_count = n // 16
    small_half = seq // 2
    part_width = 256
    arrivals = 11 * ring + 68 + 9 * (rest_count - 1) - min(36, 6 * ring + 6)
    vmem = pltpu.VMEM
    shared = 2 * rows_per
    scratch = dict(
        send_sems=pltpu.SemaphoreType.DMA((dims.send_depth,)),
        recv_sems=pltpu.SemaphoreType.DMA((arrivals,)),
        w_all=vmem((slots, shared, width), BF16),
        b_all=vmem((slots, 8, LANES), F32),
        cot_all=vmem((4, seq, width), BF16),
        meta=vmem((2, 8, LANES), jnp.int32),
        load_sems=pltpu.SemaphoreType.DMA((dims.load_depth,)),
        kept=vmem((1, dims.patches), jnp.int32),
        tokens=vmem((1, dims.tok_rows, width), BF16),
        prompts=vmem((dims.prompt_rows, width), BF16),
        gain_one=vmem((width,), BF16),
        shift_one=vmem((width,), BF16),
        b_query=vmem((local,), BF16),
        b_value=vmem((local,), BF16),
        b_out=vmem((width,), BF16),
        gain_two=vmem((width,), BF16),
        shift_two=vmem((width,), BF16),
        b_fc1=vmem((dims.rows,), BF16),
        b_fc2=vmem((width,), BF16),
        vecs=vmem((8, width), F32),
        w_pair=vmem((pairs, width, 3 * LANES), BF16),
        wout=vmem((local, width), BF16),
        unit_one=vmem((seq, width), F32),
        unit_two=vmem((seq, width), F32),
        scale_one=vmem((seq, 1), F32),
        scale_two=vmem((seq, 1), F32),
        own_rows=vmem((1, seq, width), BF16),
        own_tok=vmem((1, dims.tok_rows, width), F32),
        own_fc1=vmem((rows_per, width), F32),
        own_fc2=vmem((rows_per, width), F32),
        own_bias=vmem((8, LANES), F32),
        attn=vmem((4, width, local), BF16),
        src=vmem((dims.tok_pad + dims.prompt_pad, width), BF16),
        pick=vmem((dims.tok_pad + dims.prompt_pad, seq), BF16),
        idx=vmem((8, seq), jnp.int32),
        stream=vmem((seq, width), F32),
        middle=vmem((seq, width), F32),
        n1=vmem((2, seq, width), BF16),
        n2=vmem((4, seq, width), BF16),
        q=vmem((2, pairs, seq, LANES), BF16),
        k=vmem((2, pairs, seq, LANES), BF16),
        v=vmem((2, pairs, seq, LANES), BF16),
        probs=vmem((4 * pairs, seq, seq), F32),
        mixed_t=vmem((2, local, seq), BF16),
        branch_out=vmem((seq, width), F32),
        branch_in=vmem((seq, width), F32),
        branch_own=vmem((seq, width), F32),
        hidden=vmem((slots // dims.chunk_slots, 4, seq, chunk), BF16),
        grad_before=vmem((4, seq, chunk), BF16),
        result=vmem((4, seq, width), F32),
        grad_two=vmem((4, seq, width), F32),
        part_out=vmem((2, 2, seq, width), BF16),
        part_in=vmem((2, 2, seq, width), BF16),
        cross_out=vmem((2, seq, width), BF16),
        cross_in=vmem((2, seq, width), BF16),
        g_all=vmem((slots, shared, width), BF16),
        gb_all=vmem((slots, 8, LANES), F32),
        ry=vmem((ring, rows_per, width), BF16),
        ry_last=vmem((rows_per, width), BF16),
        rb_out=vmem((ring, 2, rows_per, width), BF16),
        rb_in=vmem((ring, 2, rows_per, width), BF16),
        n1_t=vmem((width, 2 * seq), BF16),
        ryb=vmem((ring, 8, LANES), F32),
        rz_out=vmem((ring, rows_per, width), BF16),
        rzb_out=vmem((ring, 8, LANES), F32),
        rz_in=vmem((ring, rows_per, width), BF16),
        rzb_in=vmem((ring, 8, LANES), F32),
        grad_branch=vmem((2, seq, width), BF16),
        grad_mixed=vmem((2, pairs, seq, LANES), BF16),
        grads_pair=vmem((pairs, 2, seq, 3 * LANES), BF16),
        rows_out=vmem((seq, width), BF16),
        rows_in=vmem((seq, width), BF16),
        ar=vmem((4, width, local), BF16),
        ar_one=vmem((4, width // 2, local), BF16),
        ar_two=vmem((4, width // 4, local), BF16),
        ar_z=vmem((4, 3, width // 16, local), BF16),
        ar_rest=vmem((4, rest_count, width // 16, local), BF16),
        small_full=vmem((seq, part_width), F32),
        small_out=vmem((seq, part_width), F32),
        small_in=vmem((2, small_half, part_width), F32),
        small=vmem((small_half, part_width), F32),
        small_one=vmem((small_half // 2, part_width), F32),
        small_two=vmem((small_half // 4, part_width), F32),
        small_z=vmem((3, small_half // 16, part_width), F32),
        small_rest=vmem((rest_count, small_half // 16, part_width), F32),
        small_all=vmem((small_half, part_width), F32),
    )
    dims = SimpleNamespace(**vars(dims), scratch=tuple(scratch))
    anywhere = pl.BlockSpec(memory_space=pl.ANY)
    shape = jax.ShapeDtypeStruct
    return pl.pallas_call(
        functools.partial(layer_kernel, dims),
        out_shape=(
            shape((1, seq, width), BF16),
            shape((dims.tok_rows, 1, width), F32),
            shape((4, width, local), BF16),
            shape((seq, part_width), F32),
            shape((rows_per, width), F32),
            shape((rows_per, width), F32),
            shape((8, LANES), F32),
        ),
        in_specs=[pl.BlockSpec(memory_space=pltpu.SMEM)] + [anywhere] * (len(operands) - 1),
        out_specs=[anywhere] * 7,
        scratch_shapes=list(scratch.values()),
        compiler_params=pltpu.CompilerParams(
            collective_id=0, has_side_effects=True, vmem_limit_bytes=63 * 2**20
        ),
    )(*operands)


def finish(dims, results):
    seq, width, local, rows = dims.seq, dims.width, dims.local, dims.rows
    vmem = pltpu.VMEM
    scratch = dict(
        load_sems=pltpu.SemaphoreType.DMA((dims.finish_depth,)),
        attn=vmem((4, width, local), BF16),
        wide=vmem((local, width), F32),
        tall=vmem((3, width, local), F32),
        small=vmem(results[3].shape, F32),
        bias=vmem((8, LANES), F32),
        prompts=vmem((dims.prompt_rows, width), F32),
        row=vmem((8, width), F32),
        flat=vmem((6, width), F32),
        half_flat=vmem((2, local), F32),
        rows=vmem((1, seq, width), BF16),
        tok=vmem((dims.tok_rows, 1, width), F32),
        fc1=vmem((dims.rows_per, width), F32),
        fc2=vmem((dims.rows_per, width), F32),
        cut=vmem((rows, width), F32),
    )
    dims = SimpleNamespace(**vars(dims), finish=tuple(scratch))
    anywhere = pl.BlockSpec(memory_space=pl.ANY)
    whole = pl.BlockSpec(memory_space=pltpu.VMEM)

    def out(*sizes, dtype=F32):
        return jax.ShapeDtypeStruct(sizes, dtype)

    shapes = (
        out(1, seq, width, dtype=BF16), out(dims.tok_rows, 1, width), out(dims.prompt_rows, width),
        out(width), out(width), out(width, local), out(local), out(width, local),
        out(width, local), out(local), out(local, width), out(width), out(width), out(width),
        out(rows, width), out(rows), out(rows, width), out(width),
    )
    return pl.pallas_call(
        functools.partial(finish_kernel, dims),
        out_shape=shapes,
        in_specs=[anywhere] * 7,
        out_specs=[whole if place == 15 else anywhere for place in range(len(shapes))],
        scratch_shapes=list(scratch.values()),
        compiler_params=pltpu.CompilerParams(vmem_limit_bytes=60 * 2**20),
    )(*results)


def body(n, *arguments):
    (
        tokens, kept_index, kept_count, prompts, gain_one, shift_one, w_query, b_query, w_key,
        w_value, b_value, w_out, b_out, gain_two, shift_two, w_fc1, b_fc1, w_fc2, b_fc2, cotangent,
    ) = arguments
    seq, width = cotangent.shape[1:]
    local = w_query.shape[1]
    rows = w_fc1.shape[0]
    rows_per = round_up(rows, 16)
    ring = n // 4
    slots = 2 * ring
    halves = slots // 2
    chunk_slots = halves if (halves % 2 == 0 and halves * rows_per % LANES == 0) else slots
    tok_rows, prompt_rows = tokens.shape[1], prompts.shape[0]
    dims = SimpleNamespace(
        n=n, ring=ring, slots=slots, chunk_slots=chunk_slots, rows_per=rows_per, rows=rows, seq=seq,
        width=width, local=local, tok_rows=tok_rows, tok_pad=round_up(tok_rows, 16),
        prompt_rows=prompt_rows, prompt_pad=round_up(prompt_rows, 16),
        patches=kept_index.shape[1], send_depth=32, load_depth=17, finish_depth=32,
    )
    if rows_per != rows:
        spare = ((0, rows_per - rows), (0, 0))
        w_fc1, w_fc2 = jnp.pad(w_fc1, spare), jnp.pad(w_fc2, spare)
    operands = (
        kept_count, tokens, kept_index, prompts, w_fc1, w_fc2, cotangent, w_query, w_key, w_value,
        w_out, gain_one, shift_one, b_query, b_value, b_out, gain_two, shift_two, b_fc1, b_fc2,
    )
    outs = list(finish(dims, layer(dims, operands)))
    outs[1] = outs[1].transpose(1, 0, 2)
    return tuple(outs)


def solution(mesh):
    batch, head = mesh.axis_names
    both = (batch, head)
    placed = (
        P(both, None, None), P(both, None), P(both), P(), P(), P(), P(None, head), P(head),
        P(None, head), P(None, head), P(head), P(head, None), P(), P(), P(),
        P(both, None), P(both), P(both, None), P(), P(both, None, None),
    )
    return jax.shard_map(
        functools.partial(body, mesh.shape[batch]),
        mesh=mesh,
        in_specs=placed,
        out_specs=(
            P(both, None, None), P(both, None, None), P(), P(), P(), P(None, head), P(head),
            P(None, head), P(None, head), P(head), P(head, None), P(), P(), P(),
            P(both, None), P(both), P(both, None), P(),
        ),
        check_vma=False,
    )
```

```python
import functools
from types import SimpleNamespace

import jax
import jax.numpy as jnp
from jax import lax
from jax.experimental import pallas as pl
from jax.experimental.pallas import tpu as pltpu
from jax.sharding import PartitionSpec as P

MESH = pl.DeviceIdType.MESH
HEAD_DIM = 64
EPSILON = 1e-06
LANES = 128
BF16 = jnp.bfloat16
F32 = jnp.float32


def round_up(value, step):
    return -(-value // step) * step


def mm(left, right):
    return lax.dot_general(left, right, (((1,), (0,)), ((), ())), preferred_element_type=F32)


def mm_nt(left, right):
    return lax.dot_general(left, right, (((1,), (1,)), ((), ())), preferred_element_type=F32)


def mm_tn(left, right):
    return lax.dot_general(left, right, (((0,), (0,)), ((), ())), preferred_element_type=F32)


def fold_rows(rows):
    count, width = rows.shape
    return jnp.sum(rows.reshape(count // 8, 8, width), axis=0)


def normalise(rows):
    width = rows.shape[1]
    centre = jnp.sum(rows, axis=1, keepdims=True) * (1.0 / width)
    centred = rows - centre
    spread = jnp.sum(centred * centred, axis=1, keepdims=True) * (1.0 / width)
    scale = lax.rsqrt(spread + EPSILON)
    return centred * scale, scale


def norm_back(grad_rows, gain_row, unit_rows, scale):
    width = grad_rows.shape[1]
    scaled = grad_rows * gain_row
    mean_one = jnp.sum(scaled, axis=1, keepdims=True) * (1.0 / width)
    mean_two = jnp.sum(scaled * unit_rows, axis=1, keepdims=True) * (1.0 / width)
    return scale * (scaled - mean_one - unit_rows * mean_two)


GELU_A = 0.7978845608028654
GELU_B = 0.044715


def gelu_both(value):
    square = value * value
    bend = jnp.tanh(value * (GELU_A + (GELU_A * GELU_B) * square))
    half = 0.5 + 0.5 * bend
    slope = half + (0.5 * value) * (1.0 - bend * bend) * (
        GELU_A + (3.0 * GELU_A * GELU_B) * square
    )
    return value * half, slope


VECTORS = (
    "gain_one", "shift_one", "b_query", "b_value", "b_out", "gain_two", "shift_two", "b_fc1", "b_fc2",
)


LATE_SUM = (8, 3)
REDUCE_ORDER = (
    (0, 0), (-1, 0), (3, 0), (-2, 0), (5, 0), (1, 0), (-3, 0), (4, 0), (7, 0), (3, 1), (0, 1),
    (5, 1), (2, 0), (1, 1), (3, 2), (0, 2), (4, 1), (5, 2), (1, 2), (3, 3), (-4, 0), (7, 1),
    (6, 0), (0, 3), (1, 3), (7, 2), (4, 2), (2, 1), (3, 4), (-5, 0), (1, 4), (5, 3), (0, 4),
    (6, 1), (-6, 0), (7, 3), (2, 2), (-7, 0), (4, 3), (8, 0), (3, 5), (1, 5), (5, 4), (7, 4),
    (6, 2), (-8, 0), (8, 1), (2, 3), (0, 5), (6, 3), (5, 5), (4, 4), (8, 2), (2, 4), (7, 5),
    (8, 3), (6, 4), (3, 6), (4, 5), (2, 5), (8, 4), (7, 6), (5, 6), (6, 5), (8, 5), (0, 6), (4, 6),
    (8, 6), (6, 6), (1, 6), (2, 6),
)


class Once:
    def __init__(self, wait):
        self.pending = wait

    def wait(self):
        if self.pending is not None:
            self.pending()
            self.pending = None


class Loads:
    def __init__(self, sems, depth):
        self.sems = sems
        self.depth = depth
        self.copies = []

    def take(self):
        place = len(self.copies)
        if place >= self.depth:
            self.copies[place - self.depth].wait()
        return self.sems.at[place % self.depth]

    def start(self, source, target):
        copy = pltpu.make_async_copy(source, target, self.take())
        copy.start()
        self.copies.append(Once(copy.wait))
        return self.copies[-1]

    def start_parts(self, pieces, whole):
        sem = self.take()
        for source, target in pieces:
            pltpu.make_async_copy(source, target, sem).start()
        self.copies.append(Once(pltpu.make_async_copy(whole, whole, sem).wait))
        return self.copies[-1]


class Links:
    def __init__(self, send_sems, recv_sems, depth):
        self.send_sems = send_sems
        self.recv_sems = recv_sems
        self.depth = depth
        self.sends = []
        self.arrivals = 0
        self.spare = []
        self.clock = 0
        self.heard = 0
        self.group_spare = []

    def copy(self, source, target, device, arrival):
        place = len(self.sends)
        if place >= self.depth:
            self.sends[place - self.depth].wait()
        copy = pltpu.make_async_remote_copy(
            src_ref=source,
            dst_ref=target,
            send_sem=self.send_sems.at[place % self.depth],
            recv_sem=self.recv_sems.at[arrival],
            device_id=device,
            device_id_type=MESH,
        )
        copy.start()
        self.sends.append(Once(copy.wait_send))
        return copy

    def send(self, source, target, device, again=False):
        if again and self.spare:
            return self.copy(source, target, device, self.spare.pop(0))
        copy = self.copy(source, target, device, self.arrivals)
        self.arrivals += 1
        return copy

    def send_parts(self, pieces, whole):
        self.clock += 1
        sent = self.clock
        ready = [entry for entry in self.group_spare if entry[0] < self.heard]
        if ready:
            self.group_spare.remove(ready[0])
            arrival = ready[0][1]
        else:
            arrival = self.arrivals
            self.arrivals += 1
        for source, target, device in pieces:
            self.copy(source, target, device, arrival)
        wait = pltpu.make_async_remote_copy(
            src_ref=whole,
            dst_ref=whole,
            send_sem=self.send_sems.at[0],
            recv_sem=self.recv_sems.at[arrival],
            device_id=device,
            device_id_type=MESH,
        ).wait_recv

        def heard():
            wait()
            self.clock += 1
            self.heard = max(self.heard, sent)
            self.group_spare.append((self.clock, arrival))

        return SimpleNamespace(wait_recv=heard)

    def drain(self):
        for copy in self.sends:
            copy.wait()


def layer_kernel(dims, *refs):
    it = iter(refs)
    count_ref = next(it)
    tokens, kept, prompts, fc1, fc2, cot = (next(it) for _ in range(6))
    weights_in = [next(it) for _ in range(4)]
    vectors_in = [next(it) for _ in range(9)]
    out_rows, out_tok, out_attn, out_small, out_fc1, out_fc2, out_bias = (
        next(it) for _ in range(7)
    )
    s = SimpleNamespace(**dict(zip(dims.scratch, it)))
    w_pair, wout = s.w_pair, s.wout
    vecs = s.vecs
    seq, width, local = dims.seq, dims.width, dims.local
    pairs = local // LANES
    rows_per = dims.rows_per
    n, ring, slots = dims.n, dims.ring, dims.slots
    chunk_slots = dims.chunk_slots
    chunk = chunk_slots * rows_per
    chunks = slots // chunk_slots
    tok_rows, tok_pad, prompt_pad = dims.tok_rows, dims.tok_pad, dims.prompt_pad
    prompt_rows, patches = dims.prompt_rows, dims.patches
    rest_count = n // 16
    score_scale = HEAD_DIM**-0.5
    block = 32
    blocks = seq // block

    b = lax.axis_index("batch")
    h = lax.axis_index("head")
    bx = b % 2
    by = (b // 2) % 2
    zz = b // 4
    sib = (b, 1 - h)
    xdev = (b + 1 - 2 * bx, h)
    ydev = (b + 2 - 4 * by, h)
    corner = b % 4
    ring_next = (((zz + 1) % ring) * 4 + corner, h)
    ring_prev = (((zz + ring - 1) % ring) * 4 + corner, h)
    zq = zz % 4
    zdev = [((zz - zq + (zq + hop) % 4) * 4 + corner, h) for hop in range(4)]
    rest = b // 16
    rdev = [(((rest + hop) % rest_count) * 16 + b % 16, h) for hop in range(rest_count)]
    one_dev = (xdev[0] * (1 - h) + ydev[0] * h, h)
    two_dev = (ydev[0] * (1 - h) + xdev[0] * h, h)
    p_one = bx * (1 - h) + by * h
    p_two = by * (1 - h) + bx * h

    partners = [sib, xdev, ydev] + zdev[1:]
    if ring > 4:
        partners += [ring_next, ring_prev] + rdev[1:]
    barrier = pltpu.get_barrier_semaphore()
    for partner in partners:
        pl.semaphore_signal(barrier, inc=1, device_id=partner, device_id_type=MESH)

    links = Links(s.send_sems, s.recv_sems, dims.send_depth)

    w_all, b_all, cot_all = s.w_all, s.b_all, s.cot_all
    loads = Loads(s.load_sems, dims.load_depth)
    load_kept = loads.start(kept, s.kept)
    load_fc = [
        loads.start(fc1, w_all.at[0, pl.ds(0, rows_per)]),
        loads.start(fc2, w_all.at[0, pl.ds(rows_per, rows_per)]),
    ]
    load_cot = loads.start(cot.at[0], cot_all.at[0])
    load_rows = [loads.start(tokens, s.tokens), loads.start(prompts, s.prompts)]
    load_vectors = [loads.start(ref, getattr(s, name)) for ref, name in zip(vectors_in, VECTORS)]
    load_weights = [
        loads.start(weights_in[3], wout),
        loads.start_parts(
            [
                (
                    weights_in[place].at[:, pl.ds(pair * LANES, LANES)],
                    w_pair.at[pair, :, pl.ds(place * LANES, LANES)],
                )
                for pair in range(pairs)
                for place in range(3)
            ],
            w_pair,
        ),
    ]

    limit = count_ref[0] + (1 + prompt_rows)
    src, pick = s.src, s.pick
    s.meta[0] = jnp.broadcast_to(limit, (8, LANES))
    s.idx[...] = jnp.zeros((8, seq), jnp.int32)
    src[tok_rows - tok_rows % 16 : tok_pad] = jnp.zeros((tok_pad - tok_rows + tok_rows % 16, width), BF16)
    src[tok_pad:] = jnp.zeros((prompt_pad, width), BF16)
    vecs[...] = jnp.zeros(vecs.shape, F32)
    load_kept.wait()
    s.idx[0:1, 0:patches] = s.kept[...]
    shifted = pltpu.roll(s.idx[...], 1 + prompt_rows, axis=1)[0:1, :]
    spot = lax.broadcasted_iota(jnp.int32, (1, seq), 1)
    wanted = jnp.where(
        spot < 1 + prompt_rows,
        jnp.where(spot == 0, 0, tok_pad - 1 + spot),
        jnp.where(spot < limit, shifted + 1, -1),
    )
    pick[...] = jnp.where(
        lax.broadcasted_iota(jnp.int32, pick.shape, 0) == wanted, 1.0, 0.0
    ).astype(BF16)
    for copy in load_vectors:
        copy.wait()
    for place, name in enumerate(("gain_one", "shift_one", "b_out", "gain_two", "shift_two", "b_fc2")):
        vecs[place : place + 1, :] = getattr(s, name)[...].astype(F32).reshape(1, width)
    vecs[6:7, 0:local] = s.b_query[...].astype(F32).reshape(1, local)
    vecs[6:7, local : 2 * local] = s.b_value[...].astype(F32).reshape(1, local)
    bias_rows = s.b_fc1.shape[0]
    vecs[7:8, 0:bias_rows] = s.b_fc1[...].astype(F32).reshape(1, bias_rows)
    b_all[0] = jnp.broadcast_to(vecs[7:8, 0:LANES], (8, LANES))
    load_cot.wait()

    @pl.loop(0, blocks, unroll=4)
    def _(step):
        at = pl.ds(pl.multiple_of(step * block, block), block)
        row_ids = lax.broadcasted_iota(jnp.int32, (block, 1), 0) + step * block
        rows = cot_all[0, at, :].astype(F32)
        cot_all[0, at, :] = jnp.where(row_ids < limit, rows, 0.0).astype(BF16)

    for copy in load_rows:
        copy.wait()
    src[0:tok_rows, :] = s.tokens[0]
    src[tok_pad : tok_pad + prompt_rows, :] = s.prompts[...]
    stream = s.stream
    stream[...] = mm_tn(pick[...], src[...])

    n1 = s.n1

    @pl.loop(0, blocks, unroll=4)
    def _(step):
        at = pl.ds(pl.multiple_of(step * block, block), block)
        unit_rows, s.scale_one[at, :] = normalise(stream[at, :])
        s.unit_one[at, :] = unit_rows
        n1[0, at, :] = (unit_rows * vecs[0:1, :] + vecs[1:2, :]).astype(BF16)

    for copy in load_fc:
        copy.wait()
    pl.semaphore_wait(barrier, len(partners))

    gather_ring, gather_y = {}, {}

    def gather_step(distance, kind):
        if distance > 0:
            for copy in gather_ring[distance, kind]:
                copy.wait_recv()
        rows = pl.ds(kind * rows_per, rows_per)
        mine = 2 * distance

        def hand_on(slot, device):
            copies = [links.send(w_all.at[mine, rows], w_all.at[slot, rows], device)]
            if kind == 0:
                copies.append(links.send(b_all.at[mine], b_all.at[slot], device))
            return copies

        if distance + 1 < ring:
            gather_ring[distance + 1, kind] = hand_on(mine + 2, ring_next)
        gather_y[distance, kind] = hand_on(mine + 1, ydev)

    gather_done = [0]

    def gather_until(distance, kind):
        while gather_done[0] <= min(2 * distance + kind, 2 * ring - 1):
            gather_step(gather_done[0] // 2, gather_done[0] % 2)
            gather_done[0] += 1

    n1_sib = links.send(n1.at[0], n1.at[1], sib)
    gather_until(0, 1)
    cot_x = links.send(cot_all.at[0], cot_all.at[2], xdev)
    cot_sib = links.send(cot_all.at[0], cot_all.at[1], sib)
    meta_sib = links.send(s.meta.at[0], s.meta.at[1], sib)


    def project(image):
        rows = n1[image]
        for pair in range(pairs):
            found = mm(rows, w_pair[pair])
            at = slice(pair * LANES, (pair + 1) * LANES)
            s.q[image, pair] = (found[:, 0:LANES] + vecs[6:7, at]).astype(BF16)
            s.k[image, pair] = found[:, LANES : 2 * LANES].astype(BF16)
            at = slice(local + pair * LANES, local + (pair + 1) * LANES)
            s.v[image, pair] = (found[:, 2 * LANES :] + vecs[6:7, at]).astype(BF16)

    lane_ids = lax.broadcasted_iota(jnp.int32, (1, LANES), 1)
    lane_half = [
        jnp.where(lane_ids // HEAD_DIM == half, 1.0, 0.0).astype(BF16) for half in range(2)
    ]
    lane_scaled = [
        jnp.where(lane_ids // HEAD_DIM == half, score_scale, 0.0).astype(BF16) for half in range(2)
    ]
    lane_spare = [
        jnp.where(lane_ids == (1 - half) * HEAD_DIM, 1.0, 0.0).astype(BF16) for half in range(2)
    ]
    key_ids = lax.broadcasted_iota(jnp.int32, (seq, 1), 0)

    def attend(image, first, last):
        key_bias = jnp.where(key_ids < s.meta[image, 0:1, 0:1], 0.0, -1e30).astype(BF16)

        for pair in range(first, last):
            queries, keys = s.q[image, pair], s.k[image, pair]
            values_t = s.v[image, pair].T
            for half in range(2):
                scores = mm_nt(
                    keys * lane_half[half] + key_bias * lane_spare[half],
                    queries * lane_scaled[half] + lane_spare[half],
                )
                weights = jnp.exp(scores - jnp.max(scores, axis=0, keepdims=True))
                probs = weights * (1.0 / jnp.sum(weights, axis=0, keepdims=True))
                s.probs[image * 2 * pairs + pair * 2 + half] = probs
                mixed_t = mm(values_t[half * HEAD_DIM : (half + 1) * HEAD_DIM], probs.astype(BF16))
                at = pl.ds(pair * LANES + half * HEAD_DIM, HEAD_DIM)
                s.mixed_t[image, at, :] = mixed_t.astype(BF16)

    for copy in load_weights:
        copy.wait()
    project(0)
    n1_sib.wait_recv()
    meta_sib.wait_recv()
    project(1)
    attend(1, 0, pairs)
    s.branch_out[...] = mm_tn(s.mixed_t[1], wout[...])
    branch_sib = links.send(s.branch_out, s.branch_in, sib)
    gather_until(1, 0)
    attend(0, 0, pairs)
    gather_until(1, 1)
    s.branch_own[...] = mm_tn(s.mixed_t[0], wout[...])
    branch_sib.wait_recv()
    middle, n2 = s.middle, s.n2

    @pl.loop(0, blocks, unroll=4)
    def _(step):
        at = pl.ds(pl.multiple_of(step * block, block), block)
        rows = stream[at, :] + (s.branch_own[at, :] + s.branch_in[at, :] + vecs[2:3, :])
        middle[at, :] = rows
        unit_rows, s.scale_two[at, :] = normalise(rows)
        s.unit_two[at, :] = unit_rows
        n2[0, at, :] = (unit_rows * vecs[3:4, :] + vecs[4:5, :]).astype(BF16)

    n2_x = links.send(n2.at[0], n2.at[2], xdev)
    n2_sib = links.send(n2.at[0], n2.at[1], sib)
    gather_until(2, 0)
    cot_x.wait_recv()
    cot_far = links.send(cot_all.at[2], cot_all.at[3], sib)
    hidden_all, before_all = s.hidden, s.grad_before
    result, grad_two = s.result, s.grad_two
    unpack = jnp.where(
        lax.broadcasted_iota(jnp.int32, (LANES, chunk), 1) % rows_per
        == lax.broadcasted_iota(jnp.int32, (LANES, chunk), 0),
        1.0,
        0.0,
    )
    owner_of = (
        lax.broadcasted_iota(jnp.int32, (chunk_slots, chunk), 1) // rows_per
        == lax.broadcasted_iota(jnp.int32, (chunk_slots, chunk), 0)
    )

    def feed_spans(part):
        span = slice(part * chunk_slots, (part + 1) * chunk_slots)
        return (
            w_all[span, 0:rows_per].reshape(chunk, width),
            w_all[span, rows_per : 2 * rows_per].reshape(chunk, width),
        )

    def feed(part, images, totals):
        span = slice(part * chunk_slots, (part + 1) * chunk_slots)
        tiles = b_all[span, 0, :].astype(BF16)
        bias_row = jnp.sum(
            jnp.where(owner_of, mm(tiles, unpack.astype(BF16)), 0.0), axis=0, keepdims=True
        )
        up, down = feed_spans(part)
        for image in images:
            before = mm_nt(n2[image], up) + bias_row
            hidden, slope = gelu_both(before)
            hidden_all[part, image] = hidden.astype(BF16)
            grad_before = (mm_nt(cot_all[image], down) * slope).astype(BF16)
            before_all[image] = grad_before
            if part == 0:
                grad_two[image] = mm(grad_before, up)
            else:
                grad_two[image] += mm(grad_before, up)
            totals += fold_rows(grad_before.astype(F32))
        return totals

    def feed_result(part):
        @pl.loop(0, 4)
        def _(image):
            _, down = feed_spans(part)
            if part == 0:
                result[image] = mm(hidden_all[part, image], down)
            else:
                result[image] += mm(hidden_all[part, image], down)

    g_all, gb_all = s.g_all, s.gb_all

    def feed_weights(part, bias_total):
        first = part * chunk_slots
        span = slice(first, first + chunk_slots)

        for left, right, base in ((before_all, n2, 0), (hidden_all.at[part], cot_all, rows_per)):
            total = jnp.zeros((chunk, width), F32)
            for image in range(4):
                total += mm_tn(left[image], right[image])
            g_all[span, base : base + rows_per] = (
                total.astype(BF16).reshape(chunk_slots, rows_per, width)
            )
        bias_row = jnp.sum(bias_total, axis=0, keepdims=True)
        spread = jnp.where(owner_of, jnp.broadcast_to(bias_row, owner_of.shape), 0.0)
        high = spread.astype(BF16)
        low = (spread - high.astype(F32)).astype(BF16)
        packed = mm_nt(high, unpack.astype(BF16)) + mm_nt(low, unpack.astype(BF16))
        for slot in range(chunk_slots):
            gb_all[first + slot] = jnp.broadcast_to(packed[slot : slot + 1], (8, LANES))

    order = list(range(1, ring)) + [0]
    stores = []
    sum_y, sum_ring, sum_both, sum_last = {}, {}, {}, []
    first_rows, second_rows = pl.ds(0, rows_per), pl.ds(rows_per, rows_per)

    def sum_send_y(distance):
        slot = 2 * distance + 1
        sum_y[distance] = [
            links.send(g_all.at[slot, first_rows], s.ry.at[distance], ydev),
            links.send(gb_all.at[slot], s.ryb.at[distance], ydev),
        ]

    def sum_a_step(distance):
        for copy in sum_y[distance]:
            copy.wait_recv()
        mine = 2 * distance
        total = g_all[mine, 0:rows_per].astype(F32) + s.ry[distance].astype(F32)
        bias = gb_all[mine] + s.ryb[distance]
        if distance != 1:
            before = (distance + ring - 1) % ring
            for copy in sum_ring[before]:
                copy.wait_recv()
            total += s.rz_in[before].astype(F32)
            bias += s.rzb_in[before]
        if distance == 0:
            s.own_fc1[...] = total
            s.own_bias[...] = bias
            stores.append(loads.start(s.own_fc1, out_fc1))
            stores.append(loads.start(s.own_bias, out_bias))
        else:
            s.rz_out[distance] = total.astype(BF16)
            s.rzb_out[distance] = bias
            sum_ring[distance] = [
                links.send(s.rz_out.at[distance], s.rz_in.at[distance], ring_next),
                links.send(s.rzb_out.at[distance], s.rzb_in.at[distance], ring_next),
            ]

    def sum_b_step(distance):
        if distance == 1:
            source = g_all.at[pl.ds(2, 2), second_rows]
            sum_both[1] = links.send(source, s.rb_in.at[1], ring_next)
            return
        before = (distance + ring - 1) % ring
        sum_both[before].wait_recv()
        for line in range(2):
            total = g_all[2 * distance + line, rows_per:].astype(F32) + s.rb_in[before, line].astype(F32)
            if distance == 0 and line == 0:
                s.own_fc2[...] = total
            else:
                s.rb_out[distance, line] = total.astype(BF16)
        if distance == 0:
            sum_last.append(links.send(s.rb_out.at[0, 1], s.ry_last, ydev))
        else:
            sum_both[distance] = links.send(s.rb_out.at[distance], s.rb_in.at[distance], ring_next)

    def sum_b_end():
        sum_last[0].wait_recv()
        s.own_fc2[...] += s.ry_last[...].astype(F32)
        stores.append(loads.start(s.own_fc2, out_fc2))

    sums_done = [0, 1]

    def sum_a_until(steps):
        while sums_done[0] < min(steps, ring):
            sum_a_step(order[sums_done[0]])
            sums_done[0] += 1

    def sum_b_until(steps):
        while sums_done[1] < min(steps, ring):
            sum_b_step(order[sums_done[1]])
            sums_done[1] += 1

    def gather_wait(part):
        per = chunk_slots // 2
        gather_until((part + 1) * per - 1, 1)
        for distance in range(part * per, (part + 1) * per):
            for kind in range(2):
                for copy in gather_y[distance, kind]:
                    copy.wait_recv()

    part_out, part_in = s.part_out, s.part_in
    cross_out, cross_in = s.cross_out, s.cross_in
    part_sib, cross = {}, {}

    def hand_part(kind, place):
        total = (grad_two, result)[kind]
        part_out[kind, place] = total[(3, 1)[place]].astype(BF16)
        part_sib[kind, place] = links.send(part_out.at[kind, place], part_in.at[kind, place], sib)

    def hand_cross(kind):
        total = (grad_two, result)[kind]
        part_sib[kind, 0].wait_recv()
        cross_out[kind] = (total[2] + part_in[kind, 0].astype(F32)).astype(BF16)
        cross[kind] = links.send(cross_out.at[kind], cross_in.at[kind], xdev)

    gather_until(2, 1)
    gather_wait(0)
    n2_sib.wait_recv()
    cot_sib.wait_recv()
    no_bias = jnp.zeros((8, chunk), F32)
    bias_total = feed(0, (0, 1), no_bias)
    gather_until(ring - 1, 0)
    n2_x.wait_recv()
    n2_far = links.send(n2.at[2], n2.at[3], sib)
    gather_until(ring - 1, 1)
    cot_far.wait_recv()
    bias_total = feed(0, (2,), bias_total)
    n2_far.wait_recv()
    bias_total = feed(0, (3,), bias_total)
    early = links.arrivals
    feed_weights(0, bias_total)
    sum_b_step(1)
    for distance in range(1, chunk_slots // 2):
        sum_send_y(distance)
    feed_result(0)
    if chunks == 2:
        gather_wait(1)
        bias_total = feed(1, (3,), no_bias)
        hand_part(0, 0)
        bias_total = feed(1, (2,), bias_total)
    else:
        hand_part(0, 0)
    hand_cross(0)
    if chunks == 2:
        bias_total = feed(1, (0, 1), bias_total)
    hand_part(0, 1)
    sum_a_until(1)
    if chunks == 2:
        feed_weights(1, bias_total)
    for distance in range(chunk_slots // 2, ring):
        sum_send_y(distance)
    sum_send_y(0)
    sum_b_until(2)
    if chunks == 2:
        feed_result(1)
    hand_part(1, 0)
    hand_part(1, 1)
    hand_cross(1)
    for image in range(2):
        s.n1_t[:, image * seq : (image + 1) * seq] = n1[image].T
    sum_a_until(2)
    part_sib[0, 1].wait_recv()
    cross[0].wait_recv()
    grad_mid, grad_branch = stream, s.grad_branch

    def mid_back(step, totals):
        at = pl.ds(pl.multiple_of(step * block, block), block)
        grads = (
            grad_two[0, at, :] + part_in[0, 1, at, :].astype(F32) + cross_in[0, at, :].astype(F32)
        )
        unit_rows, scale = s.unit_two[at, :], s.scale_two[at, :]
        passed = cot_all[0, at, :].astype(F32)
        mid = passed + norm_back(grads, vecs[3:4, :], unit_rows, scale)
        grad_mid[at, :] = mid
        low = mid.astype(BF16)
        grad_branch[0, at, :] = low
        return (
            totals[0] + fold_rows(grads * unit_rows),
            totals[1] + fold_rows(grads),
            totals[2] + fold_rows(low.astype(F32)),
            totals[3] + fold_rows(passed),
        )

    empty = jnp.zeros((8, width), F32)
    gain_two_sum, shift_two_sum, out_bias_sum, fc2_bias_sum = lax.fori_loop(
        0, blocks, mid_back, (empty,) * 4, unroll=4
    )
    branch_back = links.send(grad_branch.at[0], grad_branch.at[1], sib)

    def mixed_back(image):
        grads = mm_nt(grad_branch[image], wout[...])
        for pair in range(pairs):
            s.grad_mixed[image, pair] = grads[:, pair * LANES : (pair + 1) * LANES].astype(BF16)

    grads_pair = s.grads_pair

    def attend_back(image, pair):
        queries, keys = s.q[image, pair], s.k[image, pair]
        values, grads = s.v[image, pair], s.grad_mixed[image, pair]
        keys_t = (keys * score_scale).T
        grad_values = jnp.zeros((seq, LANES), F32)
        grad_keys = jnp.zeros((seq, LANES), F32)
        grad_queries = []
        for half in range(2):
            probs = s.probs[image * 2 * pairs + pair * 2 + half]
            grads_half = grads * lane_half[half]
            grad_values += mm(probs.astype(BF16), grads_half)
            grad_probs = mm_nt(values, grads_half)
            inner = jnp.sum(grad_probs * probs, axis=0, keepdims=True)
            grad_scores = (probs * (grad_probs - inner)).astype(BF16)
            grad_keys += mm(grad_scores, queries * lane_scaled[half])
            grad_queries.append(
                mm(keys_t[half * HEAD_DIM : (half + 1) * HEAD_DIM], grad_scores)
            )
        grad_query = jnp.concatenate(grad_queries, axis=0).T
        for place, value in enumerate(
            (grad_query, grad_keys, grad_values)
        ):
            grads_pair[pair, image, :, place * LANES : (place + 1) * LANES] = value.astype(BF16)

    def rows_back(image):
        total = mm_nt(grads_pair[0, image], w_pair[0])
        for pair in range(1, pairs):
            total += mm_nt(grads_pair[pair, image], w_pair[pair])
        return total

    def weights_back(pair):
        both = grads_pair[pair].reshape(2 * seq, 3 * LANES)
        for base in range(0, width, 256):
            rows = slice(base, base + 256)
            ar[1 + pair, rows, :] = mm(s.n1_t[rows, :], both).astype(BF16)

    mixed_back(0)
    attend_back(0, 0)
    branch_back.wait_recv()
    mixed_back(1)

    ar = s.ar
    by_core = (one_dev, two_dev, p_one, p_two)
    cuts = [(array, lanes) for array in range(4) for lanes in (pl.ds(0, 256), pl.ds(256, local - 256))]
    flat = [
        (ar.at[array, :, lanes], s.ar_one.at[array, :, lanes], s.ar_two.at[array, :, lanes],
         s.ar_z.at[array, :, :, lanes], s.ar_rest.at[array, :, :, lanes], s.attn.at[array, :, lanes],
         width, by_core)
        for array, lanes in cuts
    ]
    small_half = seq // 2
    small = (s.small, s.small_one, s.small_two, s.small_z, s.small_rest,
             s.small_all, small_half, by_core)
    items = flat + [small]
    stages = [dict() for _ in range(7)]

    def piece(item):
        total_rows = items[item][6]
        _, _, p_one, p_two = items[item][7]
        half, quarter, leaf = total_rows // 2, total_rows // 4, total_rows // 16
        at_one = pl.multiple_of(p_one * half, half)
        at_two = pl.multiple_of(at_one + p_two * quarter, quarter)
        return half, quarter, leaf, at_one, at_two

    def reduce_one(item):
        data, one = items[item][0], items[item][1]
        half, _, _, _, _ = piece(item)
        device, _, p_one, _ = items[item][7]
        other = pl.ds(pl.multiple_of((1 - p_one) * half, half), half)
        stages[0][item] = [links.send(data.at[other], one, device, again=True)]

    def reduce_two(item):
        data, one, two = items[item][:3]
        half, quarter, _, at_one, _ = piece(item)
        stages[0][item][0].wait_recv()
        mine = pl.ds(at_one, half)
        data[mine] = (data[mine].astype(F32) + one[...].astype(F32)).astype(data.dtype)
        _, device, _, p_two = items[item][7]
        other = pl.ds(pl.multiple_of(at_one + (1 - p_two) * quarter, quarter), quarter)
        stages[1][item] = [links.send(data.at[other], two, device, again=True)]

    def reduce_z(item):
        data, _, two, by_z = items[item][:4]
        _, quarter, leaf, _, at_two = piece(item)
        stages[1][item][0].wait_recv()
        mine = pl.ds(at_two, quarter)
        data[mine] = (data[mine].astype(F32) + two[...].astype(F32)).astype(data.dtype)
        stages[2][item] = links.send_parts(
            [
                (
                    data.at[pl.ds(pl.multiple_of(at_two + ((zq + hop) % 4) * leaf, leaf), leaf)],
                    by_z.at[hop - 1],
                    zdev[hop],
                )
                for hop in range(1, 4)
            ],
            by_z,
        )

    def spread_z(item):
        data, _, _, by_z, by_rest, done = items[item][:6]
        _, _, leaf, _, at_two = piece(item)
        stages[2][item].wait_recv()
        mine = pl.ds(pl.multiple_of(at_two + zq * leaf, leaf), leaf)
        total = data[mine].astype(F32)
        for hop in range(3):
            total += by_z[hop].astype(F32)
        if rest_count > 1:
            by_rest[0] = total.astype(data.dtype)
            copies = [
                links.send(by_rest.at[0], by_rest.at[hop], rdev[hop])
                for hop in range(1, rest_count)
            ]
            for copy in copies:
                copy.wait_recv()
            total = jnp.zeros(total.shape, F32)
            for owner in range(rest_count):
                total += by_rest[(rest - owner + rest_count) % rest_count].astype(F32)
        done[mine] = total.astype(done.dtype)
        stages[3][item] = links.send_parts(
            [(done.at[mine], done.at[mine], zdev[hop]) for hop in range(1, 4)],
            done.at[pl.ds(0, 3 * leaf)],
        )

    def spread_two(item):
        done = items[item][5]
        _, quarter, _, _, at_two = piece(item)
        stages[3][item].wait_recv()
        mine = pl.ds(at_two, quarter)
        stages[4][item] = [links.send(done.at[mine], done.at[mine], items[item][7][1], again=True)]

    def spread_one(item):
        done = items[item][5]
        half, _, _, at_one, _ = piece(item)
        stages[4][item][0].wait_recv()
        mine = pl.ds(at_one, half)
        stages[5][item] = [links.send(done.at[mine], done.at[mine], items[item][7][0], again=True)]

    def finish(item):
        stages[5][item][0].wait_recv()
        if item < len(cuts):
            array, lanes = cuts[item]
            stores.append(loads.start(s.attn.at[array, :, lanes], out_attn.at[array, :, lanes]))

    for half in range(2):
        at = slice(half * local, (half + 1) * local)
        total = mm(s.mixed_t[0], grad_branch[0, :, at]) + mm(
            s.mixed_t[1], grad_branch[1, :, at]
        )
        ar[0, at, :] = total.astype(BF16)
    links.spare = list(range(early))
    def out_back():
        part_sib[1, 1].wait_recv()
        cross[1].wait_recv()

        @pl.loop(0, blocks, unroll=4)
        def _(step):
            at = pl.ds(pl.multiple_of(step * block, block), block)
            row_ids = lax.broadcasted_iota(jnp.int32, (block, 1), 0) + step * block
            total = result[0, at, :] + part_in[1, 1, at, :].astype(F32) + cross_in[1, at, :].astype(F32)
            rows = middle[at, :] + (total + vecs[5:6, :])
            s.own_rows[0, at, :] = jnp.where(row_ids < limit, rows, 0.0).astype(BF16)

        stores.append(loads.start(s.own_rows, out_rows))

    def pair_back(pair):
        if pair == 0:
            sum_b_until(3)
        attend_back(1, pair)
        if pair > 0:
            attend_back(0, pair)
        weights_back(pair)
        if pair == 1:
            sum_a_until(3)

    held = SimpleNamespace()

    def rows_hand():
        s.rows_out[...] = rows_back(1).astype(BF16)
        held.rows_sib = links.send(s.rows_out, s.rows_in, sib)

    def rows_keep():
        s.branch_own[...] = rows_back(0)

    def norm_one_back():
        held.rows_sib.wait_recv()

        def in_back(step, totals):
            at = pl.ds(pl.multiple_of(step * block, block), block)
            grads = (s.branch_own[at, :] + s.rows_in[at, :].astype(F32))
            unit_rows, scale = s.unit_one[at, :], s.scale_one[at, :]
            grad_mid[at, :] += norm_back(grads, vecs[0:1, :], unit_rows, scale)
            return (totals[0] + fold_rows(grads * unit_rows), totals[1] + fold_rows(grads))

        held.sums = lax.fori_loop(0, blocks, in_back, (empty,) * 2, unroll=4)

    theirs = pl.ds(pl.multiple_of((1 - h) * small_half, small_half), small_half)
    ours = pl.ds(pl.multiple_of(h * small_half, small_half), small_half)
    small_ref, small_own = s.small_full, s.small
    small_base = (width // small_ref.shape[1]) * prompt_pad + 6 * (width // small_ref.shape[1])

    def place_small():
        gain_one_sum, shift_one_sum = held.sums
        grad_in = grad_mid[...]
        high = grad_in.astype(BF16)
        low = (grad_in - high.astype(F32)).astype(BF16)
        placed = mm(pick[...], high) + mm(pick[...], low)
        s.own_tok[0] = placed[0:tok_rows]
        stores.append(loads.start(s.own_tok.at[0], out_tok.at[:, 0, :]))

        small_ref[...] = jnp.zeros(small_ref.shape, F32)
        part_width = small_ref.shape[1]
        parts = width // part_width
        for part in range(parts):
            small_ref[part * prompt_pad : part * prompt_pad + prompt_pad, :] = placed[
                tok_pad : tok_pad + prompt_pad, part * part_width : (part + 1) * part_width
            ]
        base = parts * prompt_pad
        sums = (gain_one_sum, shift_one_sum, out_bias_sum, gain_two_sum, shift_two_sum, fc2_bias_sum)
        for place, total in enumerate(sums):
            row = jnp.sum(total, axis=0, keepdims=True)
            for part in range(parts):
                at = base + place * parts + part
                small_ref[at : at + 1, :] = row[:, part * part_width : (part + 1) * part_width]
        base += len(sums) * parts
        for place in range(2):
            at = slice(2 * place * LANES, 2 * place * LANES + LANES)
            row = jnp.concatenate(
                [
                    jnp.sum(
                        grads_pair[pair, 0, :, at].astype(F32) + grads_pair[pair, 1, :, at].astype(F32),
                        axis=0,
                        keepdims=True,
                    )
                    for pair in range(pairs)
                ],
                axis=1,
            )
            for head in range(2):
                chosen = row * (h if head == 1 else 1 - h).astype(F32)
                at = base + head * 4 + place * 2
                small_ref[at : at + 1, :] = chosen[:, 0:part_width]
                small_ref[at + 1 : at + 2, 0 : local - part_width] = chosen[:, part_width:local]
        held.small_sib = links.send(small_ref.at[theirs], s.small_in.at[1], sib)
        sum_a_until(ring)
        sum_b_until(ring)

    def reduce_small():
        held.small_sib.wait_recv()
        small_own[...] = small_ref[ours] + s.small_in[1]

    final = s.small_out

    def hand_small():
        final[ours] = s.small_all[...]
        held.small_back = links.send(s.small_all, s.small_in.at[0], sib)

    blocks_beside = [
        functools.partial(pair_back, 0), functools.partial(pair_back, 1), functools.partial(pair_back, 2),
        rows_hand, rows_keep, norm_one_back, place_small, out_back,
    ]
    steps = [reduce_one, reduce_two, reduce_z, spread_z, spread_two, spread_one, finish]
    for item, stage in REDUCE_ORDER:
        if item < 0:
            blocks_beside[-1 - item]()
        else:
            if stage == 0 and item == len(cuts):
                reduce_small()
            steps[stage](item)
            if (item, stage) == LATE_SUM:
                sum_b_end()
            if (item, stage) == (len(cuts), len(steps) - 1):
                hand_small()
    held.small_back.wait_recv()
    final[theirs] = s.small_in[0]
    final[small_base + 8 : small_base + 12, :] = jnp.where(
        h == 0, final[small_base : small_base + 4, :], final[small_base + 4 : small_base + 8, :]
    )
    stores.append(loads.start(final, out_small))
    links.drain()
    for copy in stores:
        copy.wait()


def finish_kernel(dims, *refs):
    it = iter(refs)
    rows_in, tok_in, attn_in, small_in, fc1_in, fc2_in, bias_in = (next(it) for _ in range(7))
    (
        layer_out, grad_tokens, grad_prompts, gain_one, shift_one, w_query, b_query, w_key,
        w_value, b_value, w_out, b_out, gain_two, shift_two, w_fc1, b_fc1, w_fc2, b_fc2,
    ) = (next(it) for _ in range(18))
    s = SimpleNamespace(**dict(zip(dims.finish, it)))
    width, local = dims.width, dims.local
    rows = w_fc1.shape[0]
    loads = Loads(s.load_sems, dims.finish_depth)
    whole_shards = rows == fc1_in.shape[0]
    passing = [(tok_in, s.tok, grad_tokens), (rows_in, s.rows, layer_out)]
    if whole_shards:
        passing += [(fc1_in, s.fc1, w_fc1), (fc2_in, s.fc2, w_fc2)]
    passing = [(loads.start(source, held), held, target) for source, held, target in passing]
    load_attn = [loads.start(attn_in.at[array], s.attn.at[array]) for array in (1, 2, 3, 0)]
    load_small = loads.start(small_in, s.small)
    load_bias = loads.start(bias_in, s.bias)
    stores = []
    for load, held, target in passing:
        load.wait()
        stores.append(loads.start(held, target))
    for pair in range(3):
        load_attn[pair].wait()
        at = slice(pair * LANES, (pair + 1) * LANES)
        for place, target in enumerate((w_query, w_key, w_value)):
            s.tall[place, :, at] = s.attn[1 + pair, :, place * LANES : (place + 1) * LANES].astype(F32)
            stores.append(loads.start(s.tall.at[place, :, pl.ds(pair * LANES, LANES)], target.at[:, pl.ds(pair * LANES, LANES)]))
    load_attn[3].wait()
    s.wide[:, 0:local] = s.attn[0, 0:local].astype(F32)
    s.wide[:, local : 2 * local] = s.attn[0, local : 2 * local].astype(F32)
    stores.append(loads.start(s.wide, w_out))
    load_small.wait()
    load_bias.wait()
    part_width = s.small.shape[1]
    parts = width // part_width
    for part in range(parts):
        at = slice(part * part_width, (part + 1) * part_width)
        s.prompts[:, at] = s.small[part * dims.prompt_pad : part * dims.prompt_pad + dims.prompt_rows]
    stores.append(loads.start(s.prompts, grad_prompts))
    base = parts * dims.prompt_pad
    for place, target in enumerate((gain_one, shift_one, b_out, gain_two, shift_two, b_fc2)):
        for part in range(parts):
            at = base + place * parts + part
            s.row[place : place + 1, part * part_width : (part + 1) * part_width] = s.small[at : at + 1]
        s.flat[place, :] = s.row[place : place + 1, :].reshape(width)
        stores.append(loads.start(s.flat.at[place], target))
    base += 6 * parts + 8
    for place, target in enumerate((b_query, b_value)):
        at = base + 2 * place
        s.row[6:7, 0:part_width] = s.small[at : at + 1]
        s.row[6:7, part_width : 2 * part_width] = s.small[at + 1 : at + 2]
        s.half_flat[place, :] = s.row[6:7, 0:local].reshape(local)
        stores.append(loads.start(s.half_flat.at[place], target))
    b_fc1[...] = s.bias[0:1, 0:rows].reshape(rows)
    if not whole_shards:
        for source, held, target in ((fc1_in, s.fc1, w_fc1), (fc2_in, s.fc2, w_fc2)):
            loads.start(source, held).wait()
            s.cut[...] = held[0:rows]
            loads.start(s.cut, target).wait()
    for copy in stores:
        copy.wait()


def layer(dims, operands):
    seq, width, local = dims.seq, dims.width, dims.local
    n, ring, slots, rows_per = dims.n, dims.ring, dims.slots, dims.rows_per
    pairs = local // LANES
    chunk = dims.chunk_slots * rows_per
    rest_count = n // 16
    small_half = seq // 2
    part_width = 256
    arrivals = 11 * ring + 68 + 9 * (rest_count - 1) - min(36, 6 * ring + 6) - 8
    vmem = pltpu.VMEM
    shared = 2 * rows_per
    scratch = dict(
        send_sems=pltpu.SemaphoreType.DMA((dims.send_depth,)),
        recv_sems=pltpu.SemaphoreType.DMA((arrivals,)),
        w_all=vmem((slots, shared, width), BF16),
        b_all=vmem((slots, 8, LANES), F32),
        cot_all=vmem((4, seq, width), BF16),
        meta=vmem((2, 8, LANES), jnp.int32),
        load_sems=pltpu.SemaphoreType.DMA((dims.load_depth,)),
        kept=vmem((1, dims.patches), jnp.int32),
        tokens=vmem((1, dims.tok_rows, width), BF16),
        prompts=vmem((dims.prompt_rows, width), BF16),
        gain_one=vmem((width,), BF16),
        shift_one=vmem((width,), BF16),
        b_query=vmem((local,), BF16),
        b_value=vmem((local,), BF16),
        b_out=vmem((width,), BF16),
        gain_two=vmem((width,), BF16),
        shift_two=vmem((width,), BF16),
        b_fc1=vmem((dims.rows,), BF16),
        b_fc2=vmem((width,), BF16),
        vecs=vmem((8, width), F32),
        w_pair=vmem((pairs, width, 3 * LANES), BF16),
        wout=vmem((local, width), BF16),
        unit_one=vmem((seq, width), F32),
        unit_two=vmem((seq, width), F32),
        scale_one=vmem((seq, 1), F32),
        scale_two=vmem((seq, 1), F32),
        own_rows=vmem((1, seq, width), BF16),
        own_tok=vmem((1, dims.tok_rows, width), F32),
        own_fc1=vmem((rows_per, width), F32),
        own_fc2=vmem((rows_per, width), F32),
        own_bias=vmem((8, LANES), F32),
        attn=vmem((4, width, local), BF16),
        src=vmem((dims.tok_pad + dims.prompt_pad, width), BF16),
        pick=vmem((dims.tok_pad + dims.prompt_pad, seq), BF16),
        idx=vmem((8, seq), jnp.int32),
        stream=vmem((seq, width), F32),
        middle=vmem((seq, width), F32),
        n1=vmem((2, seq, width), BF16),
        n2=vmem((4, seq, width), BF16),
        q=vmem((2, pairs, seq, LANES), BF16),
        k=vmem((2, pairs, seq, LANES), BF16),
        v=vmem((2, pairs, seq, LANES), BF16),
        probs=vmem((4 * pairs, seq, seq), F32),
        mixed_t=vmem((2, local, seq), BF16),
        branch_out=vmem((seq, width), F32),
        branch_in=vmem((seq, width), F32),
        branch_own=vmem((seq, width), F32),
        hidden=vmem((slots // dims.chunk_slots, 4, seq, chunk), BF16),
        grad_before=vmem((4, seq, chunk), BF16),
        result=vmem((4, seq, width), F32),
        grad_two=vmem((4, seq, width), F32),
        part_out=vmem((2, 2, seq, width), BF16),
        part_in=vmem((2, 2, seq, width), BF16),
        cross_out=vmem((2, seq, width), BF16),
        cross_in=vmem((2, seq, width), BF16),
        g_all=vmem((slots, shared, width), BF16),
        gb_all=vmem((slots, 8, LANES), F32),
        ry=vmem((ring, rows_per, width), BF16),
        ry_last=vmem((rows_per, width), BF16),
        rb_out=vmem((ring, 2, rows_per, width), BF16),
        rb_in=vmem((ring, 2, rows_per, width), BF16),
        n1_t=vmem((width, 2 * seq), BF16),
        ryb=vmem((ring, 8, LANES), F32),
        rz_out=vmem((ring, rows_per, width), BF16),
        rzb_out=vmem((ring, 8, LANES), F32),
        rz_in=vmem((ring, rows_per, width), BF16),
        rzb_in=vmem((ring, 8, LANES), F32),
        grad_branch=vmem((2, seq, width), BF16),
        grad_mixed=vmem((2, pairs, seq, LANES), BF16),
        grads_pair=vmem((pairs, 2, seq, 3 * LANES), BF16),
        rows_out=vmem((seq, width), BF16),
        rows_in=vmem((seq, width), BF16),
        ar=vmem((4, width, local), BF16),
        ar_one=vmem((4, width // 2, local), BF16),
        ar_two=vmem((4, width // 4, local), BF16),
        ar_z=vmem((4, 3, width // 16, local), BF16),
        ar_rest=vmem((4, rest_count, width // 16, local), BF16),
        small_full=vmem((seq, part_width), F32),
        small_out=vmem((seq, part_width), F32),
        small_in=vmem((2, small_half, part_width), F32),
        small=vmem((small_half, part_width), F32),
        small_one=vmem((small_half // 2, part_width), F32),
        small_two=vmem((small_half // 4, part_width), F32),
        small_z=vmem((3, small_half // 16, part_width), F32),
        small_rest=vmem((rest_count, small_half // 16, part_width), F32),
        small_all=vmem((small_half, part_width), F32),
    )
    dims = SimpleNamespace(**vars(dims), scratch=tuple(scratch))
    anywhere = pl.BlockSpec(memory_space=pl.ANY)
    shape = jax.ShapeDtypeStruct
    return pl.pallas_call(
        functools.partial(layer_kernel, dims),
        out_shape=(
            shape((1, seq, width), BF16),
            shape((dims.tok_rows, 1, width), F32),
            shape((4, width, local), BF16),
            shape((seq, part_width), F32),
            shape((rows_per, width), F32),
            shape((rows_per, width), F32),
            shape((8, LANES), F32),
        ),
        in_specs=[pl.BlockSpec(memory_space=pltpu.SMEM)] + [anywhere] * (len(operands) - 1),
        out_specs=[anywhere] * 7,
        scratch_shapes=list(scratch.values()),
        compiler_params=pltpu.CompilerParams(
            collective_id=0, has_side_effects=True, vmem_limit_bytes=63 * 2**20
        ),
    )(*operands)


def finish(dims, results):
    seq, width, local, rows = dims.seq, dims.width, dims.local, dims.rows
    vmem = pltpu.VMEM
    scratch = dict(
        load_sems=pltpu.SemaphoreType.DMA((dims.finish_depth,)),
        attn=vmem((4, width, local), BF16),
        wide=vmem((local, width), F32),
        tall=vmem((3, width, local), F32),
        small=vmem(results[3].shape, F32),
        bias=vmem((8, LANES), F32),
        prompts=vmem((dims.prompt_rows, width), F32),
        row=vmem((8, width), F32),
        flat=vmem((6, width), F32),
        half_flat=vmem((2, local), F32),
        rows=vmem((1, seq, width), BF16),
        tok=vmem((dims.tok_rows, 1, width), F32),
        fc1=vmem((dims.rows_per, width), F32),
        fc2=vmem((dims.rows_per, width), F32),
        cut=vmem((rows, width), F32),
    )
    dims = SimpleNamespace(**vars(dims), finish=tuple(scratch))
    anywhere = pl.BlockSpec(memory_space=pl.ANY)
    whole = pl.BlockSpec(memory_space=pltpu.VMEM)

    def out(*sizes, dtype=F32):
        return jax.ShapeDtypeStruct(sizes, dtype)

    shapes = (
        out(1, seq, width, dtype=BF16), out(dims.tok_rows, 1, width), out(dims.prompt_rows, width),
        out(width), out(width), out(width, local), out(local), out(width, local),
        out(width, local), out(local), out(local, width), out(width), out(width), out(width),
        out(rows, width), out(rows), out(rows, width), out(width),
    )
    return pl.pallas_call(
        functools.partial(finish_kernel, dims),
        out_shape=shapes,
        in_specs=[anywhere] * 7,
        out_specs=[whole if place == 15 else anywhere for place in range(len(shapes))],
        scratch_shapes=list(scratch.values()),
        compiler_params=pltpu.CompilerParams(vmem_limit_bytes=60 * 2**20),
    )(*results)


def body(n, *arguments):
    (
        tokens, kept_index, kept_count, prompts, gain_one, shift_one, w_query, b_query, w_key,
        w_value, b_value, w_out, b_out, gain_two, shift_two, w_fc1, b_fc1, w_fc2, b_fc2, cotangent,
    ) = arguments
    seq, width = cotangent.shape[1:]
    local = w_query.shape[1]
    rows = w_fc1.shape[0]
    rows_per = round_up(rows, 16)
    ring = n // 4
    slots = 2 * ring
    halves = slots // 2
    chunk_slots = halves if (halves % 2 == 0 and halves * rows_per % LANES == 0) else slots
    tok_rows, prompt_rows = tokens.shape[1], prompts.shape[0]
    dims = SimpleNamespace(
        n=n, ring=ring, slots=slots, chunk_slots=chunk_slots, rows_per=rows_per, rows=rows, seq=seq,
        width=width, local=local, tok_rows=tok_rows, tok_pad=round_up(tok_rows, 16),
        prompt_rows=prompt_rows, prompt_pad=round_up(prompt_rows, 16),
        patches=kept_index.shape[1], send_depth=32, load_depth=17, finish_depth=32,
    )
    if rows_per != rows:
        spare = ((0, rows_per - rows), (0, 0))
        w_fc1, w_fc2 = jnp.pad(w_fc1, spare), jnp.pad(w_fc2, spare)
    operands = (
        kept_count, tokens, kept_index, prompts, w_fc1, w_fc2, cotangent, w_query, w_key, w_value,
        w_out, gain_one, shift_one, b_query, b_value, b_out, gain_two, shift_two, b_fc1, b_fc2,
    )
    outs = list(finish(dims, layer(dims, operands)))
    outs[1] = outs[1].transpose(1, 0, 2)
    return tuple(outs)


def solution(mesh):
    batch, head = mesh.axis_names
    both = (batch, head)
    placed = (
        P(both, None, None), P(both, None), P(both), P(), P(), P(), P(None, head), P(head),
        P(None, head), P(None, head), P(head), P(head, None), P(), P(), P(),
        P(both, None), P(both), P(both, None), P(), P(both, None, None),
    )
    return jax.shard_map(
        functools.partial(body, mesh.shape[batch]),
        mesh=mesh,
        in_specs=placed,
        out_specs=(
            P(both, None, None), P(both, None, None), P(), P(), P(), P(None, head), P(head),
            P(None, head), P(None, head), P(head), P(head, None), P(), P(), P(),
            P(both, None), P(both), P(both, None), P(),
        ),
        check_vma=False,
    )
```
